32 devices in a mesh: dp: 8 (over z, y), tensor: 4 (over x, core).
Axes of the slice: x: 2, y: 2, z: 4, core: 2. Of those that a mesh axis runs over, the one named last changes fastest.
Arguments:
- tokens: bfloat16 [2048, 2, 2048], P(('dp', 'tensor')), may hold values from -6 to 6
- cotangent: bfloat16 [2048, 2, 2048], P(('dp', 'tensor')), may hold values from -6 to 6
- segments: int32 [2048, 2], P('dp'), may hold values from 0 to 3, as said below
- expert_ids: int32 [2048, 2, 8], P('dp'), may hold values from 0 to 31, all different within a row; in each aligned block of 512 rows (0 to 511, 512 to 1023, ..., all dimensions but the last counted through in order) at most 176 rows name the same one
- attn_gain: bfloat16 [2048], P('dp'), may hold values from 0.5 to 1.5
- w_qkv: bfloat16 [2048, 3, 2048], P('dp', None, 'tensor'), may hold values from -0.125 to 0.125
- qk_gain: bfloat16 [128, 2, 16], P('dp', None, 'tensor'), may hold values from 0.5 to 1.5
- w_out: bfloat16 [2048, 2048], P('dp', 'tensor'), may hold values from -1 to 1
- mlp_gain: bfloat16 [2048], P('dp'), may hold values from 0.5 to 1.5
- router: bfloat16 [2048, 32], P('dp'), may hold values from -0.0625 to 0.0625
- expert_in: bfloat16 [32, 2048, 2, 1024], P(None, 'dp', None, 'tensor'), may hold values from -0.125 to 0.125
- expert_out: bfloat16 [32, 2048, 1024], P(None, 'dp', 'tensor'), may hold values from -3 to 3
Outputs:
- layer_out: bfloat16 [2048, 2, 2048], P(('dp', 'tensor'))
- grad_tokens: bfloat16 [2048, 2, 2048], P(('dp', 'tensor'))
- grad_attn_gain: float32 [2048], P('dp')
- grad_w_qkv: float32 [2048, 3, 2048], P('dp', None, 'tensor')
- grad_qk_gain: float32 [128, 2, 16], P('dp', None, 'tensor')
- grad_w_out: float32 [2048, 2048], P('dp', 'tensor')
- grad_mlp_gain: float32 [2048], P('dp')
- grad_router: float32 [2048, 32], P('dp')
- grad_expert_in: float32 [32, 2048, 2, 1024], P(None, 'dp', None, 'tensor')
- grad_expert_out: float32 [32, 2048, 1024], P(None, 'dp', 'tensor')
The draws below stay inside these ranges and needn't reach their ends.
Inputs may be any that keep to these rules, and one draw needn't show every extreme that they name: `segments`: document numbers start at 0 and never fall along a sequence; a sequence holds one document or 4; in each group one micro-batch, drawn from the seed, holds a single document. `expert_ids`: A token's 8 experts differ; within the 512 rows of one group no expert is named more than 176 times, and in some group an expert is named exactly 176 times.
All inputs are finite; a program needn't handle non-finite values.
Results may differ from the reference program's by a relative error of at most 0.024.
Values may be sent and summed in bfloat16 or wider, within the bound.
A program may use at most 384 MiB of HBM per device.

```python
import math
import jax
import jax.numpy as jnp
import numpy as np
from jax import lax

D = 2048
H = 16
HD = 128
FF = 1024
TOP = 8
E = 32
DOCS = 4
MICRO = 2
SEQ = 256
WINDOW = 128
CAP = 176
TOKENS = 2048


def draw_segments(key, part):
    key = jax.random.fold_in(key, 7)
    pick_key, cut_key = jax.random.split(key)
    group_count = TOKENS // SEQ
    single = jax.random.randint(pick_key, (group_count, 1, 1), 0, MICRO)
    drawn = jax.random.randint(cut_key, (group_count, MICRO, SEQ - 1), 0, 2 ** 19)
    distinct = drawn * SEQ + jnp.arange(SEQ - 1, dtype=jnp.int32)
    boundaries = lax.top_k(distinct, DOCS - 1)[1] + 1
    positions = jnp.arange(SEQ, dtype=jnp.int32)
    numbers = jnp.sum((boundaries[:, :, None, :] <= positions[None, None, :, None]).astype(jnp.int32), axis=-1)
    micro_index = jnp.arange(MICRO, dtype=jnp.int32)[None, :, None]
    numbers = jnp.where(micro_index == single, 0, numbers)
    return jnp.transpose(numbers, (0, 2, 1)).reshape(TOKENS, MICRO)


def steps_of(rng, shape, shards, low, high):
    level = 1.0
    for dim, blocks in shards:
        heights = jax.random.uniform(jax.random.fold_in(jax.random.fold_in(rng, 6), dim), (blocks,), jnp.float32, low / len(shards), high / len(shards))
        level = level * jnp.repeat(jnp.exp(heights), shape[dim] // blocks).reshape((-1,) + (1,) * (len(shape) - 1 - dim))
    return level


def routed_block(key, own, number, rows, amount, top, bound, skew):
    sequence = jax.random.permutation(key, amount)
    packed, ordinary = shares(amount, rows * top, bound, skew, True), shares(amount, rows * top, bound, skew, False)
    places = jnp.arange(amount)

    def named(sizes, rotation):
        used = int((sizes > 0).sum())
        fixed = max(1, used // 4)
        shifted = fixed + (places - fixed + rotation * (used - fixed)) % max(1, amount - fixed)
        return jnp.zeros((amount,), jnp.int32).at[sequence[jnp.where(places < fixed, places, shifted)]].set(jnp.asarray(sizes, jnp.int32))

    sizes = jnp.where(number % 4 == 0, named(packed, number // 4), named(ordinary, number - number // 4 - 1))
    mixed = jax.random.permutation(jax.random.fold_in(own, 3), amount)
    donor, sink = mixed[0:amount // 2 * 2:2], mixed[1:amount // 2 * 2:2]
    slack = jnp.minimum(sizes[donor] - 1, bound - sizes[sink]) // 2
    slack = jnp.where((donor == sequence[0]) | (sink == sequence[0]) | (sizes[sink] == 0), 0, jnp.maximum(slack, 0))
    shifted = jax.random.randint(jax.random.fold_in(own, 4), (amount // 2,), 0, 1 << 20) % (slack + 1)
    sizes = sizes.at[donor].add(-shifted).at[sink].add(shifted)
    items = jnp.searchsorted(jnp.cumsum(sizes), jnp.arange(rows * top), side="right").astype(jnp.int32)
    listing = items.reshape(top, rows).T
    listing = listing[jax.random.permutation(jax.random.fold_in(own, 1), rows)]
    rotation = jax.random.randint(jax.random.fold_in(own, 2), (rows, 1), 0, top)
    return jnp.take_along_axis(listing, (jnp.arange(top)[None, :] + rotation) % top, axis=1)


def shares(amount, total, most, lean, full):
    loads = [(1 << 20) // math.isqrt(standing ** lean) + 1 for standing in range(1, amount + 1)]
    largest = most if full else min(most, max(-(-total // amount), total * loads[0] // sum(loads)))
    least = 1 if total - largest >= amount - 1 else 0
    counts, surplus = [largest] + [least] * (amount - 1), total - largest - least * (amount - 1)
    while surplus > 0:
        movable = [i for i in range(1, amount) if counts[i] < largest] or [i for i in range(1, amount) if counts[i] < most]
        pool, budget = sum([loads[i] for i in movable]), surplus
        for i in movable:
            more = min(most - counts[i], max(1, budget * loads[i] // pool), surplus)
            counts[i] = counts[i] + more
            surplus = surplus - more
    return np.array(counts)


def bell_draw(rng, extent, scale, most, shards=(), held_as=jnp.bfloat16):
    loudness = steps_of(rng, extent, shards, -0.22, 0.18) if shards else 1.0
    values = jax.random.normal(rng, extent, jnp.float32) * scale * loudness
    return jnp.minimum(jnp.maximum(values, -most), most).astype(held_as)


def setup_inputs(seed: int = 0) -> dict:
    arg_keys = jax.random.split(jax.random.key(seed), 13)
    tokens = bell_draw(arg_keys[0], (TOKENS, MICRO, D), 1.0, 6.0, ((0, 32),))
    cotangent = bell_draw(arg_keys[1], (TOKENS, MICRO, D), 1.0, 6.0, ((0, 32),))
    segments = draw_segments(jax.random.fold_in(arg_keys[12], 71), 0)
    expert_ids_keys = jax.random.split(jax.random.fold_in(arg_keys[3], 1), TOKENS * MICRO // (SEQ * MICRO))
    expert_ids_turns = jax.random.permutation(jax.random.fold_in(arg_keys[3], 3), TOKENS * MICRO // (SEQ * MICRO))
    expert_ids = jax.vmap(lambda own, number: routed_block(jax.random.fold_in(arg_keys[3], 2), own, number, SEQ * MICRO, E, TOP, CAP, 1))(expert_ids_keys, expert_ids_turns).reshape((TOKENS, MICRO, TOP))
    attn_gain = jnp.clip(1.0 + 0.1 * jax.random.normal(arg_keys[4], (D,), jnp.float32), 0.5, 1.5).astype(jnp.bfloat16)
    w_qkv = bell_draw(arg_keys[5], (D, 3, D), D ** -0.5, 0.125, ((0, 8), (2, 4)))
    qk_gain = jnp.clip(1.0 + 0.1 * jax.random.normal(arg_keys[6], (HD, 2, H), jnp.float32), 0.5, 1.5).astype(jnp.bfloat16)
    w_out = bell_draw(arg_keys[7], (D, D), 32 ** -0.5, 1.0, ((0, 8), (1, 4)))
    mlp_gain = jnp.clip(1.0 + 0.1 * jax.random.normal(arg_keys[8], (D,), jnp.float32), 0.5, 1.5).astype(jnp.bfloat16)
    router = bell_draw(arg_keys[9], (D, E), (4 * D) ** -0.5, 0.0625, ((0, 8),))
    expert_in = bell_draw(arg_keys[10], (E, D, 2, FF), D ** -0.5, 0.125, ((1, 8), (3, 4)))
    expert_out = bell_draw(arg_keys[11], (E, D, FF), 4 ** -0.5, 3.0, ((1, 8), (2, 4)))
    return {"tokens": tokens, "cotangent": cotangent, "segments": segments, "expert_ids": expert_ids, "attn_gain": attn_gain, "w_qkv": w_qkv, "qk_gain": qk_gain, "w_out": w_out, "mlp_gain": mlp_gain, "router": router, "expert_in": expert_in, "expert_out": expert_out}


EPSILON = 1e-05
MASKED = -1e+30
PRECISE = lax.Precision.HIGHEST

@jax.custom_vjp
def low(v):
    return lax.optimization_barrier(v.astype(jnp.bfloat16)).astype(jnp.float32)

@jax.custom_vjp
def low_back(v):
    return v

def low_keep(v):
    return (low(v), None)

def low_pass(kept, grad):
    return (grad,)

def back_keep(v):
    return (v, None)

def back_low(kept, grad):
    return (low(grad),)
low.defvjp(low_keep, low_pass)
low_back.defvjp(back_keep, back_low)

def norm_factor(values):
    return lax.rsqrt(lax.optimization_barrier(jnp.mean(values * values, axis=-1, keepdims=True)) + EPSILON)

def softmax_rows(logits):
    highest = lax.optimization_barrier(jnp.max(logits, axis=-1, keepdims=True))
    raised = jnp.exp(logits - highest)
    return raised / lax.optimization_barrier(jnp.sum(raised, axis=-1, keepdims=True))

def layer(params, inputs, segment_ids, routed):
    attn_gain, w_qkv, qk_gain, w_out, mlp_gain, router, expert_in, expert_out = params
    seq_len = inputs.shape[0]
    micro_count = inputs.shape[1]
    features = inputs.shape[2]
    head_dim = qk_gain.shape[0]
    head_count = features // head_dim
    normed_one = low(inputs * norm_factor(inputs) * attn_gain)
    projected = jnp.einsum('smd,djf->jsmf', normed_one, w_qkv, precision=PRECISE)
    query_raw = low_back(projected[0])
    key_raw = low_back(projected[1])
    value_rows = low(low_back(projected[2]))
    norm_gain = jnp.transpose(qk_gain, (1, 2, 0)).reshape(2, features)
    queries = low(low_back(query_raw * norm_factor(query_raw) * norm_gain[0]))
    keys_normed = low(low_back(key_raw * norm_factor(key_raw) * norm_gain[1]))
    query_heads = queries.reshape(seq_len, micro_count, head_count, head_dim)
    key_heads = keys_normed.reshape(seq_len, micro_count, head_count, head_dim)
    value_heads = value_rows.reshape(seq_len, micro_count, head_count, head_dim)
    positions = jnp.arange(seq_len)
    seq_major = segment_ids.T
    same_doc = seq_major[:, :, None] == seq_major[:, None, :]
    distance = positions[:, None] - positions[None, :]
    allowed = same_doc & (distance >= 0) & (distance < WINDOW)
    raw_scores = jnp.einsum('qmhc,kmhc->mhqk', query_heads, key_heads, precision=PRECISE)
    scores = low_back(raw_scores * head_dim ** (-0.5))
    scores = jnp.where(allowed[:, None], scores, MASKED)
    weights_attn = low(softmax_rows(scores))
    head_mixed = jnp.einsum('mhqk,kmhc->qmhc', weights_attn, value_heads, precision=PRECISE)
    head_mixed = low(low_back(head_mixed.reshape(seq_len, micro_count, features)))
    attended = low_back(jnp.einsum('smf,df->smd', head_mixed, w_out, precision=PRECISE))
    residual = inputs + attended
    normed_two = low(residual * norm_factor(residual) * mlp_gain)
    logits = low_back(jnp.einsum('smd,de->sme', normed_two, router, precision=PRECISE))
    router_probs = softmax_rows(logits)
    experts = router.shape[1]
    top_count = routed.shape[2]
    choose = (routed[..., None] == jnp.arange(experts, dtype=jnp.int32)).astype(jnp.float32)
    gate_values = lax.optimization_barrier(jnp.sum(choose * router_probs[:, :, None, :], axis=-1))
    flat_routes = routed.reshape(-1)
    tokens_all = seq_len * micro_count
    member = (flat_routes[:, None] == jnp.arange(experts, dtype=jnp.int32)).astype(jnp.int32)
    position = lax.optimization_barrier(jnp.sum(jnp.cumsum(member, axis=0) * member, axis=1)) - 1
    slot_index = flat_routes * CAP + position
    row_tokens = jnp.arange(flat_routes.shape[0], dtype=jnp.int32) // top_count
    source = jnp.full((experts * CAP,), tokens_all, jnp.int32).at[slot_index].set(row_tokens)
    padded_rows = jnp.concatenate([normed_two.reshape(tokens_all, features), jnp.zeros((1, features), jnp.float32)], axis=0)
    chosen = padded_rows[source].reshape(experts, CAP, features)
    gate_up = low_back(jnp.einsum('ecd,edjf->ecjf', chosen, expert_in, precision=PRECISE))
    gate_part = gate_up[:, :, 0]
    hidden = low(gate_part * jax.nn.sigmoid(gate_part) * gate_up[:, :, 1])
    expert_rows = low_back(jnp.einsum('ecf,edf->ecd', hidden, expert_out, precision=PRECISE))
    picked = expert_rows.reshape(experts * CAP, features)[slot_index]
    picked = picked.reshape(seq_len, micro_count, top_count, features)
    mixture = lax.optimization_barrier(jnp.sum(gate_values[..., None] * picked, axis=2))
    return residual + mixture

def reference(tokens, cotangent, segments, expert_ids, attn_gain, w_qkv, qk_gain, w_out, mlp_gain, router, expert_in, expert_out):
    params = tuple((weight.astype(jnp.float32) for weight in (attn_gain, w_qkv, qk_gain, w_out, mlp_gain, router, expert_in, expert_out)))
    group_count = segments.shape[0] // SEQ
    features = tokens.shape[2]
    grouped = tokens.astype(jnp.float32).reshape(group_count, SEQ, MICRO, features)
    pulls = cotangent.astype(jnp.float32).reshape(group_count, SEQ, MICRO, features)
    seg_groups = segments.reshape(group_count, SEQ, MICRO)
    route_groups = expert_ids.reshape(group_count, SEQ, MICRO, TOP)

    def step(totals, item):
        inputs, pull, seg_group, route_group = item
        result, backward = jax.vjp(lambda weights_all, values_in: layer(weights_all, values_in, seg_group, route_group), params, inputs)
        grad_params, grad_inputs = backward(pull)
        totals = jax.tree.map(lambda first, second: first + second, totals, grad_params)
        return (totals, (result.astype(jnp.bfloat16), grad_inputs.astype(jnp.bfloat16)))
    zeros = jax.tree.map(jnp.zeros_like, params)
    totals, outputs = lax.scan(step, zeros, (grouped, pulls, seg_groups, route_groups))
    results = outputs[0].reshape(tokens.shape)
    grad_inputs = outputs[1].reshape(tokens.shape)
    return (results, grad_inputs, totals[0], totals[1], totals[2], totals[3], totals[4], totals[5], totals[6], totals[7])
```

```python
import functools

import jax
import jax.numpy as jnp
from jax import lax
from jax.sharding import PartitionSpec as P

WINDOW = 128
CAP = 176
EPSILON = 1e-05
MASKED = -1e30

F32 = jnp.float32
BF16 = jnp.bfloat16


def norm_factor(values):
    return lax.rsqrt(jnp.mean(values * values, axis=-1, keepdims=True) + EPSILON)


def norm_back(values, factor, gain_row, upstream):
    features = values.shape[-1]
    inner = jnp.sum(values * gain_row * upstream, axis=-1, keepdims=True)
    return factor * gain_row * upstream - values * factor**3 * inner / features


def softmax_rows(logits):
    highest = jnp.max(logits, axis=-1, keepdims=True)
    raised = jnp.exp(logits - highest)
    return raised / jnp.sum(raised, axis=-1, keepdims=True)


def dot(spec, left, right):
    return jnp.einsum(spec, left, right, preferred_element_type=F32)


def swap_blocks(blocks, ranks):
    own = lax.axis_index("dp")
    result = jnp.zeros_like(blocks)
    kept = lax.dynamic_index_in_dim(blocks, own, 0, keepdims=True)
    result = lax.dynamic_update_slice_in_dim(result, kept, own, 0)
    for shift in range(1, ranks):
        target = lax.rem(own + shift, ranks)
        origin = lax.rem(own + ranks - shift, ranks)
        block = lax.dynamic_index_in_dim(blocks, target, 0, keepdims=True)
        moved = lax.ppermute(block, "dp", [(j, (j + shift) % ranks) for j in range(ranks)])
        result = lax.dynamic_update_slice_in_dim(result, moved, origin, 0)
    return result


def body(
    ranks,
    quarters,
    tokens,
    cotangent,
    segments,
    expert_ids,
    attn_gain,
    w_qkv,
    qk_gain,
    w_out,
    mlp_gain,
    router,
    expert_in,
    expert_out,
):
    everyone = ("dp", "tensor")
    rank = lax.axis_index("dp")
    quarter = lax.axis_index("tensor")
    local_rows, micro_count, features = tokens.shape
    experts, depth, _, width = expert_in.shape
    owned = experts // ranks
    local_tokens = local_rows * micro_count
    group_tokens = quarters * local_tokens
    all_tokens = ranks * group_tokens
    head_dim = qk_gain.shape[0] * ranks
    local_heads = qk_gain.shape[2]
    local_width = local_heads * head_dim
    seq_len = local_rows * quarters
    scale = head_dim ** (-0.5)

    in_blocks = expert_in.reshape(ranks, owned, depth, 2 * width)
    out_blocks = expert_out.reshape(ranks, owned, depth, width)
    held_in = swap_blocks(in_blocks, ranks)
    held_out = swap_blocks(out_blocks, ranks)

    full_qkv = lax.all_gather(w_qkv, "dp", axis=0, tiled=True)
    full_out = lax.all_gather(w_out, "dp", axis=0, tiled=True)
    small = jnp.concatenate(
        [router, attn_gain[:, None], mlp_gain[:, None]], axis=1
    ).reshape(1, -1)
    small = jnp.concatenate([small, qk_gain.reshape(1, -1)], axis=1)
    small = lax.all_gather(small, "dp", axis=0, tiled=True)
    columns = experts + 2
    small_rows = small[:, : depth * columns].reshape(features, columns)
    full_router = small_rows[:, :experts]
    gain_one = small_rows[:, experts].astype(F32)
    gain_two = small_rows[:, experts + 1].astype(F32)
    full_qk = small[:, depth * columns :].reshape(head_dim, 2, local_heads)
    all_ids = lax.all_gather(expert_ids, "dp", axis=0, tiled=True)

    raw_rows = lax.all_gather(tokens, "tensor", axis=0, tiled=True).astype(F32)
    rows_one = (raw_rows * norm_factor(raw_rows) * gain_one).astype(BF16)
    projected = dot("smd,djf->jmsf", rows_one, full_qkv)
    query_raw = projected[0]
    key_raw = projected[1]
    value_rows = projected[2].astype(BF16)
    square_q, square_k = lax.psum(
        (jnp.sum(query_raw * query_raw, axis=-1), jnp.sum(key_raw * key_raw, axis=-1)), "tensor"
    )
    factor_q = lax.rsqrt(square_q[..., None] / features + EPSILON)
    factor_k = lax.rsqrt(square_k[..., None] / features + EPSILON)
    qk_rows = jnp.transpose(full_qk.astype(F32), (1, 2, 0)).reshape(2, local_width)
    heads_shape = (micro_count, seq_len, local_heads, head_dim)
    query_heads = (query_raw * factor_q * qk_rows[0]).astype(BF16).reshape(heads_shape)
    key_heads = (key_raw * factor_k * qk_rows[1]).astype(BF16).reshape(heads_shape)
    value_heads = value_rows.reshape(heads_shape)
    seq_major = segments.T
    positions = jnp.arange(seq_len)
    distance = positions[:, None] - positions[None, :]
    same_doc = seq_major[:, :, None] == seq_major[:, None, :]
    allowed = (same_doc & (distance >= 0) & (distance < WINDOW))[:, None]
    scores = jnp.where(allowed, dot("mqhc,mkhc->mhqk", query_heads, key_heads) * scale, MASKED)
    weights_full = softmax_rows(scores)
    weights_low = weights_full.astype(BF16)
    head_out = dot("mhqk,mkhc->mqhc", weights_low, value_heads).astype(BF16)
    head_out = head_out.reshape(micro_count, seq_len, local_width)
    attended = lax.psum_scatter(
        dot("msf,df->smd", head_out, full_out), "tensor", scatter_dimension=0, tiled=True
    )
    inputs = tokens.astype(F32)
    residual = inputs + attended
    factor_two = norm_factor(residual)
    normed_two = (residual * factor_two * gain_two).astype(BF16)

    rows_all = lax.all_gather(
        normed_two.reshape(local_tokens, features), everyone, axis=0, tiled=True
    )
    pull_all = lax.all_gather(
        cotangent.reshape(local_tokens, features), everyone, axis=0, tiled=True
    )
    router_probs = softmax_rows(dot("td,de->te", rows_all, full_router))

    first = rank * owned
    routes = all_ids.reshape(ranks, group_tokens, -1)
    names = first + jnp.arange(owned, dtype=jnp.int32)
    member = jnp.any(routes[None] == names[:, None, None, None], axis=-1)
    order = jnp.arange(group_tokens)
    earlier = (order[:, None] < order[None, :]).astype(BF16)
    position = dot("egs,st->egt", member.astype(BF16), earlier)
    position = jnp.where(member, position, -1.0).astype(jnp.int32)
    place = position[:, :, None, :] == jnp.arange(CAP, dtype=jnp.int32)[:, None]
    gate_own = lax.dynamic_slice_in_dim(router_probs, first, owned, 1)
    gate_own = gate_own.T.reshape(owned, ranks, 1, group_tokens)
    gate_slot = jnp.sum(jnp.where(place, gate_own, 0.0), axis=-1)
    place = place.astype(BF16)
    grouped_rows = rows_all.reshape(ranks, group_tokens, features)
    grouped_pull = pull_all.reshape(ranks, group_tokens, features)

    mixed_rows = []
    returned_rows = []
    slot_dots = []
    grads_in = []
    grads_out = []
    for e in range(owned):
        weight_in = held_in[:, e].reshape(features, 2 * width)
        weight_out = held_out[:, e].reshape(features, width)
        slots = ranks * CAP
        chosen = dot("gpt,gtd->gpd", place[e], grouped_rows).astype(BF16).reshape(slots, features)
        pulled = dot("gpt,gtd->gpd", place[e], grouped_pull).astype(BF16).reshape(slots, features)
        gate = gate_slot[e].reshape(slots, 1)
        gate_up = dot("sd,df->sf", chosen, weight_in)
        gate_part = gate_up[:, :width]
        up_part = gate_up[:, width:]
        sigmoid_gate = jax.nn.sigmoid(gate_part)
        activated = gate_part * sigmoid_gate
        hidden = activated * up_part
        d_plain = dot("sd,df->sf", pulled, weight_out)
        slot_dots.append(jnp.sum(hidden * d_plain, axis=-1))
        d_hidden = d_plain * gate
        d_gate_part = d_hidden * up_part * sigmoid_gate * (1.0 + gate_part * (1.0 - sigmoid_gate))
        d_gate_up = jnp.concatenate([d_gate_part, d_hidden * activated], axis=1).astype(BF16)
        hidden_gated = (hidden * gate).astype(BF16)
        mixed_rows.append(
            dot("sf,df->sd", hidden_gated, weight_out).astype(BF16).reshape(ranks, CAP, features)
        )
        returned_rows.append(
            dot("sf,df->sd", d_gate_up, weight_in).astype(BF16).reshape(ranks, CAP, features)
        )
        grads_in.append(dot("sd,sf->df", chosen, d_gate_up).astype(BF16))
        grads_out.append(dot("sd,sf->df", pulled, hidden_gated).astype(BF16))
    slot_dots = jnp.stack(slot_dots).reshape(owned, ranks, CAP, 1)
    d_gate_token = jnp.sum(jnp.where(place > 0, slot_dots, 0.0), axis=2)
    d_gate_token = d_gate_token.reshape(owned, all_tokens).T
    spread = lax.dynamic_update_slice(
        jnp.zeros((all_tokens, 128), F32), d_gate_token, (0, first)
    ).astype(BF16)
    mixed = jnp.stack(mixed_rows)
    returned = jnp.stack(returned_rows)
    mixture_all = dot("egpt,egpd->gtd", place, mixed).astype(BF16)
    returned_all = dot("egpt,egpd->gtd", place, returned).astype(BF16)
    returned_all = jnp.concatenate([returned_all.reshape(all_tokens, features), spread], axis=1)
    returned_own = lax.psum_scatter(returned_all, everyone, scatter_dimension=0, tiled=True)
    mixture_own = lax.psum_scatter(
        mixture_all.reshape(all_tokens, features), everyone, scatter_dimension=0, tiled=True
    )
    layer_out = (
        residual + mixture_own.astype(F32).reshape(local_rows, micro_count, features)
    ).astype(BF16)

    def home(parts):
        stacked = jnp.stack([part.reshape(ranks, depth, -1) for part in parts], axis=1)
        return swap_blocks(stacked, ranks).reshape(experts, depth, -1).astype(F32)

    grad_expert_in = home(grads_in).reshape(experts, depth, 2, width)
    grad_expert_out = home(grads_out)

    returned_f = returned_own[:, :features].astype(F32).reshape(local_rows, micro_count, features)
    d_probs = returned_own[:, features : features + experts].astype(F32)
    first_token = (rank * quarters + quarter) * local_tokens
    probs_own = lax.dynamic_slice_in_dim(router_probs, first_token, local_tokens, 0)
    d_logits = (
        probs_own * (d_probs - jnp.sum(d_probs * probs_own, axis=-1, keepdims=True))
    ).astype(BF16)
    d_normed_two = returned_f + dot("te,de->td", d_logits, full_router).reshape(residual.shape)
    grad_router = dot("td,te->de", normed_two.reshape(local_tokens, features), d_logits)
    d_residual = cotangent.astype(F32) + norm_back(residual, factor_two, gain_two, d_normed_two)
    grad_gain_two = jnp.sum(residual * factor_two * d_normed_two, axis=(0, 1))
    d_attended = d_residual.astype(BF16)

    rows_back = lax.all_gather(d_attended, "tensor", axis=0, tiled=True)
    d_head_out = dot("smd,df->msf", rows_back, full_out).astype(BF16)
    grad_w_out = dot("smd,msf->df", rows_back, head_out)
    d_heads = d_head_out.reshape(heads_shape)
    d_weights = dot("mqhc,mkhc->mhqk", d_heads, value_heads)
    d_scores = (
        weights_full * (d_weights - jnp.sum(d_weights * weights_full, axis=-1, keepdims=True))
    ).astype(BF16)
    flat_shape = (micro_count, seq_len, local_width)
    d_queries = (dot("mhqk,mkhc->mqhc", d_scores, key_heads) * scale).reshape(flat_shape)
    d_keys = (dot("mhqk,mqhc->mkhc", d_scores, query_heads) * scale).reshape(flat_shape)
    d_values = dot("mhqk,mqhc->mkhc", weights_low, d_heads).reshape(flat_shape).astype(BF16)
    inner_q, inner_k = lax.psum(
        (
            jnp.sum(query_raw * qk_rows[0] * d_queries, axis=-1),
            jnp.sum(key_raw * qk_rows[1] * d_keys, axis=-1),
        ),
        "tensor",
    )
    d_query_raw = (
        factor_q * qk_rows[0] * d_queries - query_raw * factor_q**3 * inner_q[..., None] / features
    )
    d_key_raw = (
        factor_k * qk_rows[1] * d_keys - key_raw * factor_k**3 * inner_k[..., None] / features
    )
    grad_qk_rows = jnp.stack(
        [
            jnp.sum(query_raw * factor_q * d_queries, axis=(0, 1)),
            jnp.sum(key_raw * factor_k * d_keys, axis=(0, 1)),
        ]
    )
    grad_qk = jnp.transpose(grad_qk_rows.reshape(2, local_heads, head_dim), (2, 0, 1))
    d_projected = jnp.stack([d_query_raw.astype(BF16), d_key_raw.astype(BF16), d_values])
    grad_qkv = dot("smd,jmsf->djf", rows_one, d_projected)
    d_normed_one = lax.psum_scatter(
        dot("jmsf,djf->smd", d_projected, full_qkv).astype(BF16),
        "tensor",
        scatter_dimension=0,
        tiled=True,
    ).astype(F32)
    factor_one = norm_factor(inputs)
    grad_tokens = (d_residual + norm_back(inputs, factor_one, gain_one, d_normed_one)).astype(BF16)
    grad_gain_one = jnp.sum(inputs * factor_one * d_normed_one, axis=(0, 1))

    grad_qkv_own = lax.psum_scatter(
        grad_qkv.astype(BF16), "dp", scatter_dimension=0, tiled=True
    ).astype(F32)
    grad_out_own = lax.psum_scatter(
        grad_w_out.astype(BF16), "dp", scatter_dimension=0, tiled=True
    ).astype(F32)
    small_grads = jnp.concatenate(
        [grad_router, grad_gain_one[:, None], grad_gain_two[:, None]], axis=1
    ).reshape(ranks, -1)
    small_grads = jnp.concatenate([small_grads, grad_qk.reshape(ranks, -1)], axis=1)
    small_own = lax.psum_scatter(small_grads, "dp", scatter_dimension=0, tiled=True)[0]
    grad_qk_own = small_own[depth * columns :].reshape(qk_gain.shape)
    shared_own = lax.psum(small_own[: depth * columns], "tensor").reshape(depth, columns)
    return (
        layer_out,
        grad_tokens,
        shared_own[:, experts],
        grad_qkv_own,
        grad_qk_own,
        grad_out_own,
        shared_own[:, experts + 1],
        shared_own[:, :experts],
        grad_expert_in,
        grad_expert_out,
    )


def solution(mesh):
    placed = (
        P(("dp", "tensor"), None, None),
        P(("dp", "tensor"), None, None),
        P("dp", None),
        P("dp", None, None),
        P("dp"),
        P("dp", None, "tensor"),
        P("dp", None, "tensor"),
        P("dp", "tensor"),
        P("dp"),
        P("dp", None),
        P(None, "dp", None, "tensor"),
        P(None, "dp", "tensor"),
    )
    return jax.shard_map(
        functools.partial(body, mesh.shape["dp"], mesh.shape["tensor"]),
        mesh=mesh,
        in_specs=placed,
        out_specs=(
            P(("dp", "tensor"), None, None),
            P(("dp", "tensor"), None, None),
            P("dp"),
            P("dp", None, "tensor"),
            P("dp", None, "tensor"),
            P("dp", "tensor"),
            P("dp"),
            P("dp", None),
            P(None, "dp", None, "tensor"),
            P(None, "dp", "tensor"),
        ),
        check_vma=False,
    )
```

```python
import functools
import itertools

import jax
import jax.numpy as jnp
from jax import lax
from jax.experimental import pallas as pl
from jax.experimental.pallas import tpu as pltpu
from jax.sharding import PartitionSpec as P

WINDOW = 128
CAP = 176
EPSILON = 1e-05
MASKED = -1e30

MESH = pl.DeviceIdType.MESH
F32 = jnp.float32
BF16 = jnp.bfloat16


def norm_factor(values):
    return lax.rsqrt(jnp.mean(values * values, axis=-1, keepdims=True) + EPSILON)


def norm_back(values, factor, gain_row, upstream):
    features = values.shape[-1]
    inner = jnp.sum(values * gain_row * upstream, axis=-1, keepdims=True)
    return factor * gain_row * upstream - values * factor**3 * inner / features


def softmax_rows(logits):
    highest = jnp.max(logits, axis=-1, keepdims=True)
    raised = jnp.exp(logits - highest)
    return raised / jnp.sum(raised, axis=-1, keepdims=True)


def dot(spec, left, right):
    return jnp.einsum(spec, left, right, preferred_element_type=F32)


def mesh_places(ranks):
    rank = lax.axis_index("dp")
    quarter = lax.axis_index("tensor")
    return rank // 2, {
        "inner": lax.rem(rank, 2),
        "side": quarter // 2,
        "core": lax.rem(quarter, 2),
    }


def device_at(ranks, steps, flips):
    outer, pairs = mesh_places(ranks)
    place = {name: 1 - at if name in flips else at for name, at in pairs.items()}
    return (outer + steps) * 2 + place["inner"], place["side"] * 2 + place["core"]


def run_if(conditions, action):
    conditions = [condition for condition in conditions if condition is not None]
    if not conditions:
        action()
        return
    pl.when(functools.reduce(jnp.logical_and, conditions))(action)


def on_chain(ranks, steps):
    outer, _ = mesh_places(ranks)
    if steps == 0:
        return None
    return outer + steps < ranks // 2 if steps > 0 else outer + steps >= 0


def greet(ranks, pieces):
    barrier = pltpu.get_barrier_semaphore()
    pairs = sorted({name for piece in pieces for name in piece[4]})
    targets = [(None, 0, (name,)) for name in pairs]
    if any(piece[3] for piece in pieces):
        targets += [(on_chain(ranks, steps), steps, ()) for steps in (-1, 1)]

    def signal(steps, flips):
        target = device_at(ranks, steps, flips)
        pl.semaphore_signal(barrier, inc=1, device_id=target, device_id_type=MESH)

    expected = len(pairs)
    for condition, steps, flips in targets:
        run_if([condition], functools.partial(signal, steps, flips))
        if condition is not None:
            expected = expected + condition.astype(jnp.int32)
    pl.semaphore_wait(barrier, expected)


def chain_steps(ranks, outer):
    count = ranks // 2
    return [0] + [sign * k for k in range(1, count) for sign in (-1, 1)] if outer else [0]


def row_start(ranks, piece, steps, flips, rows):
    rank, quarter = device_at(ranks, steps, flips)
    if not piece[3]:
        index = quarter
    elif "side" not in piece[4]:
        index = rank
    else:
        index = rank * 4 + quarter
    return pl.ds(pl.multiple_of(index * rows, rows), rows)


def all_bits(dims):
    return list(itertools.product((0, 1), repeat=len(dims)))


def level_of(bits):
    return max((n + 1 for n, bit in enumerate(bits) if bit), default=0)


def gather_kernel(ranks, arrays, pieces, *refs):
    in_refs, out_refs = refs[:arrays], refs[arrays : 2 * arrays]
    send_sem, recv_sem, local_sem = refs[2 * arrays :]
    count = ranks // 2
    greet(ranks, pieces)
    started = []

    def flips_of(p, bits):
        return tuple(name for name, bit in zip(pieces[p][4], bits) if bit)

    def copy(p, steps, bits, as_seen, target_steps, target_flips):
        array, start, width, _, dims = pieces[p]
        rows = in_refs[array].shape[0]
        columns = pl.ds(start, width)
        place = out_refs[array].at[
            row_start(ranks, pieces[p], steps, flips_of(p, bits), rows), columns
        ]
        own = steps == 0 and not any(bits)
        seen_steps, seen_bits = as_seen
        sem = (seen_steps + count - 1) * 2 ** len(dims) + all_bits(dims).index(seen_bits)
        return pltpu.make_async_remote_copy(
            src_ref=in_refs[array].at[:, columns] if own else place,
            dst_ref=place,
            send_sem=send_sem.at[p, sem],
            recv_sem=recv_sem.at[p, sem],
            device_id=device_at(ranks, target_steps, target_flips),
            device_id_type=MESH,
        )

    def send(conditions, *description):
        run_if(conditions, lambda: copy(*description).start())
        started.append((conditions, description))

    def forward(p, steps, bits):
        outer, dims = pieces[p][3:]
        here = on_chain(ranks, steps)
        level = level_of(bits)
        if outer and level == 0:
            for direction in (-1, 1):
                if steps * direction <= 0 and abs(steps) < count - 1:
                    there = on_chain(ranks, direction)
                    seen = (steps - direction, bits)
                    send([here, there], p, steps, bits, seen, direction, ())
        for n in range(level, len(dims)):
            seen = (steps, bits[:n] + (1,) + bits[n + 1 :])
            send([here], p, steps, bits, seen, 0, (dims[n],))

    def receive(p, steps, bits):
        here = on_chain(ranks, steps)
        run_if([here], lambda: copy(p, steps, bits, (steps, bits), 0, (pieces[p][4][0],)).wait_recv())
        forward(p, steps, bits)

    kept = []
    for array in range(arrays):
        piece = next(piece for piece in pieces if piece[0] == array)
        rows = in_refs[array].shape[0]
        keep = pltpu.make_async_copy(
            in_refs[array],
            out_refs[array].at[row_start(ranks, piece, 0, (), rows)],
            local_sem.at[array],
        )
        keep.start()
        kept.append(keep)
    events = []
    for p, (_, _, _, outer, dims) in enumerate(pieces):
        for n, steps in enumerate(chain_steps(ranks, outer)):
            for bits in all_bits(dims):
                level = level_of(bits)
                turn = len(dims) + 1 if level == len(dims) else max(level - 1, 0)
                events.append((turn, abs(steps), n, level, p, steps, bits))
    for event in sorted(event for event in events if event[1] == 0 and event[3] == 0):
        forward(*event[4:])
    for event in sorted(event for event in events if event[1] or event[3]):
        receive(*event[4:])
    for conditions, description in started:
        run_if(conditions, lambda: copy(*description).wait_send())
    for keep in kept:
        keep.wait()


def gather_blocks(blocks, results, pieces, ranks, collective_id):
    arrays = len(blocks)
    transfers = (ranks - 1) * 8
    return pl.pallas_call(
        functools.partial(gather_kernel, ranks, arrays, pieces),
        out_shape=tuple(
            jax.ShapeDtypeStruct((number * block.shape[0], block.shape[1]), block.dtype)
            for block, number in zip(blocks, results)
        ),
        in_specs=[pl.BlockSpec(memory_space=pl.ANY)] * arrays,
        out_specs=(pl.BlockSpec(memory_space=pl.ANY),) * arrays,
        scratch_shapes=[
            pltpu.SemaphoreType.DMA((len(pieces), transfers)),
            pltpu.SemaphoreType.DMA((len(pieces), transfers)),
            pltpu.SemaphoreType.DMA((arrays,)),
        ],
        compiler_params=pltpu.CompilerParams(collective_id=collective_id, has_side_effects=True),
        cost_estimate=pl.CostEstimate(
            flops=0,
            bytes_accessed=sum(2 * n * block.size for block, n in zip(blocks, results)),
            transcendentals=0,
        ),
    )(*blocks)


def gather_everywhere(block, ranks, collective_id):
    half = block.shape[1] // 2
    pieces = (
        (0, 0, half, True, ("inner", "side", "core")),
        (0, half, half, True, ("side", "inner", "core")),
    )
    return gather_blocks([block], [4 * ranks], pieces, ranks, collective_id)[0]


def scatter_kernel(ranks, pieces, in_ref, out_ref, *scratch):
    buffers, (send_sem, recv_sem, load_sem) = scratch[:-3], scratch[-3:]
    rows = out_ref.shape[0]
    count = ranks // 2
    tile = min(rows, 32)
    greet(ranks, pieces)
    outer_place, _ = mesh_places(ranks)
    started = []
    held = []
    for _, _, _, _, dims in pieces:
        depth = len(dims)
        own, *paired = buffers[: depth + 1]
        up, down = buffers[depth + 1 : depth + 3]
        held.append((own, paired, up, down))
        buffers = buffers[depth + 3 :]

    def region(p, steps, bits):
        _, start, width, _, dims = pieces[p]
        flips = tuple(name for name, bit in zip(dims, bits) if bit)
        return in_ref.at[row_start(ranks, pieces[p], steps, flips, rows), pl.ds(start, width)]

    def slot(steps, bits):
        place = outer_place + steps if pieces[0][3] else 0
        number = 0
        for bit in bits:
            number = 2 * number + bit
        return place * 2 ** len(bits) + number

    def sem_of(steps, bits, kind):
        code = 0
        for bit in bits:
            code = 2 * code + bit
        return ((steps + count - 1) * 2 ** len(bits) + code) * 2 + kind

    def own_at(p, steps, bits):
        return held[p][0].at[slot(steps, bits)]

    def load(p, steps, bits):
        return pltpu.make_async_copy(
            region(p, steps, bits + (0,)),
            own_at(p, steps, bits),
            load_sem.at[p, sem_of(steps, bits, 0) // 2],
        )

    def pair_copy(p, steps, bits, n):
        dims = pieces[p][4]
        whole = bits[:n] + (1,) + (0,) * (len(dims) - n - 1)
        last = n == len(dims) - 1
        return pltpu.make_async_remote_copy(
            src_ref=region(p, steps, whole) if last else own_at(p, steps, whole[:-1]),
            dst_ref=held[p][1][n].at[slot(steps, bits[:n])],
            send_sem=send_sem.at[p, sem_of(steps, whole, 0)],
            recv_sem=recv_sem.at[p, sem_of(steps, whole, 0)],
            device_id=device_at(ranks, 0, (dims[n],)),
            device_id_type=MESH,
        )

    def chain_copy(p, steps, direction):
        zeros = (0,) * (len(pieces[p][4]) - 1)
        sem = sem_of(steps - direction, zeros + (0,), 1)
        return pltpu.make_async_remote_copy(
            src_ref=own_at(p, steps, zeros),
            dst_ref=held[p][2 if direction > 0 else 3].at[slot(steps, ())],
            send_sem=send_sem.at[p, sem + (0 if direction > 0 else 2)],
            recv_sem=recv_sem.at[p, sem + (0 if direction > 0 else 2)],
            device_id=device_at(ranks, direction, ()),
            device_id_type=MESH,
        )

    def chain_arrival(p, steps, direction):
        zeros = (0,) * (len(pieces[p][4]) - 1)
        sem = sem_of(steps, zeros + (0,), 1) + (0 if direction > 0 else 2)
        place = held[p][2 if direction > 0 else 3].at[slot(steps, ())]
        return pltpu.make_async_remote_copy(
            src_ref=place,
            dst_ref=place,
            send_sem=send_sem.at[p, sem],
            recv_sem=recv_sem.at[p, sem],
            device_id=device_at(ranks, -direction, ()),
            device_id_type=MESH,
        )

    def add(target, sources):
        def step(n, carry):
            part = pl.ds(pl.multiple_of(n * tile, tile), tile)
            total = sources[0][part].astype(F32)
            for source in sources[1:]:
                total = total + source[part].astype(F32)
            target[part] = total.astype(target.dtype)
            return carry

        lax.fori_loop(0, rows // tile, step, 0)

    order = []
    for p, (_, _, _, outer, dims) in enumerate(pieces):
        for n, steps in enumerate(chain_steps(ranks, outer)):
            for bits in all_bits(dims[:-1]):
                order.append((-level_of(bits), -abs(steps), n, p, steps, bits))
    order = [entry[3:] for entry in sorted(order)]
    for p, steps, bits in order:
        here = on_chain(ranks, steps)
        last = len(pieces[p][4]) - 1

        def begin(p=p, steps=steps, bits=bits, last=last):
            pair_copy(p, steps, bits, last).start()
            load(p, steps, bits).start()

        run_if([here], begin)
        started.append(([here], functools.partial(pair_copy, p, steps, bits, last)))
    for p, steps, bits in order:
        here = on_chain(ranks, steps)
        dims = pieces[p][4]
        level = level_of(bits)
        own, paired, up, down = held[p]

        def gather_terms(p=p, steps=steps, bits=bits, level=level, dims=dims, paired=paired):
            load(p, steps, bits).wait()
            sources = [own_at(p, steps, bits)]
            for n in range(len(dims) - 1, level - 1, -1):
                pair_copy(p, steps, bits, n).wait_recv()
                sources.append(paired[n].at[slot(steps, bits[:n])])
            add(own_at(p, steps, bits), sources)

        run_if([here], gather_terms)
        if level:

            def send_pair(p=p, steps=steps, bits=bits, level=level):
                return pair_copy(p, steps, bits, level - 1)

            run_if([here], lambda: send_pair().start())
            started.append(([here], send_pair))
            continue
        if pieces[p][3]:
            for direction in (1, -1):
                if steps * direction < 0 or abs(steps) == count - 1:
                    continue
                behind = on_chain(ranks, -direction)

                def take(p=p, steps=steps, bits=bits, direction=direction):
                    chain_arrival(p, steps, direction).wait_recv()
                    arrived = held[p][2 if direction > 0 else 3].at[slot(steps, ())]
                    add(own_at(p, steps, bits), [own_at(p, steps, bits), arrived])

                run_if([here, behind], take)
        if steps:
            direction = 1 if steps > 0 else -1

            def send_chain(p=p, steps=steps, direction=direction):
                return chain_copy(p, steps, direction)

            run_if([here], lambda: send_chain().start())
            started.append(([here], send_chain))
        else:
            start, width = pieces[p][1:3]
            begin_column = start - pieces[0][1]
            add(out_ref.at[:, pl.ds(begin_column, width)], [own_at(p, 0, bits)])
    for conditions, build in started:
        run_if(conditions, lambda: build().wait_send())


def scatter_blocks(array, pieces, blocks, ranks, collective_id):
    rows = array.shape[0] // blocks
    columns = sum(piece[2] for piece in pieces)
    count = ranks // 2
    scratch = []
    for _, _, width, outer, dims in pieces:
        chain = count if outer else 1
        sizes = [chain * 2 ** (len(dims) - 1)]
        sizes += [chain * 2**n for n in range(len(dims))]
        sizes += [chain, chain] if outer else [1, 1]
        scratch += [pltpu.VMEM((size, rows, width), array.dtype) for size in sizes]
    transfers = ranks * 8 * 2
    return pl.pallas_call(
        functools.partial(scatter_kernel, ranks, pieces),
        out_shape=jax.ShapeDtypeStruct((rows, columns), array.dtype),
        in_specs=[pl.BlockSpec(memory_space=pl.ANY)],
        out_specs=pl.BlockSpec(memory_space=pltpu.VMEM),
        scratch_shapes=[
            *scratch,
            pltpu.SemaphoreType.DMA((len(pieces), transfers)),
            pltpu.SemaphoreType.DMA((len(pieces), transfers)),
            pltpu.SemaphoreType.DMA((len(pieces), transfers)),
        ],
        compiler_params=pltpu.CompilerParams(
            collective_id=collective_id,
            has_side_effects=True,
            vmem_limit_bytes=56 * 1024 * 1024,
        ),
        cost_estimate=pl.CostEstimate(
            flops=array.shape[0] * columns,
            bytes_accessed=2 * array.shape[0] * columns,
            transcendentals=0,
        ),
    )(array)


def scatter_everywhere(array, ranks, collective_id):
    tiles = array.shape[1] // 128
    calls = max(1, ranks // 8)
    results = []
    for call in range(calls):
        first, last = tiles * call // calls, tiles * (call + 1) // calls
        middle = (first + last + 1) // 2
        pieces = (
            (0, first * 128, (middle - first) * 128, True, ("inner", "side", "core")),
            (0, middle * 128, (last - middle) * 128, True, ("side", "inner", "core")),
        )
        results.append(scatter_blocks(array, pieces, 4 * ranks, ranks, collective_id + call))
    return results[0] if calls == 1 else jnp.concatenate(results, axis=1)


def send_blocks(blocks, ranks):
    own = lax.axis_index("dp")
    received = []
    for shift in range(1, ranks):
        target = lax.rem(own + shift, ranks)
        origin = lax.rem(own + ranks - shift, ranks)
        block = lax.dynamic_index_in_dim(blocks, target, 0, keepdims=True)
        moved = lax.ppermute(block, "dp", [(j, (j + shift) % ranks) for j in range(ranks)])
        received.append((origin, moved))
    return received


def join_blocks(blocks, received):
    for origin, block in received:
        blocks = lax.dynamic_update_slice_in_dim(blocks, block, origin, 0)
    return blocks


def tie(value, received, first, last):
    blocks = [block for _, block in received[first:last]]
    if not blocks:
        return value, received
    value, blocks = lax.optimization_barrier((value, blocks))
    renewed = [(origin, block) for (origin, _), block in zip(received[first:last], blocks)]
    return value, received[:first] + renewed + received[last:]


def expert_kernel(
    owned,
    width,
    rows_ref,
    pull_ref,
    position_ref,
    gate_ref,
    column_ref,
    weight_ref,
    mixture_ref,
    returned_ref,
    chosen_ref,
    pulled_ref,
    d_gate_up_ref,
    hidden_ref,
    place_ref,
    mixed_ref,
    back_ref,
):
    group_tokens, features = rows_ref.shape
    chunk = min(features, 512)
    slot = lax.broadcasted_iota(jnp.int32, (CAP, group_tokens), 0)
    last = (((1,), (1,)), ((), ()))
    first = (((0,), (0,)), ((), ()))
    for e in range(owned):
        place_ref[e * CAP : (e + 1) * CAP] = (position_ref[0, e : e + 1] == slot).astype(BF16)
    for start in range(0, features, chunk):
        columns = slice(start, start + chunk)
        chosen = jnp.dot(place_ref[...], rows_ref[:, columns], preferred_element_type=F32)
        chosen_ref[:, 0, :, columns] = chosen.astype(BF16).reshape(owned, CAP, chunk)
        pulled = jnp.dot(place_ref[...], pull_ref[:, columns], preferred_element_type=F32)
        pulled_ref[:, 0, :, columns] = pulled.astype(BF16).reshape(owned, CAP, chunk)
    spread = jnp.zeros((group_tokens, 128), F32)
    for e in range(owned):
        weight_in = weight_ref[:, e, :, : 2 * width].reshape(features, 2 * width)
        weight_out = weight_ref[:, e, :, 2 * width :].reshape(features, width)
        here = position_ref[0, e : e + 1] == slot
        gate = jnp.sum(jnp.where(here, gate_ref[0, e : e + 1], 0.0), axis=1, keepdims=True)
        gate_up = jnp.dot(chosen_ref[e, 0], weight_in, preferred_element_type=F32)
        d_plain = jnp.dot(pulled_ref[e, 0], weight_out, preferred_element_type=F32)
        gate_part = gate_up[:, :width]
        up_part = gate_up[:, width:]
        sigmoid_gate = jax.nn.sigmoid(gate_part)
        activated = gate_part * sigmoid_gate
        hidden = activated * up_part
        slot_dots = jnp.sum(hidden * d_plain, axis=1, keepdims=True)
        spread = spread + lax.dot_general(
            place_ref[e * CAP : (e + 1) * CAP],
            (slot_dots * column_ref[e : e + 1]).astype(BF16),
            first,
            preferred_element_type=F32,
        )
        d_hidden = d_plain * gate
        d_gate_part = d_hidden * up_part * sigmoid_gate * (1.0 + gate_part * (1.0 - sigmoid_gate))
        d_up_part = d_hidden * activated
        hidden_ref[e, 0] = (hidden * gate).astype(BF16)
        d_gate_up_ref[e, 0, :, :width] = d_gate_part.astype(BF16)
        d_gate_up_ref[e, 0, :, width:] = d_up_part.astype(BF16)
        mixed_ref[e * CAP : (e + 1) * CAP] = lax.dot_general(
            hidden_ref[e, 0], weight_out, last, preferred_element_type=F32
        ).astype(BF16)
        back_ref[e * CAP : (e + 1) * CAP] = lax.dot_general(
            d_gate_up_ref[e, 0], weight_in, last, preferred_element_type=F32
        ).astype(BF16)
    returned_ref[:, features:] = spread.astype(BF16)
    for start in range(0, features, chunk):
        columns = slice(start, start + chunk)
        mixture_ref[:, columns] = lax.dot_general(
            place_ref[...], mixed_ref[:, columns], first, preferred_element_type=F32
        ).astype(BF16)
        returned_ref[:, columns] = lax.dot_general(
            place_ref[...], back_ref[:, columns], first, preferred_element_type=F32
        ).astype(BF16)


def expert_math(rows, pull, position, gate, column, weights):
    groups, owned, group_tokens = position.shape
    tokens, features = rows.shape
    ranks, _, depth, _ = weights.shape
    width = weights.shape[3] // 3
    slots = owned * CAP
    by_rows = pl.BlockSpec((group_tokens, features), lambda g: (g, 0))
    by_group = pl.BlockSpec((1, owned, group_tokens), lambda g: (g, 0, 0))

    def by_slots(columns):
        return pl.BlockSpec((owned, 1, CAP, columns), lambda g: (0, g, 0, 0))

    def slot_array(columns):
        return jax.ShapeDtypeStruct((owned, groups, CAP, columns), BF16)

    flops = 2 * groups * slots * features * (4 * group_tokens + 6 * width)
    return pl.pallas_call(
        functools.partial(expert_kernel, owned, width),
        grid=(groups,),
        out_shape=(
            jax.ShapeDtypeStruct((tokens, features), BF16),
            jax.ShapeDtypeStruct((tokens, features + 128), BF16),
            slot_array(features),
            slot_array(features),
            slot_array(2 * width),
            slot_array(width),
        ),
        in_specs=[
            by_rows,
            by_rows,
            by_group,
            by_group,
            pl.BlockSpec((owned, 128), lambda g: (0, 0)),
            pl.BlockSpec(
                (ranks, owned, depth, 3 * width),
                lambda g: (0, 0, 0, 0),
                pipeline_mode=pl.Buffered(1),
            ),
        ],
        out_specs=(
            by_rows,
            pl.BlockSpec((group_tokens, features + 128), lambda g: (g, 0)),
            by_slots(features),
            by_slots(features),
            by_slots(2 * width),
            by_slots(width),
        ),
        scratch_shapes=[
            pltpu.VMEM((slots, group_tokens), BF16),
            pltpu.VMEM((slots, features), BF16),
            pltpu.VMEM((slots, features), BF16),
        ],
        input_output_aliases={1: 0},
        compiler_params=pltpu.CompilerParams(vmem_limit_bytes=60 * 1024 * 1024),
        cost_estimate=pl.CostEstimate(
            flops=flops, bytes_accessed=4 * tokens * features * 2 + slots * groups * features * 4, transcendentals=0
        ),
    )(rows, pull, position, gate, column, weights)


def body(
    ranks,
    quarters,
    tokens,
    cotangent,
    segments,
    expert_ids,
    attn_gain,
    w_qkv,
    qk_gain,
    w_out,
    mlp_gain,
    router,
    expert_in,
    expert_out,
):
    rank = lax.axis_index("dp")
    quarter = lax.axis_index("tensor")
    local_rows, micro_count, features = tokens.shape
    experts, depth, _, width = expert_in.shape
    top_count = expert_ids.shape[2]
    owned = experts // ranks
    local_tokens = local_rows * micro_count
    group_tokens = quarters * local_tokens
    all_tokens = ranks * group_tokens
    head_dim = qk_gain.shape[0] * ranks
    local_heads = qk_gain.shape[2]
    local_width = local_heads * head_dim
    seq_len = local_rows * quarters
    scale = head_dim ** (-0.5)
    own_shape = (micro_count, local_rows, features)

    def by_micro(array):
        return jnp.swapaxes(array, 0, 1).reshape(local_tokens, features)

    def to_sequences(array):
        array = array.reshape(quarters, micro_count, local_rows, -1)
        return jnp.swapaxes(array, 0, 1).reshape(micro_count, seq_len, -1)

    def from_sequences(array):
        array = array.reshape(micro_count, quarters, local_rows, -1)
        return jnp.swapaxes(array, 0, 1).reshape(group_tokens, -1)

    small_parts = [router, attn_gain, mlp_gain, qk_gain, expert_ids.astype(BF16)]
    sizes = [part.size for part in small_parts]
    small = jnp.concatenate([part.reshape(-1) for part in small_parts])
    small_width = -(-small.size // (depth * 128)) * 128
    small = jnp.pad(small, (0, depth * small_width - small.size)).reshape(depth, small_width)
    own_tokens = by_micro(tokens)
    sources = [w_qkv[:, 0], w_qkv[:, 1], w_qkv[:, 2], small, w_out, own_tokens]
    pieces = tuple((n, 0, sources[n].shape[1], True, ("inner",)) for n in range(5))
    pieces += ((5, 0, features, False, ("side", "core")),)
    full_q, full_k, full_v, small_all, full_out, raw_rows = gather_blocks(
        sources, [ranks] * 5 + [quarters], pieces, ranks, 1
    )
    small_all = small_all.reshape(ranks, depth * small_width)
    ends = [sum(sizes[: n + 1]) for n in range(len(sizes))]
    full_router = small_all[:, : ends[0]].reshape(features, experts)
    gain_one = small_all[:, ends[0] : ends[1]].reshape(features).astype(F32)
    gain_two = small_all[:, ends[1] : ends[2]].reshape(features).astype(F32)
    full_qk = small_all[:, ends[2] : ends[3]].reshape(head_dim, 2, local_heads).astype(F32)
    all_ids = small_all[:, ends[3] : ends[4]].astype(jnp.int32)
    qk_rows = jnp.transpose(full_qk, (1, 2, 0)).reshape(2, local_width)

    blocks = jnp.concatenate(
        [
            expert_in.reshape(ranks, owned, depth, 2 * width),
            expert_out.reshape(ranks, owned, depth, width),
        ],
        axis=3,
    )
    blocks, raw_rows = lax.optimization_barrier((blocks, raw_rows))
    held = send_blocks(blocks, ranks)

    raw_rows = raw_rows.astype(F32)
    rows_one = (raw_rows * norm_factor(raw_rows) * gain_one).astype(BF16)
    query_raw = to_sequences(dot("td,df->tf", rows_one, full_q))
    key_raw = to_sequences(dot("td,df->tf", rows_one, full_k))
    value_rows = to_sequences(dot("td,df->tf", rows_one, full_v).astype(BF16))
    square_q, square_k = lax.psum(
        (jnp.sum(query_raw * query_raw, axis=-1), jnp.sum(key_raw * key_raw, axis=-1)), "tensor"
    )
    factor_q = lax.rsqrt(square_q[..., None] / features + EPSILON)
    factor_k = lax.rsqrt(square_k[..., None] / features + EPSILON)
    heads_shape = (micro_count, seq_len, local_heads, head_dim)
    query_heads = (query_raw * factor_q * qk_rows[0]).astype(BF16).reshape(heads_shape)
    key_heads = (key_raw * factor_k * qk_rows[1]).astype(BF16).reshape(heads_shape)
    value_heads = value_rows.reshape(heads_shape)
    seq_major = segments.T
    positions = jnp.arange(seq_len)
    distance = positions[:, None] - positions[None, :]
    same_doc = seq_major[:, :, None] == seq_major[:, None, :]
    allowed = (same_doc & (distance >= 0) & (distance < WINDOW))[:, None]
    scores = jnp.where(allowed, dot("mqhc,mkhc->mhqk", query_heads, key_heads) * scale, MASKED)
    weights_full = softmax_rows(scores)
    weights_low = weights_full.astype(BF16)
    head_out = dot("mhqk,mkhc->mqhc", weights_low, value_heads).astype(BF16)
    head_out = from_sequences(head_out.reshape(micro_count, seq_len, local_width))

    def scatter_quarters(array):
        across = ((0, 0, features, False, ("side", "core")),)
        return scatter_blocks(array, across, quarters, ranks, 2).astype(F32).reshape(own_shape)

    attended = scatter_quarters(dot("tf,df->td", head_out, full_out).astype(BF16))
    attended, held = tie(attended, held, 0, ranks // 4)
    inputs = own_tokens.astype(F32).reshape(own_shape)
    residual = inputs + attended
    factor_two = norm_factor(residual)
    normed_two = (residual * factor_two * gain_two).astype(BF16).reshape(local_tokens, features)

    rows_all = gather_everywhere(normed_two, ranks, 3)
    pull_own = by_micro(cotangent)
    pull_own, rows_all = lax.optimization_barrier((pull_own, rows_all))
    pull_all = gather_everywhere(pull_own, ranks, 3)
    router_probs = softmax_rows(dot("td,de->te", rows_all, full_router))

    first = rank * owned
    routes = all_ids.reshape(ranks, quarters, local_rows, micro_count, top_count)
    routes = jnp.swapaxes(routes, 2, 3).reshape(ranks, 1, group_tokens, top_count)
    names = first + jnp.arange(owned, dtype=jnp.int32)
    member = jnp.any(routes == names[:, None, None], axis=-1)
    order = jnp.arange(group_tokens)
    earlier = (order[:, None] < order[None, :]).astype(BF16)
    position = dot("ges,st->get", member.astype(BF16), earlier)
    position = jnp.where(member, position, -1.0).astype(jnp.int32)
    gate_own = lax.dynamic_slice_in_dim(router_probs, first, owned, 1)
    gate_own = jnp.swapaxes(gate_own.reshape(ranks, group_tokens, owned), 1, 2)
    lanes = jnp.arange(128, dtype=jnp.int32)
    column = (names[:, None] == lanes).astype(F32)
    mixture_all, returned_all, chosen, pulled, d_gate_up, hidden = expert_math(
        rows_all, pull_all, position, gate_own, column, join_blocks(blocks, held)
    )

    grad_in = dot("egsrk,egsf->rekf", chosen.reshape(owned, ranks, CAP, ranks, depth), d_gate_up)
    grad_out = dot("egsrk,egsf->rekf", pulled.reshape(owned, ranks, CAP, ranks, depth), hidden)
    grad_blocks = jnp.concatenate([grad_in.astype(BF16), grad_out.astype(BF16)], axis=3)
    returned_all, grad_blocks = lax.optimization_barrier((returned_all, grad_blocks))
    sent = send_blocks(grad_blocks, ranks)
    returned_own = scatter_everywhere(returned_all, ranks, 4)

    returned_f = returned_own[:, :features].astype(F32)
    d_probs = returned_own[:, features : features + experts].astype(F32)
    first_token = (rank * quarters + quarter) * local_tokens
    probs_own = lax.dynamic_slice_in_dim(router_probs, first_token, local_tokens, 0)
    d_logits = (
        probs_own * (d_probs - jnp.sum(d_probs * probs_own, axis=-1, keepdims=True))
    ).astype(BF16)
    d_normed_two = (returned_f + dot("te,de->td", d_logits, full_router)).reshape(own_shape)
    grad_router = dot("td,te->de", normed_two, d_logits)
    pull_f = pull_own.astype(F32).reshape(own_shape)
    d_residual = pull_f + norm_back(residual, factor_two, gain_two, d_normed_two)
    grad_gain_two = jnp.sum(residual * factor_two * d_normed_two, axis=(0, 1))
    d_attended = d_residual.astype(BF16).reshape(local_tokens, features)

    (rows_back,) = gather_blocks(
        [d_attended], [quarters], ((0, 0, features, False, ("side", "core")),), ranks, 8
    )
    rows_back, sent = tie(rows_back, sent, 0, ranks // 4)
    d_heads = to_sequences(dot("td,df->tf", rows_back, full_out).astype(BF16)).reshape(heads_shape)
    grad_w_out = dot("td,tf->df", rows_back, head_out)
    d_weights = dot("mqhc,mkhc->mhqk", d_heads, value_heads)
    d_scores = (
        weights_full * (d_weights - jnp.sum(d_weights * weights_full, axis=-1, keepdims=True))
    ).astype(BF16)
    flat_shape = (micro_count, seq_len, local_width)
    d_queries = (dot("mhqk,mkhc->mqhc", d_scores, key_heads) * scale).reshape(flat_shape)
    d_keys = (dot("mhqk,mqhc->mkhc", d_scores, query_heads) * scale).reshape(flat_shape)
    d_values = dot("mhqk,mqhc->mkhc", weights_low, d_heads).reshape(flat_shape).astype(BF16)
    inner_q, inner_k = lax.psum(
        (
            jnp.sum(query_raw * qk_rows[0] * d_queries, axis=-1),
            jnp.sum(key_raw * qk_rows[1] * d_keys, axis=-1),
        ),
        "tensor",
    )
    d_query_raw = (
        factor_q * qk_rows[0] * d_queries - query_raw * factor_q**3 * inner_q[..., None] / features
    )
    d_key_raw = (
        factor_k * qk_rows[1] * d_keys - key_raw * factor_k**3 * inner_k[..., None] / features
    )
    grad_qk_rows = jnp.stack(
        [
            jnp.sum(query_raw * factor_q * d_queries, axis=(0, 1)),
            jnp.sum(key_raw * factor_k * d_keys, axis=(0, 1)),
        ]
    )
    grad_qk = jnp.transpose(grad_qk_rows.reshape(2, local_heads, head_dim), (2, 0, 1))
    d_q = from_sequences(d_query_raw.astype(BF16))
    d_k = from_sequences(d_key_raw.astype(BF16))
    d_v = from_sequences(d_values)
    d_normed_one = scatter_quarters(
        (
            dot("tf,df->td", d_q, full_q)
            + dot("tf,df->td", d_k, full_k)
            + dot("tf,df->td", d_v, full_v)
        ).astype(BF16)
    )
    factor_one = norm_factor(inputs)
    grad_tokens = (d_residual + norm_back(inputs, factor_one, gain_one, d_normed_one)).astype(BF16)
    grad_gain_one = jnp.sum(inputs * factor_one * d_normed_one, axis=(0, 1))

    small_grads = [
        part.reshape(ranks, -1) for part in (grad_router, grad_gain_one, grad_gain_two, grad_qk)
    ]
    small_grads = jnp.concatenate(small_grads, axis=1)
    shared = depth * (experts + 2)
    slim = -(-small_grads.shape[1] // (depth * 128)) * 128
    small_grads = jnp.pad(small_grads, ((0, 0), (0, depth * slim - small_grads.shape[1])))
    grads = [dot("td,tf->df", rows_one, part).astype(BF16) for part in (d_q, d_k, d_v)]
    grads += [grad_w_out.astype(BF16), small_grads.reshape(features, slim).astype(BF16)]
    grads = jnp.concatenate(grads, axis=1)
    cut = 2 * local_width
    pieces = (
        (0, 0, cut, True, ("inner",)),
        (0, cut, grads.shape[1] - cut, True, ("inner",)),
    )
    grads_own = scatter_blocks(grads, pieces, ranks, ranks, 9).astype(F32)
    grad_qkv_own = grads_own[:, : 3 * local_width].reshape(depth, 3, local_width)
    grad_out_own = grads_own[:, 3 * local_width : 4 * local_width]
    small_own = grads_own[:, 4 * local_width :].reshape(-1)
    shared_own = lax.psum(small_own[:shared], "tensor")
    grad_qk_own = small_own[shared : shared + qk_gain.size].reshape(qk_gain.shape)

    mixture_all, _ = lax.optimization_barrier((mixture_all, rows_back))
    mixture_own = scatter_everywhere(mixture_all, ranks, 10)
    layer_out = (residual + mixture_own.astype(F32).reshape(own_shape)).astype(BF16)
    expert_grads = join_blocks(grad_blocks, sent).astype(F32).reshape(experts, depth, 3 * width)
    grad_expert_in = expert_grads[:, :, : 2 * width].reshape(experts, depth, 2, width)
    grad_expert_out = expert_grads[:, :, 2 * width :]
    return (
        jnp.swapaxes(layer_out, 0, 1),
        jnp.swapaxes(grad_tokens, 0, 1),
        shared_own[depth * experts : depth * experts + depth],
        grad_qkv_own,
        grad_qk_own,
        grad_out_own,
        shared_own[depth * (experts + 1) :],
        shared_own[: depth * experts].reshape(depth, experts),
        grad_expert_in,
        grad_expert_out,
    )


def solution(mesh):
    placed = (
        P(("dp", "tensor"), None, None),
        P(("dp", "tensor"), None, None),
        P("dp", None),
        P("dp", None, None),
        P("dp"),
        P("dp", None, "tensor"),
        P("dp", None, "tensor"),
        P("dp", "tensor"),
        P("dp"),
        P("dp", None),
        P(None, "dp", None, "tensor"),
        P(None, "dp", "tensor"),
    )
    return jax.shard_map(
        functools.partial(body, mesh.shape["dp"], mesh.shape["tensor"]),
        mesh=mesh,
        in_specs=placed,
        out_specs=(
            P(("dp", "tensor"), None, None),
            P(("dp", "tensor"), None, None),
            P("dp"),
            P("dp", None, "tensor"),
            P("dp", None, "tensor"),
            P("dp", "tensor"),
            P("dp"),
            P("dp", None),
            P(None, "dp", None, "tensor"),
            P(None, "dp", "tensor"),
        ),
        check_vma=False,
    )
```

```python
import functools
import itertools

import jax
import jax.numpy as jnp
from jax import lax
from jax.experimental import pallas as pl
from jax.experimental.pallas import tpu as pltpu
from jax.sharding import PartitionSpec as P

WINDOW = 128
CAP = 176
EPSILON = 1e-05
MASKED = -1e30

MESH = pl.DeviceIdType.MESH
F32 = jnp.float32
BF16 = jnp.bfloat16


def norm_factor(values):
    return lax.rsqrt(jnp.mean(values * values, axis=-1, keepdims=True) + EPSILON)


def norm_back(values, factor, gain_row, upstream):
    features = values.shape[-1]
    inner = jnp.sum(values * gain_row * upstream, axis=-1, keepdims=True)
    return factor * gain_row * upstream - values * factor**3 * inner / features


def softmax_rows(logits):
    highest = jnp.max(logits, axis=-1, keepdims=True)
    raised = jnp.exp(logits - highest)
    return raised / jnp.sum(raised, axis=-1, keepdims=True)


def dot(spec, left, right):
    return jnp.einsum(spec, left, right, preferred_element_type=F32)


class Places:
    def __init__(self, ranks, pieces):
        rank = lax.axis_index("dp")
        quarter = lax.axis_index("tensor")
        count = ranks // 2
        self.count = count
        self.outer = rank // 2
        self.rank_base = self.outer * 2
        pairs = {
            "inner": lax.rem(rank, 2),
            "side": quarter // 2,
            "core": lax.rem(quarter, 2),
        }
        self.exists = {0: None}
        if any(piece[3] for piece in pieces):
            for steps in range(1, count):
                self.exists[steps] = self.outer + steps < count
                self.exists[-steps] = self.outer - steps >= 0
        self.inner = {}
        self.quarter = {}
        self.whole = {}
        for flips in itertools.product((0, 1), repeat=3):
            names = frozenset(name for name, bit in zip(("inner", "side", "core"), flips) if bit)
            place = {name: 1 - at if name in names else at for name, at in pairs.items()}
            self.inner[names] = self.rank_base + place["inner"]
            self.quarter[names] = place["side"] * 2 + place["core"]
            self.whole[names] = self.inner[names] * 4 + self.quarter[names]

    def device(self, steps, flips):
        names = frozenset(flips)
        return self.inner[names] + 2 * steps if steps else self.inner[names], self.quarter[names]

    def rows(self, piece, steps, flips, rows):
        names = frozenset(flips)
        if not piece[3]:
            index = self.quarter[names]
        elif "side" not in piece[4]:
            index = self.inner[names] + 2 * steps
        else:
            index = self.whole[names] + 8 * steps
        return pl.ds(pl.multiple_of(index * rows, rows), rows)


def run_if(conditions, action):
    conditions = [condition for condition in conditions if condition is not None]
    if not conditions:
        action()
        return
    pl.when(functools.reduce(jnp.logical_and, conditions))(action)


def greet(places, pieces):
    barrier = pltpu.get_barrier_semaphore()
    pairs = sorted({name for piece in pieces for name in piece[4]})
    targets = [(None, 0, (name,)) for name in pairs]
    if any(piece[3] for piece in pieces):
        targets += [(places.exists[steps], steps, ()) for steps in (-1, 1)]

    def signal(steps, flips):
        target = places.device(steps, flips)
        pl.semaphore_signal(barrier, inc=1, device_id=target, device_id_type=MESH)

    expected = len(pairs)
    for condition, steps, flips in targets:
        run_if([condition], functools.partial(signal, steps, flips))
        if condition is not None:
            expected = expected + condition.astype(jnp.int32)
    pl.semaphore_wait(barrier, expected)


def chain_steps(ranks, outer):
    count = ranks // 2
    return [0] + [sign * k for k in range(1, count) for sign in (-1, 1)] if outer else [0]


def all_bits(dims):
    return list(itertools.product((0, 1), repeat=len(dims)))


def semaphores(ranks, pieces):
    starts = [0]
    for _, _, _, outer, dims in pieces:
        starts.append(starts[-1] + len(chain_steps(ranks, outer)) * 2 ** len(dims))
    return starts


def chain_number(ranks, piece, steps):
    return steps + ranks // 2 - 1 if piece[3] else 0


def level_of(bits):
    return max((n + 1 for n, bit in enumerate(bits) if bit), default=0)


def gather_kernel(ranks, arrays, pieces, *refs):
    in_refs, out_refs = refs[:arrays], refs[arrays : 2 * arrays]
    send_sem, recv_sem, local_sem = refs[2 * arrays :]
    count = ranks // 2
    starts = semaphores(ranks, pieces)
    places = Places(ranks, pieces)
    greet(places, pieces)
    started = []

    def flips_of(p, bits):
        return tuple(name for name, bit in zip(pieces[p][4], bits) if bit)

    def copy(p, steps, bits, as_seen, target_steps, target_flips):
        array, start, width, _, dims = pieces[p]
        rows = in_refs[array].shape[0]
        columns = pl.ds(start, width)
        place = out_refs[array].at[
            places.rows(pieces[p], steps, flips_of(p, bits), rows), columns
        ]
        own = steps == 0 and not any(bits)
        seen_steps, seen_bits = as_seen
        sem = chain_number(ranks, pieces[p], seen_steps) * 2 ** len(dims)
        sem += starts[p] + all_bits(dims).index(seen_bits)
        return pltpu.make_async_remote_copy(
            src_ref=in_refs[array].at[:, columns] if own else place,
            dst_ref=place,
            send_sem=send_sem.at[sem],
            recv_sem=recv_sem.at[sem],
            device_id=places.device(target_steps, target_flips),
            device_id_type=MESH,
        )

    def send(conditions, *description):
        run_if(conditions, lambda: copy(*description).start())
        started.append((conditions, description))

    def forward(p, steps, bits):
        outer, dims = pieces[p][3:]
        here = places.exists[steps]
        level = level_of(bits)
        if outer and level == 0:
            for direction in (-1, 1):
                if steps * direction <= 0 and abs(steps) < count - 1:
                    there = places.exists[direction]
                    seen = (steps - direction, bits)
                    send([here, there], p, steps, bits, seen, direction, ())
        for n in range(level, len(dims)):
            seen = (steps, bits[:n] + (1,) + bits[n + 1 :])
            send([here], p, steps, bits, seen, 0, (dims[n],))

    def receive(p, steps, bits):
        here = places.exists[steps]
        run_if([here], lambda: copy(p, steps, bits, (steps, bits), 0, (pieces[p][4][0],)).wait_recv())
        forward(p, steps, bits)

    kept = []
    for array in range(arrays):
        piece = next(piece for piece in pieces if piece[0] == array)
        rows = in_refs[array].shape[0]
        keep = pltpu.make_async_copy(
            in_refs[array],
            out_refs[array].at[places.rows(piece, 0, (), rows)],
            local_sem.at[array],
        )
        keep.start()
        kept.append(keep)
    events = []
    for p, (_, _, _, outer, dims) in enumerate(pieces):
        for n, steps in enumerate(chain_steps(ranks, outer)):
            for bits in all_bits(dims):
                level = level_of(bits)
                turn = len(dims) + 1 if level == len(dims) else max(level - 1, 0)
                events.append((turn, abs(steps), n, level, p, steps, bits))
    for event in sorted(event for event in events if event[1] == 0 and event[3] == 0):
        forward(*event[4:])
    for event in sorted(event for event in events if event[1] or event[3]):
        receive(*event[4:])
    for conditions, description in started:
        run_if(conditions, lambda: copy(*description).wait_send())
    for keep in kept:
        keep.wait()


def gather_blocks(blocks, results, pieces, ranks, collective_id):
    arrays = len(blocks)
    transfers = semaphores(ranks, pieces)[-1]
    return pl.pallas_call(
        functools.partial(gather_kernel, ranks, arrays, pieces),
        out_shape=tuple(
            jax.ShapeDtypeStruct((number * block.shape[0], block.shape[1]), block.dtype)
            for block, number in zip(blocks, results)
        ),
        in_specs=[pl.BlockSpec(memory_space=pl.ANY)] * arrays,
        out_specs=(pl.BlockSpec(memory_space=pl.ANY),) * arrays,
        scratch_shapes=[
            pltpu.SemaphoreType.DMA((transfers,)),
            pltpu.SemaphoreType.DMA((transfers,)),
            pltpu.SemaphoreType.DMA((arrays,)),
        ],
        compiler_params=pltpu.CompilerParams(collective_id=collective_id, has_side_effects=True),
        cost_estimate=pl.CostEstimate(
            flops=0,
            bytes_accessed=sum(2 * n * block.size for block, n in zip(blocks, results)),
            transcendentals=0,
        ),
    )(*blocks)


def gather_everywhere(block, ranks, collective_id):
    half = block.shape[1] // 2
    pieces = (
        (0, 0, half, True, ("inner", "side", "core")),
        (0, half, half, True, ("side", "inner", "core")),
    )
    return gather_blocks([block], [4 * ranks], pieces, ranks, collective_id)[0]


def scatter_kernel(ranks, arrays, pieces, *refs):
    in_refs, out_refs, scratch = refs[:arrays], refs[arrays : 2 * arrays], refs[2 * arrays :]
    buffers, (send_sem, recv_sem, load_sem) = scratch[:-3], scratch[-3:]
    count = ranks // 2
    starts = semaphores(ranks, pieces)
    places = Places(ranks, pieces)
    greet(places, pieces)
    started = []
    held = []
    for _, _, _, _, dims in pieces:
        depth = len(dims)
        own, *paired = buffers[: depth + 1]
        up, down = buffers[depth + 1 : depth + 3]
        held.append((own, paired, up, down))
        buffers = buffers[depth + 3 :]

    def region(p, steps, bits):
        array, start, width, _, dims = pieces[p]
        flips = tuple(name for name, bit in zip(dims, bits) if bit)
        rows = out_refs[array].shape[0]
        return in_refs[array].at[places.rows(pieces[p], steps, flips, rows), pl.ds(start, width)]

    def slot(p, steps, bits):
        place = places.outer + steps if pieces[p][3] else 0
        number = 0
        for bit in bits:
            number = 2 * number + bit
        return place * 2 ** len(bits) + number

    def sem_of(p, steps, bits, kind):
        code = 0
        for bit in bits:
            code = 2 * code + bit
        number = chain_number(ranks, pieces[p], steps) * 2 ** len(bits) + code
        return (starts[p] + number) * 2 + kind

    def own_at(p, steps, bits):
        return held[p][0].at[slot(p, steps, bits)]

    def load(p, steps, bits):
        return pltpu.make_async_copy(
            region(p, steps, bits + (0,)),
            own_at(p, steps, bits),
            load_sem.at[sem_of(p, steps, bits + (0,), 0) // 2],
        )

    def pair_copy(p, steps, bits, n):
        dims = pieces[p][4]
        whole = bits[:n] + (1,) + (0,) * (len(dims) - n - 1)
        last = n == len(dims) - 1
        return pltpu.make_async_remote_copy(
            src_ref=region(p, steps, whole) if last else own_at(p, steps, whole[:-1]),
            dst_ref=held[p][1][n].at[slot(p, steps, bits[:n])],
            send_sem=send_sem.at[sem_of(p, steps, whole, 0)],
            recv_sem=recv_sem.at[sem_of(p, steps, whole, 0)],
            device_id=places.device(0, (dims[n],)),
            device_id_type=MESH,
        )

    def chain_copy(p, steps, direction):
        zeros = (0,) * (len(pieces[p][4]) - 1)
        sem = sem_of(p, steps - direction, zeros + (0,), 1)
        return pltpu.make_async_remote_copy(
            src_ref=own_at(p, steps, zeros),
            dst_ref=held[p][2 if direction > 0 else 3].at[slot(p, steps, ())],
            send_sem=send_sem.at[sem + (0 if direction > 0 else 2)],
            recv_sem=recv_sem.at[sem + (0 if direction > 0 else 2)],
            device_id=places.device(direction, ()),
            device_id_type=MESH,
        )

    def chain_arrival(p, steps, direction):
        zeros = (0,) * (len(pieces[p][4]) - 1)
        sem = sem_of(p, steps, zeros + (0,), 1) + (0 if direction > 0 else 2)
        place = held[p][2 if direction > 0 else 3].at[slot(p, steps, ())]
        return pltpu.make_async_remote_copy(
            src_ref=place,
            dst_ref=place,
            send_sem=send_sem.at[sem],
            recv_sem=recv_sem.at[sem],
            device_id=places.device(-direction, ()),
            device_id_type=MESH,
        )

    def add(target, sources):
        rows = target.shape[0]
        tile = min(rows, 32)

        def step(n, carry):
            part = pl.ds(pl.multiple_of(n * tile, tile), tile)
            total = sources[0][part].astype(F32)
            for source in sources[1:]:
                total = total + source[part].astype(F32)
            target[part] = total.astype(target.dtype)
            return carry

        lax.fori_loop(0, rows // tile, step, 0)

    order = []
    for array in range(arrays):
        entries = []
        for p, (of, _, _, outer, dims) in enumerate(pieces):
            if of == array:
                for n, steps in enumerate(chain_steps(ranks, outer)):
                    for bits in all_bits(dims[:-1]):
                        entries.append((-level_of(bits), -abs(steps), n, p, steps, bits))
        for n, entry in enumerate(sorted(entries)):
            order.append(((n + 1) / len(entries), array, n, entry[3:]))
    order = [entry[3] for entry in sorted(order)]
    for p, steps, bits in order:
        here = places.exists[steps]
        last = len(pieces[p][4]) - 1

        def begin(p=p, steps=steps, bits=bits, last=last):
            pair_copy(p, steps, bits, last).start()
            load(p, steps, bits).start()

        run_if([here], begin)
        started.append(([here], functools.partial(pair_copy, p, steps, bits, last)))
    for p, steps, bits in order:
        here = places.exists[steps]
        dims = pieces[p][4]
        level = level_of(bits)
        own, paired, up, down = held[p]

        def gather_terms(p=p, steps=steps, bits=bits, level=level, dims=dims, paired=paired):
            load(p, steps, bits).wait()
            sources = [own_at(p, steps, bits)]
            for n in range(len(dims) - 1, level - 1, -1):
                pair_copy(p, steps, bits, n).wait_recv()
                sources.append(paired[n].at[slot(p, steps, bits[:n])])
            add(own_at(p, steps, bits), sources)

        run_if([here], gather_terms)
        if level:

            def send_pair(p=p, steps=steps, bits=bits, level=level):
                return pair_copy(p, steps, bits, level - 1)

            run_if([here], lambda: send_pair().start())
            started.append(([here], send_pair))
            continue
        if pieces[p][3]:
            for direction in (1, -1):
                if steps * direction < 0 or abs(steps) == count - 1:
                    continue
                behind = places.exists[-direction]

                def take(p=p, steps=steps, bits=bits, direction=direction):
                    chain_arrival(p, steps, direction).wait_recv()
                    arrived = held[p][2 if direction > 0 else 3].at[slot(p, steps, ())]
                    add(own_at(p, steps, bits), [own_at(p, steps, bits), arrived])

                run_if([here, behind], take)
        if steps:
            direction = 1 if steps > 0 else -1

            def send_chain(p=p, steps=steps, direction=direction):
                return chain_copy(p, steps, direction)

            run_if([here], lambda: send_chain().start())
            started.append(([here], send_chain))
        else:
            array, start, width = pieces[p][:3]
            columns = pl.ds(start - min(piece[1] for piece in pieces if piece[0] == array), width)
            add(out_refs[array].at[:, columns], [own_at(p, 0, bits)])
    for conditions, build in started:
        run_if(conditions, lambda: build().wait_send())


def scatter_blocks(sources, pieces, blocks, ranks, collective_id):
    arrays = len(sources)
    count = ranks // 2
    out_shape = []
    for n, (source, number) in enumerate(zip(sources, blocks)):
        columns = sum(piece[2] for piece in pieces if piece[0] == n)
        out_shape.append(jax.ShapeDtypeStruct((source.shape[0] // number, columns), source.dtype))
    scratch = []
    for array, _, width, outer, dims in pieces:
        chain = count if outer else 1
        sizes = [chain * 2 ** (len(dims) - 1)]
        sizes += [chain * 2**n for n in range(len(dims))]
        sizes += [chain, chain] if outer else [1, 1]
        rows = out_shape[array].shape[0]
        scratch += [pltpu.VMEM((size, rows, width), sources[array].dtype) for size in sizes]
    transfers = semaphores(ranks, pieces)[-1]
    return pl.pallas_call(
        functools.partial(scatter_kernel, ranks, arrays, pieces),
        out_shape=tuple(out_shape),
        in_specs=[pl.BlockSpec(memory_space=pl.ANY)] * arrays,
        out_specs=(pl.BlockSpec(memory_space=pltpu.VMEM),) * arrays,
        scratch_shapes=[
            *scratch,
            pltpu.SemaphoreType.DMA((2 * transfers,)),
            pltpu.SemaphoreType.DMA((2 * transfers,)),
            pltpu.SemaphoreType.DMA((transfers,)),
        ],
        compiler_params=pltpu.CompilerParams(
            collective_id=collective_id,
            has_side_effects=True,
            vmem_limit_bytes=58 * 1024 * 1024,
        ),
        cost_estimate=pl.CostEstimate(
            flops=sum(source.size for source in sources),
            bytes_accessed=sum(2 * source.size for source in sources),
            transcendentals=0,
        ),
    )(*sources)


def scatter_everywhere(array, ranks, collective_id, beside=None):
    tiles = array.shape[1] // 128
    calls = max(1, ranks // 8)
    results = []
    other = None
    for call in range(calls):
        first, last = tiles * call // calls, tiles * (call + 1) // calls
        middle = (first + last + 1) // 2
        dims = ("inner", "side", "core")
        second = dims if beside is not None else ("side", "inner", "core")
        pieces = (
            (0, first * 128, (middle - first) * 128, True, dims),
            (0, middle * 128, (last - middle) * 128, True, second),
        )
        if beside is None or call:
            (result,) = scatter_blocks([array], pieces, [4 * ranks], ranks, collective_id + call)
        else:
            cut = beside.shape[1] // 256 * 128
            pieces += (
                (1, 0, cut, True, ("inner",)),
                (1, cut, beside.shape[1] - cut, True, ("inner",)),
            )
            result, other = scatter_blocks(
                [array, beside], pieces, [4 * ranks, ranks], ranks, collective_id
            )
        results.append(result)
    result = results[0] if calls == 1 else jnp.concatenate(results, axis=1)
    return (result, other) if beside is not None else result


def send_blocks(block_for, ranks):
    own = lax.axis_index("dp")
    received = [(own, block_for(own))]
    for shift in range(1, ranks):
        target = lax.rem(own + shift, ranks)
        origin = lax.rem(own + ranks - shift, ranks)
        pairs = [(j, (j + shift) % ranks) for j in range(ranks)]
        received.append((origin, lax.ppermute(block_for(target), "dp", pairs)))
    return received


def settle_kernel(width, origin_ref, *refs):
    block_refs, (in_ref, out_ref, held_ref, load_sem) = refs[:-4], refs[-4:]
    del origin_ref
    at = pl.program_id(0)
    tiles = width // 128

    def load(n):
        return pltpu.make_async_copy(block_refs[n].at[0], held_ref.at[n], load_sem.at[n])

    @pl.when(at == 0)
    def _():
        for n in range(len(block_refs)):
            load(n).start()

    for n in range(len(block_refs)):
        pl.when(at == n)(load(n).wait)
    portion, depth, _ = held_ref.shape[1:]
    for e in range(portion):
        for j in range(2):
            for tile in range(tiles):
                rows = pl.ds(tile * 2 + j, depth, stride=2 * tiles)
                start = j * width + tile * 128
                in_ref[e, rows, :] = held_ref[at, e, :, start : start + 128].astype(F32)
        out_ref[e] = held_ref[at, e, :, 2 * width :].astype(F32)


def settle(sent, owned, width):
    portions = len(sent)
    ranks = len(sent[0])
    blocks = [block for received in sent for _, block in received]
    origins = jnp.stack([origin for origin, _ in sent[0]]).astype(jnp.int32)
    portion, depth, _ = blocks[0].shape[1:]
    in_rows = depth * 2 * width // 128

    def place(step, origins):
        return origins[lax.rem(step, ranks)] * portions + step // ranks, 0, 0

    return pl.pallas_call(
        functools.partial(settle_kernel, width),
        grid_spec=pltpu.PrefetchScalarGridSpec(
            num_scalar_prefetch=1,
            grid=(len(blocks),),
            in_specs=[pl.BlockSpec(memory_space=pl.ANY)] * len(blocks),
            out_specs=(
                pl.BlockSpec((portion, in_rows, 128), place),
                pl.BlockSpec((portion, depth, width), place),
            ),
            scratch_shapes=[
                pltpu.VMEM((len(blocks),) + blocks[0].shape[1:], BF16),
                pltpu.SemaphoreType.DMA((len(blocks),)),
            ],
        ),
        out_shape=(
            jax.ShapeDtypeStruct((owned * ranks, in_rows, 128), F32),
            jax.ShapeDtypeStruct((owned * ranks, depth, width), F32),
        ),
        compiler_params=pltpu.CompilerParams(vmem_limit_bytes=40 * 1024 * 1024),
    )(origins, *blocks)


def tie(value, received, part, parts):
    number = len(received) - 1
    first, last = 1 + number * part // parts, 1 + number * (part + 1) // parts
    blocks = [block for _, block in received[first:last]]
    value, blocks = lax.optimization_barrier((value, blocks))
    renewed = [(origin, block) for (origin, _), block in zip(received[first:last], blocks)]
    return value, received[:first] + renewed + received[last:]


def expert_kernel(ranks, owned, width, added, origin_ref, rows_ref, pull_ref, *refs):
    position_ref, gate_ref, column_ref, *refs = refs
    block_refs, refs = refs[:ranks], refs[ranks:]
    before, refs = refs[: 2 * added], refs[2 * added :]
    mixture_ref, returned_ref, chosen_ref, pulled_ref, d_gate_up_ref, hidden_ref, *refs = refs
    place_ref, mixed_ref, back_ref, weight_ref, load_sem = refs

    @pl.when(pl.program_id(0) == 0)
    def _():
        loads = [
            pltpu.make_async_copy(
                block_refs[n].at[0], weight_ref.at[origin_ref[n]], load_sem.at[n]
            )
            for n in range(ranks)
        ]
        for load in loads:
            load.start()
        for load in loads:
            load.wait()

    group_tokens, features = rows_ref.shape
    chunk = min(features, 512)
    slot = lax.broadcasted_iota(jnp.int32, (CAP, group_tokens), 0)
    last = (((1,), (1,)), ((), ()))
    first = (((0,), (0,)), ((), ()))
    for e in range(owned):
        place_ref[e * CAP : (e + 1) * CAP] = (position_ref[0, e : e + 1] == slot).astype(BF16)
    for start in range(0, features, chunk):
        columns = slice(start, start + chunk)
        chosen = jnp.dot(place_ref[...], rows_ref[:, columns], preferred_element_type=F32)
        chosen_ref[:, 0, :, columns] = chosen.astype(BF16).reshape(owned, CAP, chunk)
        pulled = jnp.dot(place_ref[...], pull_ref[:, columns], preferred_element_type=F32)
        pulled_ref[:, 0, :, columns] = pulled.astype(BF16).reshape(owned, CAP, chunk)
    spread = jnp.zeros((group_tokens, 128), F32)
    for e in range(owned):
        weight_in = weight_ref[:, e, :, : 2 * width].reshape(features, 2 * width)
        weight_out = weight_ref[:, e, :, 2 * width :].reshape(features, width)
        here = position_ref[0, e : e + 1] == slot
        gate = jnp.sum(jnp.where(here, gate_ref[0, e : e + 1], 0.0), axis=1, keepdims=True)
        gate_up = jnp.dot(chosen_ref[e, 0], weight_in, preferred_element_type=F32)
        d_plain = jnp.dot(pulled_ref[e, 0], weight_out, preferred_element_type=F32)
        gate_part = gate_up[:, :width]
        up_part = gate_up[:, width:]
        sigmoid_gate = jax.nn.sigmoid(gate_part)
        activated = gate_part * sigmoid_gate
        hidden = activated * up_part
        slot_dots = jnp.sum(hidden * d_plain, axis=1, keepdims=True)
        spread = spread + lax.dot_general(
            place_ref[e * CAP : (e + 1) * CAP],
            (slot_dots * column_ref[e : e + 1]).astype(BF16),
            first,
            preferred_element_type=F32,
        )
        d_hidden = d_plain * gate
        d_gate_part = d_hidden * up_part * sigmoid_gate * (1.0 + gate_part * (1.0 - sigmoid_gate))
        d_up_part = d_hidden * activated
        hidden_ref[e, 0] = (hidden * gate).astype(BF16)
        d_gate_up_ref[e, 0, :, :width] = d_gate_part.astype(BF16)
        d_gate_up_ref[e, 0, :, width:] = d_up_part.astype(BF16)
        mixed_ref[e * CAP : (e + 1) * CAP] = lax.dot_general(
            hidden_ref[e, 0], weight_out, last, preferred_element_type=F32
        ).astype(BF16)
        back_ref[e * CAP : (e + 1) * CAP] = lax.dot_general(
            d_gate_up_ref[e, 0], weight_in, last, preferred_element_type=F32
        ).astype(BF16)
    def finish(target_ref, number, columns, total):
        if added:
            total = total + before[number][:, columns].astype(F32)
        target_ref[:, columns] = total.astype(BF16)

    finish(returned_ref, 1, slice(features, features + 128), spread)
    for start in range(0, features, chunk):
        columns = slice(start, start + chunk)
        for number, (target_ref, source_ref) in enumerate(
            ((mixture_ref, mixed_ref), (returned_ref, back_ref))
        ):
            total = lax.dot_general(
                place_ref[...], source_ref[:, columns], first, preferred_element_type=F32
            )
            finish(target_ref, number, columns, total)


def expert_math(rows, pull, position, gate, column, received, before, last):
    groups, owned, group_tokens = position.shape
    tokens, features = rows.shape
    ranks = len(received)
    depth = features // ranks
    width = received[0][1].shape[3] // 3
    slots = owned * CAP
    origins = jnp.stack([origin for origin, _ in received]).astype(jnp.int32)
    by_rows = pl.BlockSpec((group_tokens, features), lambda g, _: (g, 0))
    by_group = pl.BlockSpec((1, owned, group_tokens), lambda g, _: (g, 0, 0))
    by_returned = pl.BlockSpec((group_tokens, features + 128), lambda g, _: (g, 0))

    def by_slots(columns):
        return pl.BlockSpec((owned, 1, CAP, columns), lambda g, _: (0, g, 0, 0))

    def slot_array(columns):
        return jax.ShapeDtypeStruct((owned, groups, CAP, columns), BF16)

    aliases = {}
    if before:
        aliases = {6 + ranks: 0, 7 + ranks: 1}
    elif last:
        aliases = {2: 0}
    flops = 2 * groups * slots * features * (4 * group_tokens + 6 * width)
    return pl.pallas_call(
        functools.partial(expert_kernel, ranks, owned, width, 1 if before else 0),
        grid_spec=pltpu.PrefetchScalarGridSpec(
            num_scalar_prefetch=1,
            grid=(groups,),
            in_specs=[
                by_rows,
                by_rows,
                by_group,
                by_group,
                pl.BlockSpec((owned, 128), lambda g, _: (0, 0)),
            ]
            + [pl.BlockSpec(memory_space=pl.ANY)] * ranks
            + ([by_rows, by_returned] if before else []),
            out_specs=(
                by_rows,
                by_returned,
                by_slots(features),
                by_slots(features),
                by_slots(2 * width),
                by_slots(width),
            ),
            scratch_shapes=[
                pltpu.VMEM((slots, group_tokens), BF16),
                pltpu.VMEM((slots, features), BF16),
                pltpu.VMEM((slots, features), BF16),
                pltpu.VMEM((ranks, owned, depth, 3 * width), BF16),
                pltpu.SemaphoreType.DMA((ranks,)),
            ],
        ),
        out_shape=(
            jax.ShapeDtypeStruct((tokens, features), BF16),
            jax.ShapeDtypeStruct((tokens, features + 128), BF16),
            slot_array(features),
            slot_array(features),
            slot_array(2 * width),
            slot_array(width),
        ),
        input_output_aliases=aliases,
        compiler_params=pltpu.CompilerParams(vmem_limit_bytes=60 * 1024 * 1024),
        cost_estimate=pl.CostEstimate(
            flops=flops,
            bytes_accessed=4 * tokens * features * 2 + slots * groups * features * 4,
            transcendentals=0,
        ),
    )(
        origins,
        rows,
        pull,
        position,
        gate,
        column,
        *[block for _, block in received],
        *before,
    )


def body(
    ranks,
    quarters,
    tokens,
    cotangent,
    segments,
    expert_ids,
    attn_gain,
    w_qkv,
    qk_gain,
    w_out,
    mlp_gain,
    router,
    expert_in,
    expert_out,
):
    rank = lax.axis_index("dp")
    quarter = lax.axis_index("tensor")
    local_rows, micro_count, features = tokens.shape
    experts, depth, _, width = expert_in.shape
    top_count = expert_ids.shape[2]
    owned = experts // ranks
    local_tokens = local_rows * micro_count
    group_tokens = quarters * local_tokens
    all_tokens = ranks * group_tokens
    head_dim = qk_gain.shape[0] * ranks
    local_heads = qk_gain.shape[2]
    local_width = local_heads * head_dim
    seq_len = local_rows * quarters
    scale = head_dim ** (-0.5)
    own_shape = (micro_count, local_rows, features)

    def by_micro(array):
        return jnp.swapaxes(array, 0, 1).reshape(local_tokens, features)

    def to_sequences(array):
        array = array.reshape(quarters, micro_count, local_rows, -1)
        return jnp.swapaxes(array, 0, 1).reshape(micro_count, seq_len, -1)

    def from_sequences(array):
        array = array.reshape(micro_count, quarters, local_rows, -1)
        return jnp.swapaxes(array, 0, 1).reshape(group_tokens, -1)

    small_parts = [router, attn_gain, mlp_gain, qk_gain, expert_ids.astype(BF16)]
    sizes = [part.size for part in small_parts]
    small = jnp.concatenate([part.reshape(-1) for part in small_parts])
    small_width = -(-small.size // (depth * 128)) * 128
    small = jnp.pad(small, (0, depth * small_width - small.size)).reshape(depth, small_width)
    own_tokens = by_micro(tokens)
    pull_own = by_micro(cotangent)
    sources = [w_qkv[:, 0], w_qkv[:, 1], w_qkv[:, 2], small, w_out, own_tokens, pull_own]
    pieces = tuple((n, 0, sources[n].shape[1], True, ("inner",)) for n in range(5))
    pieces += ((5, 0, features, False, ("side", "core")),)
    half = features // 2
    pieces += tuple((6, n * half, half, True, ("inner", "side", "core")) for n in range(2))
    full_q, full_k, full_v, small_all, full_out, raw_rows, pull_all = gather_blocks(
        sources, [ranks] * 5 + [quarters, ranks * quarters], pieces, ranks, 1
    )
    small_all = small_all.reshape(ranks, depth * small_width)
    ends = [sum(sizes[: n + 1]) for n in range(len(sizes))]
    full_router = small_all[:, : ends[0]].reshape(features, experts)
    gain_one = small_all[:, ends[0] : ends[1]].reshape(features).astype(F32)
    gain_two = small_all[:, ends[1] : ends[2]].reshape(features).astype(F32)
    full_qk = small_all[:, ends[2] : ends[3]].reshape(head_dim, 2, local_heads).astype(F32)
    all_ids = small_all[:, ends[3] : ends[4]].astype(jnp.int32)
    qk_rows = jnp.transpose(full_qk, (1, 2, 0)).reshape(2, local_width)

    portions = 2 if owned % 2 == 0 else 1
    portion = owned // portions
    raw_rows, expert_in, expert_out = lax.optimization_barrier((raw_rows, expert_in, expert_out))

    def weight_block(number, target):
        start = target * owned + number * portion
        part_in = lax.dynamic_slice_in_dim(expert_in, start, portion, 0)
        part_out = lax.dynamic_slice_in_dim(expert_out, start, portion, 0)
        joined = jnp.concatenate([part_in.reshape(portion, depth, 2 * width), part_out], axis=2)
        return joined[None]

    held = [
        send_blocks(functools.partial(weight_block, number), ranks) for number in range(portions)
    ]

    raw_rows = raw_rows.astype(F32)
    rows_one = (raw_rows * norm_factor(raw_rows) * gain_one).astype(BF16)
    query_raw = to_sequences(dot("td,df->tf", rows_one, full_q))
    key_raw = to_sequences(dot("td,df->tf", rows_one, full_k))
    value_rows = to_sequences(dot("td,df->tf", rows_one, full_v).astype(BF16))
    square_q, square_k = lax.psum(
        (jnp.sum(query_raw * query_raw, axis=-1), jnp.sum(key_raw * key_raw, axis=-1)), "tensor"
    )
    factor_q = lax.rsqrt(square_q[..., None] / features + EPSILON)
    factor_k = lax.rsqrt(square_k[..., None] / features + EPSILON)
    heads_shape = (micro_count, seq_len, local_heads, head_dim)
    query_heads = (query_raw * factor_q * qk_rows[0]).astype(BF16).reshape(heads_shape)
    key_heads = (key_raw * factor_k * qk_rows[1]).astype(BF16).reshape(heads_shape)
    value_heads = value_rows.reshape(heads_shape)
    seq_major = segments.T
    positions = jnp.arange(seq_len)
    distance = positions[:, None] - positions[None, :]
    same_doc = seq_major[:, :, None] == seq_major[:, None, :]
    allowed = (same_doc & (distance >= 0) & (distance < WINDOW))[:, None]
    scores = jnp.where(allowed, dot("mqhc,mkhc->mhqk", query_heads, key_heads) * scale, MASKED)
    weights_full = softmax_rows(scores)
    weights_low = weights_full.astype(BF16)
    head_out = dot("mhqk,mkhc->mqhc", weights_low, value_heads).astype(BF16)
    head_out = from_sequences(head_out.reshape(micro_count, seq_len, local_width))

    def scatter_quarters(array):
        across = ((0, 0, features, False, ("side", "core")),)
        (result,) = scatter_blocks([array], across, [quarters], ranks, 2)
        return result.astype(F32).reshape(own_shape)

    attended = scatter_quarters(dot("tf,df->td", head_out, full_out).astype(BF16))
    attended, held[0] = tie(attended, held[0], 0, 2)
    inputs = own_tokens.astype(F32).reshape(own_shape)
    residual = inputs + attended
    factor_two = norm_factor(residual)
    normed_two = (residual * factor_two * gain_two).astype(BF16).reshape(local_tokens, features)

    rows_all = gather_everywhere(normed_two, ranks, 3)
    rows_all, held[0] = tie(rows_all, held[0], 1, 2)
    router_probs = softmax_rows(dot("td,de->te", rows_all, full_router))

    first = rank * owned
    routes = all_ids.reshape(ranks, quarters, local_rows, micro_count, top_count)
    routes = jnp.swapaxes(routes, 2, 3).reshape(ranks, 1, group_tokens, top_count)
    names = first + jnp.arange(owned, dtype=jnp.int32)
    member = jnp.any(routes == names[:, None, None], axis=-1)
    order = jnp.arange(group_tokens)
    earlier = (order[:, None] < order[None, :]).astype(BF16)
    position = dot("ges,st->get", member.astype(BF16), earlier)
    position = jnp.where(member, position, -1.0).astype(jnp.int32)
    gate_own = lax.dynamic_slice_in_dim(router_probs, first, owned, 1)
    gate_own = jnp.swapaxes(gate_own.reshape(ranks, group_tokens, owned), 1, 2)
    lanes = jnp.arange(128, dtype=jnp.int32)
    column = (names[:, None] == lanes).astype(F32)
    before = ()
    sent = []
    for number in range(portions):
        part = slice(number * portion, (number + 1) * portion)
        mixture_all, returned_all, chosen, pulled, d_gate_up, hidden = expert_math(
            rows_all,
            pull_all,
            position[:, part],
            gate_own[:, part],
            column[part],
            held[number],
            before,
            number == portions - 1,
        )
        by_depth = (portion, ranks, CAP, ranks, depth)
        grad_in = dot("egsrk,egsf->rekf", chosen.reshape(by_depth), d_gate_up)
        grad_out = dot("egsrk,egsf->rekf", pulled.reshape(by_depth), hidden)
        grad_blocks = jnp.concatenate([grad_in.astype(BF16), grad_out.astype(BF16)], axis=3)
        returned_all, grad_blocks = lax.optimization_barrier((returned_all, grad_blocks))
        before = (mixture_all, returned_all)

        def grad_block(grad_blocks, target):
            return lax.dynamic_index_in_dim(grad_blocks, target, 0, keepdims=True)

        sent.append(send_blocks(functools.partial(grad_block, grad_blocks), ranks))
    if portions > 1:
        returned_all, sent[0] = tie(returned_all, sent[0], 0, 2)
    returned_own = scatter_everywhere(returned_all, ranks, 4)
    returned_own, sent[0] = tie(returned_own, sent[0], portions - 1, portions)

    returned_f = returned_own[:, :features].astype(F32)
    d_probs = returned_own[:, features : features + experts].astype(F32)
    first_token = (rank * quarters + quarter) * local_tokens
    probs_own = lax.dynamic_slice_in_dim(router_probs, first_token, local_tokens, 0)
    d_logits = (
        probs_own * (d_probs - jnp.sum(d_probs * probs_own, axis=-1, keepdims=True))
    ).astype(BF16)
    d_normed_two = (returned_f + dot("te,de->td", d_logits, full_router)).reshape(own_shape)
    grad_router = dot("td,te->de", normed_two, d_logits)
    pull_f = pull_own.astype(F32).reshape(own_shape)
    d_residual = pull_f + norm_back(residual, factor_two, gain_two, d_normed_two)
    grad_gain_two = jnp.sum(residual * factor_two * d_normed_two, axis=(0, 1))
    d_attended = d_residual.astype(BF16).reshape(local_tokens, features)

    (rows_back,) = gather_blocks(
        [d_attended], [quarters], ((0, 0, features, False, ("side", "core")),), ranks, 8
    )
    rows_back, sent[-1] = tie(rows_back, sent[-1], 0, 4)
    d_heads = to_sequences(dot("td,df->tf", rows_back, full_out).astype(BF16)).reshape(heads_shape)
    grad_w_out = dot("td,tf->df", rows_back, head_out)
    d_weights = dot("mqhc,mkhc->mhqk", d_heads, value_heads)
    d_scores = (
        weights_full * (d_weights - jnp.sum(d_weights * weights_full, axis=-1, keepdims=True))
    ).astype(BF16)
    flat_shape = (micro_count, seq_len, local_width)
    d_queries = (dot("mhqk,mkhc->mqhc", d_scores, key_heads) * scale).reshape(flat_shape)
    d_keys = (dot("mhqk,mqhc->mkhc", d_scores, query_heads) * scale).reshape(flat_shape)
    d_values = dot("mhqk,mqhc->mkhc", weights_low, d_heads).reshape(flat_shape).astype(BF16)
    inner_q, inner_k = lax.psum(
        (
            jnp.sum(query_raw * qk_rows[0] * d_queries, axis=-1),
            jnp.sum(key_raw * qk_rows[1] * d_keys, axis=-1),
        ),
        "tensor",
    )
    d_query_raw = (
        factor_q * qk_rows[0] * d_queries - query_raw * factor_q**3 * inner_q[..., None] / features
    )
    d_key_raw = (
        factor_k * qk_rows[1] * d_keys - key_raw * factor_k**3 * inner_k[..., None] / features
    )
    grad_qk_rows = jnp.stack(
        [
            jnp.sum(query_raw * factor_q * d_queries, axis=(0, 1)),
            jnp.sum(key_raw * factor_k * d_keys, axis=(0, 1)),
        ]
    )
    grad_qk = jnp.transpose(grad_qk_rows.reshape(2, local_heads, head_dim), (2, 0, 1))
    d_q = from_sequences(d_query_raw.astype(BF16))
    d_k = from_sequences(d_key_raw.astype(BF16))
    d_v = from_sequences(d_values)
    d_q, sent[-1] = tie(d_q, sent[-1], 1, 4)
    d_normed_one = scatter_quarters(
        (
            dot("tf,df->td", d_q, full_q)
            + dot("tf,df->td", d_k, full_k)
            + dot("tf,df->td", d_v, full_v)
        ).astype(BF16)
    )
    factor_one = norm_factor(inputs)
    grad_tokens = (d_residual + norm_back(inputs, factor_one, gain_one, d_normed_one)).astype(BF16)
    grad_gain_one = jnp.sum(inputs * factor_one * d_normed_one, axis=(0, 1))

    small_grads = [
        part.reshape(ranks, -1) for part in (grad_router, grad_gain_one, grad_gain_two, grad_qk)
    ]
    small_grads = jnp.concatenate(small_grads, axis=1)
    shared = depth * (experts + 2)
    slim = -(-small_grads.shape[1] // (depth * 128)) * 128
    small_grads = jnp.pad(small_grads, ((0, 0), (0, depth * slim - small_grads.shape[1])))
    grads = [dot("td,tf->df", rows_one, part).astype(BF16) for part in (d_q, d_k, d_v)]
    grads += [grad_w_out.astype(BF16), small_grads.reshape(features, slim).astype(BF16)]
    grads = jnp.concatenate(grads, axis=1)
    grads, sent[-1] = tie(grads, sent[-1], 2, 4)
    mixture_own, grads_own = scatter_everywhere(mixture_all, ranks, 10, grads)
    grads_own = grads_own.astype(F32)
    grad_qkv_own = grads_own[:, : 3 * local_width].reshape(depth, 3, local_width)
    grad_out_own = grads_own[:, 3 * local_width : 4 * local_width]
    small_own = grads_own[:, 4 * local_width :].reshape(-1)
    shared_own = lax.psum(small_own[:shared], "tensor")
    grad_qk_own = small_own[shared : shared + qk_gain.size].reshape(qk_gain.shape)

    layer_out = (residual + mixture_own.astype(F32).reshape(own_shape)).astype(BF16)
    grad_expert_in, grad_expert_out = settle(sent, owned, width)
    grad_expert_in = grad_expert_in.reshape(experts, depth, width // 128, 2, 128)
    grad_expert_in = jnp.swapaxes(grad_expert_in, 2, 3).reshape(experts, depth, 2, width)
    return (
        jnp.swapaxes(layer_out, 0, 1),
        jnp.swapaxes(grad_tokens, 0, 1),
        shared_own[depth * experts : depth * experts + depth],
        grad_qkv_own,
        grad_qk_own,
        grad_out_own,
        shared_own[depth * (experts + 1) :],
        shared_own[: depth * experts].reshape(depth, experts),
        grad_expert_in,
        grad_expert_out,
    )


def solution(mesh):
    placed = (
        P(("dp", "tensor"), None, None),
        P(("dp", "tensor"), None, None),
        P("dp", None),
        P("dp", None, None),
        P("dp"),
        P("dp", None, "tensor"),
        P("dp", None, "tensor"),
        P("dp", "tensor"),
        P("dp"),
        P("dp", None),
        P(None, "dp", None, "tensor"),
        P(None, "dp", "tensor"),
    )
    return jax.shard_map(
        functools.partial(body, mesh.shape["dp"], mesh.shape["tensor"]),
        mesh=mesh,
        in_specs=placed,
        out_specs=(
            P(("dp", "tensor"), None, None),
            P(("dp", "tensor"), None, None),
            P("dp"),
            P("dp", None, "tensor"),
            P("dp", None, "tensor"),
            P("dp", "tensor"),
            P("dp"),
            P("dp", None),
            P(None, "dp", None, "tensor"),
            P(None, "dp", "tensor"),
        ),
        check_vma=False,
    )
```

```python
import functools
import itertools

import jax
import jax.numpy as jnp
from jax import lax
from jax.experimental import pallas as pl
from jax.experimental.pallas import tpu as pltpu
from jax.sharding import PartitionSpec as P

WINDOW = 128
CAP = 176
EPSILON = 1e-05
MASKED = -1e30

MESH = pl.DeviceIdType.MESH
F32 = jnp.float32
BF16 = jnp.bfloat16


def norm_factor(values):
    return lax.rsqrt(jnp.mean(values * values, axis=-1, keepdims=True) + EPSILON)


def norm_back(values, factor, gain_row, upstream):
    features = values.shape[-1]
    inner = jnp.sum(values * gain_row * upstream, axis=-1, keepdims=True)
    return factor * gain_row * upstream - values * factor**3 * inner / features


def softmax_rows(logits):
    highest = jnp.max(logits, axis=-1, keepdims=True)
    raised = jnp.exp(logits - highest)
    return raised / jnp.sum(raised, axis=-1, keepdims=True)


def dot(spec, left, right):
    return jnp.einsum(spec, left, right, preferred_element_type=F32)


class Places:
    def __init__(self, ranks, pieces):
        rank = lax.axis_index("dp")
        quarter = lax.axis_index("tensor")
        count = ranks // 2
        self.count = count
        self.outer = rank // 2
        self.rank_base = self.outer * 2
        pairs = {
            "inner": lax.rem(rank, 2),
            "side": quarter // 2,
            "core": lax.rem(quarter, 2),
        }
        self.exists = {0: None}
        if any(piece[3] for piece in pieces):
            for steps in range(1, count):
                self.exists[steps] = self.outer + steps < count
                self.exists[-steps] = self.outer - steps >= 0
        self.inner = {}
        self.quarter = {}
        self.whole = {}
        for flips in itertools.product((0, 1), repeat=3):
            names = frozenset(name for name, bit in zip(("inner", "side", "core"), flips) if bit)
            place = {name: 1 - at if name in names else at for name, at in pairs.items()}
            self.inner[names] = self.rank_base + place["inner"]
            self.quarter[names] = place["side"] * 2 + place["core"]
            self.whole[names] = self.inner[names] * 4 + self.quarter[names]

    def device(self, steps, flips):
        names = frozenset(flips)
        return self.inner[names] + 2 * steps if steps else self.inner[names], self.quarter[names]

    def rows(self, piece, steps, flips, rows):
        names = frozenset(flips)
        if not piece[3]:
            index = self.quarter[names]
        elif "side" not in piece[4]:
            index = self.inner[names] + 2 * steps
        else:
            index = self.whole[names] + 8 * steps
        return pl.ds(pl.multiple_of(index * rows, rows), rows)


def run_if(conditions, action):
    conditions = [condition for condition in conditions if condition is not None]
    if not conditions:
        action()
        return
    pl.when(functools.reduce(jnp.logical_and, conditions))(action)


def greet(places, pieces):
    barrier = pltpu.get_barrier_semaphore()
    pairs = sorted({name for piece in pieces for name in piece[4]})
    targets = [(None, 0, (name,)) for name in pairs]
    if any(piece[3] for piece in pieces):
        targets += [(places.exists[steps], steps, ()) for steps in (-1, 1)]

    def signal(steps, flips):
        target = places.device(steps, flips)
        pl.semaphore_signal(barrier, inc=1, device_id=target, device_id_type=MESH)

    expected = len(pairs)
    for condition, steps, flips in targets:
        run_if([condition], functools.partial(signal, steps, flips))
        if condition is not None:
            expected = expected + condition.astype(jnp.int32)
    pl.semaphore_wait(barrier, expected)


def chain_steps(ranks, outer):
    count = ranks // 2
    return [0] + [sign * k for k in range(1, count) for sign in (-1, 1)] if outer else [0]


def all_bits(dims):
    return list(itertools.product((0, 1), repeat=len(dims)))


def semaphores(ranks, pieces):
    starts = [0]
    for _, _, _, outer, dims in pieces:
        starts.append(starts[-1] + len(chain_steps(ranks, outer)) * 2 ** len(dims))
    return starts


def chain_number(ranks, piece, steps):
    return steps + ranks // 2 - 1 if piece[3] else 0


def level_of(bits):
    return max((n + 1 for n, bit in enumerate(bits) if bit), default=0)


def gather_kernel(ranks, arrays, pieces, *refs):
    in_refs, out_refs = refs[:arrays], refs[arrays : 2 * arrays]
    send_sem, recv_sem, local_sem = refs[2 * arrays :]
    count = ranks // 2
    starts = semaphores(ranks, pieces)
    places = Places(ranks, pieces)
    greet(places, pieces)
    started = []

    def flips_of(p, bits):
        return tuple(name for name, bit in zip(pieces[p][4], bits) if bit)

    def copy(p, steps, bits, as_seen, target_steps, target_flips):
        array, start, width, _, dims = pieces[p]
        rows = in_refs[array].shape[0]
        columns = pl.ds(start, width)
        place = out_refs[array].at[
            places.rows(pieces[p], steps, flips_of(p, bits), rows), columns
        ]
        own = steps == 0 and not any(bits)
        seen_steps, seen_bits = as_seen
        sem = chain_number(ranks, pieces[p], seen_steps) * 2 ** len(dims)
        sem += starts[p] + all_bits(dims).index(seen_bits)
        return pltpu.make_async_remote_copy(
            src_ref=in_refs[array].at[:, columns] if own else place,
            dst_ref=place,
            send_sem=send_sem.at[sem],
            recv_sem=recv_sem.at[sem],
            device_id=places.device(target_steps, target_flips),
            device_id_type=MESH,
        )

    def send(conditions, *description):
        run_if(conditions, lambda: copy(*description).start())
        started.append((conditions, description))

    def forward(p, steps, bits):
        outer, dims = pieces[p][3:]
        here = places.exists[steps]
        level = level_of(bits)
        if outer and level == 0:
            for direction in (-1, 1):
                if steps * direction <= 0 and abs(steps) < count - 1:
                    there = places.exists[direction]
                    seen = (steps - direction, bits)
                    send([here, there], p, steps, bits, seen, direction, ())
        for n in range(level, len(dims)):
            seen = (steps, bits[:n] + (1,) + bits[n + 1 :])
            send([here], p, steps, bits, seen, 0, (dims[n],))

    def receive(p, steps, bits):
        here = places.exists[steps]
        run_if([here], lambda: copy(p, steps, bits, (steps, bits), 0, (pieces[p][4][0],)).wait_recv())
        forward(p, steps, bits)

    kept = []
    for array in range(arrays):
        piece = next(piece for piece in pieces if piece[0] == array)
        rows = in_refs[array].shape[0]
        keep = pltpu.make_async_copy(
            in_refs[array],
            out_refs[array].at[places.rows(piece, 0, (), rows)],
            local_sem.at[array],
        )
        keep.start()
        kept.append(keep)
    events = []
    for p, (_, _, _, outer, dims) in enumerate(pieces):
        for n, steps in enumerate(chain_steps(ranks, outer)):
            for bits in all_bits(dims):
                level = level_of(bits)
                turn = len(dims) + 1 if level == len(dims) else max(level - 1, 0)
                events.append((turn, abs(steps), n, level, p, steps, bits))
    for event in sorted(event for event in events if event[1] == 0 and event[3] == 0):
        forward(*event[4:])
    for event in sorted(event for event in events if event[1] or event[3]):
        receive(*event[4:])
    for conditions, description in started:
        run_if(conditions, lambda: copy(*description).wait_send())
    for keep in kept:
        keep.wait()


def gather_blocks(blocks, results, pieces, ranks, collective_id):
    arrays = len(blocks)
    transfers = semaphores(ranks, pieces)[-1]
    return pl.pallas_call(
        functools.partial(gather_kernel, ranks, arrays, pieces),
        out_shape=tuple(
            jax.ShapeDtypeStruct((number * block.shape[0], block.shape[1]), block.dtype)
            for block, number in zip(blocks, results)
        ),
        in_specs=[pl.BlockSpec(memory_space=pl.ANY)] * arrays,
        out_specs=(pl.BlockSpec(memory_space=pl.ANY),) * arrays,
        scratch_shapes=[
            pltpu.SemaphoreType.DMA((transfers,)),
            pltpu.SemaphoreType.DMA((transfers,)),
            pltpu.SemaphoreType.DMA((arrays,)),
        ],
        compiler_params=pltpu.CompilerParams(collective_id=collective_id, has_side_effects=True),
        cost_estimate=pl.CostEstimate(
            flops=0,
            bytes_accessed=sum(2 * n * block.size for block, n in zip(blocks, results)),
            transcendentals=0,
        ),
    )(*blocks)


def gather_everywhere(block, ranks, collective_id):
    columns = block.shape[1]
    cut = columns // 256 * 128
    pieces = (
        (0, 0, cut, True, ("inner", "side", "core")),
        (0, cut, columns - cut, True, ("side", "inner", "core")),
    )
    return gather_blocks([block], [4 * ranks], pieces, ranks, collective_id)[0]


def scatter_kernel(ranks, arrays, pieces, *refs):
    in_refs, out_refs, scratch = refs[:arrays], refs[arrays : 2 * arrays], refs[2 * arrays :]
    buffers, (send_sem, recv_sem, load_sem) = scratch[:-3], scratch[-3:]
    count = ranks // 2
    starts = semaphores(ranks, pieces)
    places = Places(ranks, pieces)
    greet(places, pieces)
    started = []
    held = []
    for _, _, _, _, dims in pieces:
        depth = len(dims)
        own, *paired = buffers[: depth + 1]
        up, down = buffers[depth + 1 : depth + 3]
        held.append((own, paired, up, down))
        buffers = buffers[depth + 3 :]

    def region(p, steps, bits):
        array, start, width, _, dims = pieces[p]
        flips = tuple(name for name, bit in zip(dims, bits) if bit)
        rows = out_refs[array].shape[0]
        return in_refs[array].at[places.rows(pieces[p], steps, flips, rows), pl.ds(start, width)]

    def slot(p, steps, bits):
        place = places.outer + steps if pieces[p][3] else 0
        number = 0
        for bit in bits:
            number = 2 * number + bit
        return place * 2 ** len(bits) + number

    def sem_of(p, steps, bits, kind):
        code = 0
        for bit in bits:
            code = 2 * code + bit
        number = chain_number(ranks, pieces[p], steps) * 2 ** len(bits) + code
        return (starts[p] + number) * 2 + kind

    def own_at(p, steps, bits):
        return held[p][0].at[slot(p, steps, bits)]

    def load(p, steps, bits):
        return pltpu.make_async_copy(
            region(p, steps, bits + (0,)),
            own_at(p, steps, bits),
            load_sem.at[sem_of(p, steps, bits + (0,), 0) // 2],
        )

    def pair_copy(p, steps, bits, n):
        dims = pieces[p][4]
        whole = bits[:n] + (1,) + (0,) * (len(dims) - n - 1)
        last = n == len(dims) - 1
        return pltpu.make_async_remote_copy(
            src_ref=region(p, steps, whole) if last else own_at(p, steps, whole[:-1]),
            dst_ref=held[p][1][n].at[slot(p, steps, bits[:n])],
            send_sem=send_sem.at[sem_of(p, steps, whole, 0)],
            recv_sem=recv_sem.at[sem_of(p, steps, whole, 0)],
            device_id=places.device(0, (dims[n],)),
            device_id_type=MESH,
        )

    def chain_copy(p, steps, direction):
        zeros = (0,) * (len(pieces[p][4]) - 1)
        sem = sem_of(p, steps - direction, zeros + (0,), 1)
        return pltpu.make_async_remote_copy(
            src_ref=own_at(p, steps, zeros),
            dst_ref=held[p][2 if direction > 0 else 3].at[slot(p, steps, ())],
            send_sem=send_sem.at[sem + (0 if direction > 0 else 2)],
            recv_sem=recv_sem.at[sem + (0 if direction > 0 else 2)],
            device_id=places.device(direction, ()),
            device_id_type=MESH,
        )

    def chain_arrival(p, steps, direction):
        zeros = (0,) * (len(pieces[p][4]) - 1)
        sem = sem_of(p, steps, zeros + (0,), 1) + (0 if direction > 0 else 2)
        place = held[p][2 if direction > 0 else 3].at[slot(p, steps, ())]
        return pltpu.make_async_remote_copy(
            src_ref=place,
            dst_ref=place,
            send_sem=send_sem.at[sem],
            recv_sem=recv_sem.at[sem],
            device_id=places.device(-direction, ()),
            device_id_type=MESH,
        )

    def add(target, sources):
        rows = target.shape[0]
        tile = min(rows, 32)

        def step(n, carry):
            part = pl.ds(pl.multiple_of(n * tile, tile), tile)
            total = sources[0][part].astype(F32)
            for source in sources[1:]:
                total = total + source[part].astype(F32)
            target[part] = total.astype(target.dtype)
            return carry

        lax.fori_loop(0, rows // tile, step, 0)

    order = []
    for array in range(arrays):
        entries = []
        for p, (of, _, _, outer, dims) in enumerate(pieces):
            if of == array:
                for n, steps in enumerate(chain_steps(ranks, outer)):
                    for bits in all_bits(dims[:-1]):
                        entries.append((-level_of(bits), -abs(steps), n, p, steps, bits))
        for n, entry in enumerate(sorted(entries)):
            order.append(((n + 1) / len(entries), array, n, entry[3:]))
    order = [entry[3] for entry in sorted(order)]
    for p, steps, bits in order:
        here = places.exists[steps]
        last = len(pieces[p][4]) - 1

        def begin(p=p, steps=steps, bits=bits, last=last):
            pair_copy(p, steps, bits, last).start()
            load(p, steps, bits).start()

        run_if([here], begin)
        started.append(([here], functools.partial(pair_copy, p, steps, bits, last)))
    for p, steps, bits in order:
        here = places.exists[steps]
        dims = pieces[p][4]
        level = level_of(bits)
        own, paired, up, down = held[p]

        def gather_terms(p=p, steps=steps, bits=bits, level=level, dims=dims, paired=paired):
            load(p, steps, bits).wait()
            sources = [own_at(p, steps, bits)]
            for n in range(len(dims) - 1, level - 1, -1):
                pair_copy(p, steps, bits, n).wait_recv()
                sources.append(paired[n].at[slot(p, steps, bits[:n])])
            add(own_at(p, steps, bits), sources)

        run_if([here], gather_terms)
        if level:

            def send_pair(p=p, steps=steps, bits=bits, level=level):
                return pair_copy(p, steps, bits, level - 1)

            run_if([here], lambda: send_pair().start())
            started.append(([here], send_pair))
            continue
        if pieces[p][3]:
            for direction in (1, -1):
                if steps * direction < 0 or abs(steps) == count - 1:
                    continue
                behind = places.exists[-direction]

                def take(p=p, steps=steps, bits=bits, direction=direction):
                    chain_arrival(p, steps, direction).wait_recv()
                    arrived = held[p][2 if direction > 0 else 3].at[slot(p, steps, ())]
                    add(own_at(p, steps, bits), [own_at(p, steps, bits), arrived])

                run_if([here, behind], take)
        if steps:
            direction = 1 if steps > 0 else -1

            def send_chain(p=p, steps=steps, direction=direction):
                return chain_copy(p, steps, direction)

            run_if([here], lambda: send_chain().start())
            started.append(([here], send_chain))
        else:
            array, start, width = pieces[p][:3]
            columns = pl.ds(start - min(piece[1] for piece in pieces if piece[0] == array), width)
            add(out_refs[array].at[:, columns], [own_at(p, 0, bits)])
    for conditions, build in started:
        run_if(conditions, lambda: build().wait_send())


def scatter_blocks(sources, pieces, blocks, ranks, collective_id):
    arrays = len(sources)
    count = ranks // 2
    out_shape = []
    for n, (source, number) in enumerate(zip(sources, blocks)):
        columns = sum(piece[2] for piece in pieces if piece[0] == n)
        out_shape.append(jax.ShapeDtypeStruct((source.shape[0] // number, columns), source.dtype))
    scratch = []
    for array, _, width, outer, dims in pieces:
        chain = count if outer else 1
        sizes = [chain * 2 ** (len(dims) - 1)]
        sizes += [chain * 2**n for n in range(len(dims))]
        sizes += [chain, chain] if outer else [1, 1]
        rows = out_shape[array].shape[0]
        scratch += [pltpu.VMEM((size, rows, width), sources[array].dtype) for size in sizes]
    transfers = semaphores(ranks, pieces)[-1]
    return pl.pallas_call(
        functools.partial(scatter_kernel, ranks, arrays, pieces),
        out_shape=tuple(out_shape),
        in_specs=[pl.BlockSpec(memory_space=pl.ANY)] * arrays,
        out_specs=(pl.BlockSpec(memory_space=pltpu.VMEM),) * arrays,
        scratch_shapes=[
            *scratch,
            pltpu.SemaphoreType.DMA((2 * transfers,)),
            pltpu.SemaphoreType.DMA((2 * transfers,)),
            pltpu.SemaphoreType.DMA((transfers,)),
        ],
        compiler_params=pltpu.CompilerParams(
            collective_id=collective_id,
            has_side_effects=True,
            vmem_limit_bytes=58 * 1024 * 1024,
        ),
        cost_estimate=pl.CostEstimate(
            flops=sum(source.size for source in sources),
            bytes_accessed=sum(2 * source.size for source in sources),
            transcendentals=0,
        ),
    )(*sources)


def scatter_everywhere(array, ranks, collective_id, beside=None):
    tiles = array.shape[1] // 128
    calls = max(1, ranks // 8)
    results = []
    other = None
    for call in range(calls):
        first, last = tiles * call // calls, tiles * (call + 1) // calls
        middle = (first + last + 1) // 2
        dims = ("inner", "side", "core")
        second = dims if beside is not None else ("side", "inner", "core")
        pieces = (
            (0, first * 128, (middle - first) * 128, True, dims),
            (0, middle * 128, (last - middle) * 128, True, second),
        )
        if beside is None or call:
            (result,) = scatter_blocks([array], pieces, [4 * ranks], ranks, collective_id + call)
        else:
            cut = beside.shape[1] // 256 * 128
            pieces += (
                (1, 0, cut, True, ("inner",)),
                (1, cut, beside.shape[1] - cut, True, ("inner",)),
            )
            result, other = scatter_blocks(
                [array, beside], pieces, [4 * ranks, ranks], ranks, collective_id
            )
        results.append(result)
    result = results[0] if calls == 1 else jnp.concatenate(results, axis=1)
    return (result, other) if beside is not None else result


def send_blocks(blocks, ranks):
    own = lax.axis_index("dp")
    received = [(own, blocks[0])]
    for shift in range(1, ranks):
        origin = lax.rem(own + ranks - shift, ranks)
        pairs = [(j, (j + shift) % ranks) for j in range(ranks)]
        received.append((origin, lax.ppermute(blocks[shift], "dp", pairs)))
    return received


def pack_kernel(width, target_ref, in_ref, out_ref, *refs):
    block_refs, (wide_ref, held_ref, sem) = refs[:-3], refs[-3:]
    del target_ref
    at = pl.program_id(0)
    tiles = width // 128
    steps = len(block_refs)
    portion, depth, _ = held_ref.shape[1:]

    def store(n):
        return pltpu.make_async_copy(held_ref.at[n % 2], block_refs[n].at[0], sem.at[n % 2])

    for n in range(2, steps):
        pl.when(at == n)(store(n - 2).wait)
    slot = lax.rem(at, 2)
    for e in range(portion):
        wide_ref[...] = in_ref[e].astype(F32)
        for j in range(2):
            for tile in range(tiles):
                rows = pl.ds(tile * 2 + j, depth, stride=2 * tiles)
                start = j * width + tile * 128
                held_ref[slot, e, :, start : start + 128] = wide_ref[rows, :].astype(BF16)
        held_ref[slot, e, :, 2 * width :] = out_ref[e]
    for n in range(steps):
        pl.when(at == n)(store(n).start)

    @pl.when(at == steps - 1)
    def _():
        for n in range(max(0, steps - 2), steps):
            store(n).wait()


def pack(expert_in, expert_out, ranks, portions):
    experts, depth, _, width = expert_in.shape
    portion = experts // ranks // portions
    tiles = width // 128
    rank = lax.axis_index("dp")
    targets = lax.rem(rank + jnp.arange(ranks, dtype=jnp.int32), ranks)
    in_rows = jnp.swapaxes(expert_in.reshape(experts, depth, 2, tiles, 128), 2, 3)
    in_rows = in_rows.reshape(experts, depth * tiles * 2, 128)
    block = jax.ShapeDtypeStruct((1, portion, depth, 3 * width), BF16)

    def place(step, targets):
        return targets[lax.rem(step, ranks)] * portions + step // ranks, 0, 0

    blocks = pl.pallas_call(
        functools.partial(pack_kernel, width),
        grid_spec=pltpu.PrefetchScalarGridSpec(
            num_scalar_prefetch=1,
            grid=(portions * ranks,),
            in_specs=[
                pl.BlockSpec((portion, depth * tiles * 2, 128), place),
                pl.BlockSpec((portion, depth, width), place),
            ],
            out_specs=(pl.BlockSpec(memory_space=pl.ANY),) * (portions * ranks),
            scratch_shapes=[
                pltpu.VMEM((depth * tiles * 2, 128), F32),
                pltpu.VMEM((2, portion, depth, 3 * width), BF16),
                pltpu.SemaphoreType.DMA((2,)),
            ],
        ),
        out_shape=(block,) * (portions * ranks),
        compiler_params=pltpu.CompilerParams(vmem_limit_bytes=32 * 1024 * 1024),
    )(targets, in_rows, expert_out)
    return [list(blocks[n * ranks : (n + 1) * ranks]) for n in range(portions)]


def settle_kernel(width, origin_ref, *refs):
    block_refs, (in_ref, out_ref, held_ref, load_sem) = refs[:-4], refs[-4:]
    del origin_ref
    at = pl.program_id(0)
    tiles = width // 128

    def load(n):
        return pltpu.make_async_copy(block_refs[n].at[0], held_ref.at[n], load_sem.at[n])

    @pl.when(at == 0)
    def _():
        for n in range(len(block_refs)):
            load(n).start()

    for n in range(len(block_refs)):
        pl.when(at == n)(load(n).wait)
    portion, depth, _ = held_ref.shape[1:]
    for e in range(portion):
        for j in range(2):
            for tile in range(tiles):
                rows = pl.ds(tile * 2 + j, depth, stride=2 * tiles)
                start = j * width + tile * 128
                in_ref[e, rows, :] = held_ref[at, e, :, start : start + 128].astype(F32)
        out_ref[e] = held_ref[at, e, :, 2 * width :].astype(F32)


def settle(sent, owned, width):
    portions = len(sent)
    ranks = len(sent[0])
    blocks = [block for received in sent for _, block in received]
    origins = jnp.stack([origin for origin, _ in sent[0]]).astype(jnp.int32)
    portion, depth, _ = blocks[0].shape[1:]
    in_rows = depth * 2 * width // 128

    def place(step, origins):
        return origins[lax.rem(step, ranks)] * portions + step // ranks, 0, 0

    return pl.pallas_call(
        functools.partial(settle_kernel, width),
        grid_spec=pltpu.PrefetchScalarGridSpec(
            num_scalar_prefetch=1,
            grid=(len(blocks),),
            in_specs=[pl.BlockSpec(memory_space=pl.ANY)] * len(blocks),
            out_specs=(
                pl.BlockSpec((portion, in_rows, 128), place),
                pl.BlockSpec((portion, depth, width), place),
            ),
            scratch_shapes=[
                pltpu.VMEM((len(blocks),) + blocks[0].shape[1:], BF16),
                pltpu.SemaphoreType.DMA((len(blocks),)),
            ],
        ),
        out_shape=(
            jax.ShapeDtypeStruct((owned * ranks, in_rows, 128), F32),
            jax.ShapeDtypeStruct((owned * ranks, depth, width), F32),
        ),
        compiler_params=pltpu.CompilerParams(vmem_limit_bytes=40 * 1024 * 1024),
    )(origins, *blocks)


def tie(value, received, part, parts):
    number = len(received) - 1
    first, last = 1 + number * part // parts, 1 + number * (part + 1) // parts
    blocks = [block for _, block in received[first:last]]
    if not blocks:
        return value, received
    value, blocks = lax.optimization_barrier((value, blocks))
    renewed = [(origin, block) for (origin, _), block in zip(received[first:last], blocks)]
    return value, received[:first] + renewed + received[last:]


def expert_kernel(ranks, owned, width, added, origin_ref, rows_ref, pull_ref, *refs):
    position_ref, across_ref, column_ref, *refs = refs
    block_refs, refs = refs[:ranks], refs[ranks:]
    before, refs = refs[: 2 * added], refs[2 * added :]
    mixture_ref, returned_ref, chosen_ref, pulled_ref, d_gate_up_ref, hidden_ref, *refs = refs
    place_ref, turned_ref, mixed_ref, back_ref, weight_ref, turned_weight_ref, dots_ref, load_sem = refs

    @pl.when(pl.program_id(0) == 0)
    def _():
        loads = [
            pltpu.make_async_copy(
                block_refs[n].at[0], weight_ref.at[origin_ref[n]], load_sem.at[n]
            )
            for n in range(ranks)
        ]
        for load in loads:
            load.start()
        for load in loads:
            load.wait()
        depth = weight_ref.shape[2]
        for e in range(owned):
            for n in range(ranks):
                turned_weight_ref[e, :, n * depth : (n + 1) * depth] = weight_ref[n, e].T

    group_tokens, features = pull_ref.shape
    chunk = min(features, 512)
    slot = lax.broadcasted_iota(jnp.int32, (CAP, group_tokens), 0)
    lane = lax.broadcasted_iota(jnp.int32, (group_tokens, owned * CAP), 1)
    turned = jnp.zeros((group_tokens, owned * CAP), BF16)
    for e in range(owned):
        place_ref[e * CAP : (e + 1) * CAP] = (position_ref[0, e : e + 1] == slot).astype(BF16)
        found = across_ref[0, :, e : e + 1]
        hit = (found >= 0) & (found + e * CAP == lane)
        turned = jnp.where(hit, jnp.ones_like(turned), turned)
    turned_ref[...] = turned
    for start in range(0, features, chunk):
        columns = slice(start, start + chunk)
        chosen = jnp.dot(place_ref[...], rows_ref[:, columns], preferred_element_type=F32)
        chosen_ref[:, 0, :, columns] = chosen.astype(BF16).reshape(owned, CAP, chunk)
        pulled = jnp.dot(place_ref[...], pull_ref[:, columns], preferred_element_type=F32)
        pulled_ref[:, 0, :, columns] = pulled.astype(BF16).reshape(owned, CAP, chunk)
    for e in range(owned):
        weight_in = weight_ref[:, e, :, : 2 * width].reshape(features, 2 * width)
        weight_out = weight_ref[:, e, :, 2 * width :].reshape(features, width)
        gate = jnp.dot(
            place_ref[e * CAP : (e + 1) * CAP],
            rows_ref[:, features:],
            preferred_element_type=F32,
        )
        gate = jnp.sum(gate * column_ref[owned + e : owned + e + 1], axis=1, keepdims=True)
        gate_up = jnp.dot(chosen_ref[e, 0], weight_in, preferred_element_type=F32)
        d_plain = jnp.dot(pulled_ref[e, 0], weight_out, preferred_element_type=F32)
        gate_part = gate_up[:, :width]
        up_part = gate_up[:, width:]
        sigmoid_gate = jax.nn.sigmoid(gate_part)
        activated = gate_part * sigmoid_gate
        hidden = activated * up_part
        slot_dots = jnp.sum(hidden * d_plain, axis=1, keepdims=True)
        dots_ref[e * CAP : (e + 1) * CAP] = (slot_dots * column_ref[e : e + 1]).astype(BF16)
        d_hidden = d_plain * gate
        d_gate_part = d_hidden * up_part * sigmoid_gate * (1.0 + gate_part * (1.0 - sigmoid_gate))
        d_up_part = d_hidden * activated
        hidden_ref[e, 0] = (hidden * gate).astype(BF16)
        d_gate_up_ref[e, 0, :, :width] = d_gate_part.astype(BF16)
        d_gate_up_ref[e, 0, :, width:] = d_up_part.astype(BF16)
        mixed_ref[e * CAP : (e + 1) * CAP] = jnp.dot(
            hidden_ref[e, 0], turned_weight_ref[e, 2 * width :], preferred_element_type=F32
        ).astype(BF16)
        back_ref[e * CAP : (e + 1) * CAP] = jnp.dot(
            d_gate_up_ref[e, 0], turned_weight_ref[e, : 2 * width], preferred_element_type=F32
        ).astype(BF16)
    def finish(target_ref, number, columns, total):
        if added:
            total = total + before[number][:, columns].astype(F32)
        target_ref[:, columns] = total.astype(BF16)

    spread = jnp.dot(turned_ref[...], dots_ref[...], preferred_element_type=F32)
    finish(returned_ref, 1, slice(features, features + 128), spread)
    for start in range(0, features, chunk):
        columns = slice(start, start + chunk)
        for number, (target_ref, source_ref) in enumerate(
            ((mixture_ref, mixed_ref), (returned_ref, back_ref))
        ):
            total = jnp.dot(
                turned_ref[...], source_ref[:, columns], preferred_element_type=F32
            )
            finish(target_ref, number, columns, total)


def expert_math(rows, pull, position, column, received, before, last):
    groups, owned, group_tokens = position.shape
    tokens, features = pull.shape
    ranks = len(received)
    depth = features // ranks
    width = received[0][1].shape[3] // 3
    slots = owned * CAP
    origins = jnp.stack([origin for origin, _ in received]).astype(jnp.int32)
    by_rows = pl.BlockSpec((group_tokens, features), lambda g, _: (g, 0))
    by_group = pl.BlockSpec((1, owned, group_tokens), lambda g, _: (g, 0, 0))
    by_returned = pl.BlockSpec((group_tokens, features + 128), lambda g, _: (g, 0))

    def by_slots(columns):
        return pl.BlockSpec((owned, 1, CAP, columns), lambda g, _: (0, g, 0, 0))

    def slot_array(columns):
        return jax.ShapeDtypeStruct((owned, groups, CAP, columns), BF16)

    aliases = {}
    if before:
        aliases = {6 + ranks: 0, 7 + ranks: 1}
    elif last:
        aliases = {2: 0}
    flops = 2 * groups * slots * features * (4 * group_tokens + 6 * width)
    return pl.pallas_call(
        functools.partial(expert_kernel, ranks, owned, width, 1 if before else 0),
        grid_spec=pltpu.PrefetchScalarGridSpec(
            num_scalar_prefetch=1,
            grid=(groups,),
            in_specs=[
                by_returned,
                by_rows,
                by_group,
                pl.BlockSpec((1, group_tokens, owned), lambda g, _: (g, 0, 0)),
                pl.BlockSpec((2 * owned, 128), lambda g, _: (0, 0)),
            ]
            + [pl.BlockSpec(memory_space=pl.ANY)] * ranks
            + ([by_rows, by_returned] if before else []),
            out_specs=(
                by_rows,
                by_returned,
                by_slots(features),
                by_slots(features),
                by_slots(2 * width),
                by_slots(width),
            ),
            scratch_shapes=[
                pltpu.VMEM((slots, group_tokens), BF16),
                pltpu.VMEM((group_tokens, slots), BF16),
                pltpu.VMEM((slots, features), BF16),
                pltpu.VMEM((slots, features), BF16),
                pltpu.VMEM((ranks, owned, depth, 3 * width), BF16),
                pltpu.VMEM((owned, 3 * width, features), BF16),
                pltpu.VMEM((slots, 128), BF16),
                pltpu.SemaphoreType.DMA((ranks,)),
            ],
        ),
        out_shape=(
            jax.ShapeDtypeStruct((tokens, features), BF16),
            jax.ShapeDtypeStruct((tokens, features + 128), BF16),
            slot_array(features),
            slot_array(features),
            slot_array(2 * width),
            slot_array(width),
        ),
        input_output_aliases=aliases,
        compiler_params=pltpu.CompilerParams(vmem_limit_bytes=60 * 1024 * 1024),
        cost_estimate=pl.CostEstimate(
            flops=flops,
            bytes_accessed=4 * tokens * features * 2 + slots * groups * features * 4,
            transcendentals=0,
        ),
    )(
        origins,
        rows,
        pull,
        position,
        jnp.swapaxes(position, 1, 2),
        column,
        *[block for _, block in received],
        *before,
    )


def body(
    ranks,
    quarters,
    tokens,
    cotangent,
    segments,
    expert_ids,
    attn_gain,
    w_qkv,
    qk_gain,
    w_out,
    mlp_gain,
    router,
    expert_in,
    expert_out,
):
    rank = lax.axis_index("dp")
    local_rows, micro_count, features = tokens.shape
    experts, depth, _, width = expert_in.shape
    top_count = expert_ids.shape[2]
    owned = experts // ranks
    local_tokens = local_rows * micro_count
    group_tokens = quarters * local_tokens
    head_dim = qk_gain.shape[0] * ranks
    local_heads = qk_gain.shape[2]
    local_width = local_heads * head_dim
    seq_len = local_rows * quarters
    scale = head_dim ** (-0.5)
    own_shape = (micro_count, local_rows, features)

    def by_micro(array):
        return jnp.swapaxes(array, 0, 1).reshape(local_tokens, features)

    def to_sequences(array):
        array = array.reshape(quarters, micro_count, local_rows, -1)
        return jnp.swapaxes(array, 0, 1).reshape(micro_count, seq_len, -1)

    def from_sequences(array):
        array = array.reshape(micro_count, quarters, local_rows, -1)
        return jnp.swapaxes(array, 0, 1).reshape(group_tokens, -1)

    small_parts = [router, attn_gain, mlp_gain, qk_gain, expert_ids.astype(BF16)]
    sizes = [part.size for part in small_parts]
    small = jnp.concatenate([part.reshape(-1) for part in small_parts])
    small_width = -(-small.size // (depth * 128)) * 128
    small = jnp.pad(small, (0, depth * small_width - small.size)).reshape(depth, small_width)
    own_tokens = by_micro(tokens)
    pull_own = by_micro(cotangent)
    sources = [w_qkv[:, 0], w_qkv[:, 1], w_qkv[:, 2], small, w_out, own_tokens, pull_own]
    pieces = tuple((n, 0, sources[n].shape[1], True, ("inner",)) for n in range(5))
    pieces += ((5, 0, features, False, ("side", "core")),)
    half = features // 2
    pieces += tuple((6, n * half, half, True, ("inner", "side", "core")) for n in range(2))
    full_q, full_k, full_v, small_all, full_out, raw_rows, pull_all = gather_blocks(
        sources, [ranks] * 5 + [quarters, ranks * quarters], pieces, ranks, 1
    )
    small_all = small_all.reshape(ranks, depth * small_width)
    ends = [sum(sizes[: n + 1]) for n in range(len(sizes))]
    full_router = small_all[:, : ends[0]].reshape(features, experts)
    gain_one = small_all[:, ends[0] : ends[1]].reshape(features).astype(F32)
    gain_two = small_all[:, ends[1] : ends[2]].reshape(features).astype(F32)
    full_qk = small_all[:, ends[2] : ends[3]].reshape(head_dim, 2, local_heads).astype(F32)
    all_ids = small_all[:, ends[3] : ends[4]].astype(jnp.int32)
    qk_rows = jnp.transpose(full_qk, (1, 2, 0)).reshape(2, local_width)

    portions = 2 if owned % 2 == 0 else 1
    portion = owned // portions
    packed = pack(expert_in, expert_out, ranks, portions)
    packed, raw_rows = lax.optimization_barrier((packed, raw_rows))
    held = [send_blocks(blocks, ranks) for blocks in packed]

    raw_rows = raw_rows.astype(F32)
    rows_one = (raw_rows * norm_factor(raw_rows) * gain_one).astype(BF16)
    query_raw = to_sequences(dot("td,df->tf", rows_one, full_q))
    key_raw = to_sequences(dot("td,df->tf", rows_one, full_k))
    value_rows = to_sequences(dot("td,df->tf", rows_one, full_v).astype(BF16))
    square_q, square_k = lax.psum(
        (jnp.sum(query_raw * query_raw, axis=-1), jnp.sum(key_raw * key_raw, axis=-1)), "tensor"
    )
    factor_q = lax.rsqrt(square_q[..., None] / features + EPSILON)
    factor_k = lax.rsqrt(square_k[..., None] / features + EPSILON)
    heads_shape = (micro_count, seq_len, local_heads, head_dim)
    query_heads = (query_raw * factor_q * qk_rows[0]).astype(BF16).reshape(heads_shape)
    key_heads = (key_raw * factor_k * qk_rows[1]).astype(BF16).reshape(heads_shape)
    value_heads = value_rows.reshape(heads_shape)
    seq_major = segments.T
    positions = jnp.arange(seq_len)
    distance = positions[:, None] - positions[None, :]
    same_doc = seq_major[:, :, None] == seq_major[:, None, :]
    allowed = (same_doc & (distance >= 0) & (distance < WINDOW))[:, None]
    scores = jnp.where(allowed, dot("mqhc,mkhc->mhqk", query_heads, key_heads) * scale, MASKED)
    weights_full = softmax_rows(scores)
    weights_low = weights_full.astype(BF16)
    head_out = dot("mhqk,mkhc->mqhc", weights_low, value_heads).astype(BF16)
    head_out = from_sequences(head_out.reshape(micro_count, seq_len, local_width))

    across = ((0, 0, features, False, ("side", "core")),)

    attended = dot("tf,df->td", head_out, full_out).astype(BF16)
    (attended,) = scatter_blocks([attended], across, [quarters], ranks, 2)
    attended, held[0] = tie(attended, held[0], 0, 2)
    inputs = own_tokens.astype(F32).reshape(own_shape)
    residual = inputs + attended.astype(F32).reshape(own_shape)
    factor_two = norm_factor(residual)
    normed_two = (residual * factor_two * gain_two).astype(BF16).reshape(local_tokens, features)

    probs_own = softmax_rows(dot("td,de->te", normed_two, full_router))
    probs_high = probs_own.astype(BF16)
    probs_low = (probs_own - probs_high.astype(F32)).astype(BF16)
    beside = [probs_high, probs_low, jnp.zeros((local_tokens, 128 - 2 * experts), BF16)]
    rows_all = gather_everywhere(jnp.concatenate([normed_two] + beside, axis=1), ranks, 3)
    rows_all, held[0] = tie(rows_all, held[0], 1, 2)
    if portions > 1:
        rows_all, held[1] = tie(rows_all, held[1], 0, 3)

    first = rank * owned
    routes = all_ids.reshape(ranks, quarters, local_rows, micro_count, top_count)
    routes = jnp.swapaxes(routes, 2, 3).reshape(ranks, 1, group_tokens, top_count)
    names = first + jnp.arange(owned, dtype=jnp.int32)
    member = jnp.any(routes == names[:, None, None], axis=-1)
    order = jnp.arange(group_tokens)
    earlier = (order[:, None] < order[None, :]).astype(BF16)
    position = dot("ges,st->get", member.astype(BF16), earlier)
    position = jnp.where(member, position, -1.0).astype(jnp.int32)
    lanes = jnp.arange(128, dtype=jnp.int32)
    column = [names[:, None] == lanes, names[:, None] == lax.rem(lanes, experts)]
    column[1] = column[1] & (lanes < 2 * experts)
    before = ()
    sent = []
    for number in range(portions):
        part = slice(number * portion, (number + 1) * portion)
        mixture_all, returned_all, chosen, pulled, d_gate_up, hidden = expert_math(
            rows_all,
            pull_all,
            position[:, part],
            jnp.concatenate([masks[part] for masks in column]).astype(F32),
            held[number],
            before,
            number == portions - 1,
        )
        by_depth = (portion, ranks, CAP, ranks, depth)
        grad_in = dot("egsrk,egsf->rekf", chosen.reshape(by_depth), d_gate_up)
        grad_out = dot("egsrk,egsf->rekf", pulled.reshape(by_depth), hidden)
        grad_blocks = jnp.concatenate([grad_in.astype(BF16), grad_out.astype(BF16)], axis=3)
        returned_all, grad_blocks = lax.optimization_barrier((returned_all, grad_blocks))
        before = (mixture_all, returned_all)
        if number + 1 < portions:
            grad_blocks, held[number + 1] = tie(grad_blocks, held[number + 1], 0, 1)
        targets = [lax.rem(rank + shift, ranks) for shift in range(ranks)]
        blocks = [lax.dynamic_index_in_dim(grad_blocks, to, 0, keepdims=True) for to in targets]
        sent.append(send_blocks(blocks, ranks))
    if portions > 1:
        for part in range(4):
            returned_all, sent[0] = tie(returned_all, sent[0], part, 7)
    returned_own = scatter_everywhere(returned_all, ranks, 4)
    if portions > 1:
        for part in range(4, 7):
            returned_own, sent[0] = tie(returned_own, sent[0], part, 7)
    for part in range(2):
        returned_own, sent[-1] = tie(returned_own, sent[-1], part, 7)

    returned_f = returned_own[:, :features].astype(F32)
    d_probs = returned_own[:, features : features + experts].astype(F32)
    d_logits = (
        probs_own * (d_probs - jnp.sum(d_probs * probs_own, axis=-1, keepdims=True))
    ).astype(BF16)
    d_normed_two = (returned_f + dot("te,de->td", d_logits, full_router)).reshape(own_shape)
    grad_router = dot("td,te->de", normed_two, d_logits)
    pull_f = pull_own.astype(F32).reshape(own_shape)
    d_residual = pull_f + norm_back(residual, factor_two, gain_two, d_normed_two)
    grad_gain_two = jnp.sum(residual * factor_two * d_normed_two, axis=(0, 1))
    d_attended = d_residual.astype(BF16).reshape(local_tokens, features)

    (rows_back,) = gather_blocks(
        [d_attended], [quarters], ((0, 0, features, False, ("side", "core")),), ranks, 8
    )
    d_heads = to_sequences(dot("td,df->tf", rows_back, full_out).astype(BF16)).reshape(heads_shape)
    grad_w_out = dot("td,tf->df", rows_back, head_out)
    d_weights = dot("mqhc,mkhc->mhqk", d_heads, value_heads)
    d_scores = (
        weights_full * (d_weights - jnp.sum(d_weights * weights_full, axis=-1, keepdims=True))
    ).astype(BF16)
    flat_shape = (micro_count, seq_len, local_width)
    d_queries = (dot("mhqk,mkhc->mqhc", d_scores, key_heads) * scale).reshape(flat_shape)
    d_keys = (dot("mhqk,mqhc->mkhc", d_scores, query_heads) * scale).reshape(flat_shape)
    d_values = dot("mhqk,mqhc->mkhc", weights_low, d_heads).reshape(flat_shape).astype(BF16)
    inner_q, inner_k = lax.psum(
        (
            jnp.sum(query_raw * qk_rows[0] * d_queries, axis=-1),
            jnp.sum(key_raw * qk_rows[1] * d_keys, axis=-1),
        ),
        "tensor",
    )
    d_query_raw = (
        factor_q * qk_rows[0] * d_queries - query_raw * factor_q**3 * inner_q[..., None] / features
    )
    d_key_raw = (
        factor_k * qk_rows[1] * d_keys - key_raw * factor_k**3 * inner_k[..., None] / features
    )
    grad_qk_rows = jnp.stack(
        [
            jnp.sum(query_raw * factor_q * d_queries, axis=(0, 1)),
            jnp.sum(key_raw * factor_k * d_keys, axis=(0, 1)),
        ]
    )
    grad_qk = jnp.transpose(grad_qk_rows.reshape(2, local_heads, head_dim), (2, 0, 1))
    d_q = from_sequences(d_query_raw.astype(BF16))
    d_k = from_sequences(d_key_raw.astype(BF16))
    d_v = from_sequences(d_values)
    d_normed_one = (
        dot("tf,df->td", d_q, full_q)
        + dot("tf,df->td", d_k, full_k)
        + dot("tf,df->td", d_v, full_v)
    ).astype(BF16)
    (d_normed_one,) = scatter_blocks([d_normed_one], across, [quarters], ranks, 2)
    d_normed_one = d_normed_one.astype(F32).reshape(own_shape)
    factor_one = norm_factor(inputs)
    grad_tokens = (d_residual + norm_back(inputs, factor_one, gain_one, d_normed_one)).astype(BF16)
    grad_gain_one = jnp.sum(inputs * factor_one * d_normed_one, axis=(0, 1))

    small_grads = [
        part.reshape(ranks, -1) for part in (grad_router, grad_gain_one, grad_gain_two, grad_qk)
    ]
    small_grads = jnp.concatenate(small_grads, axis=1)
    shared = depth * (experts + 2)
    slim = -(-small_grads.shape[1] // (depth * 128)) * 128
    small_grads = jnp.pad(small_grads, ((0, 0), (0, depth * slim - small_grads.shape[1])))
    grads = [dot("td,tf->df", rows_one, part).astype(BF16) for part in (d_q, d_k, d_v)]
    grads += [grad_w_out.astype(BF16), small_grads.reshape(features, slim).astype(BF16)]
    grads = jnp.concatenate(grads, axis=1)
    for part in range(2, 6):
        grads, sent[-1] = tie(grads, sent[-1], part, 7)
    mixture_own, grads_own = scatter_everywhere(mixture_all, ranks, 10, grads)
    grads_own = grads_own.astype(F32)
    grad_qkv_own = grads_own[:, : 3 * local_width].reshape(depth, 3, local_width)
    grad_out_own = grads_own[:, 3 * local_width : 4 * local_width]
    small_own = grads_own[:, 4 * local_width :].reshape(-1)
    shared_own = lax.psum(small_own[:shared], "tensor")
    grad_qk_own = small_own[shared : shared + qk_gain.size].reshape(qk_gain.shape)

    layer_out = (residual + mixture_own.astype(F32).reshape(own_shape)).astype(BF16)
    grad_expert_in, grad_expert_out = settle(sent, owned, width)
    grad_expert_in = grad_expert_in.reshape(experts, depth, width // 128, 2, 128)
    grad_expert_in = jnp.swapaxes(grad_expert_in, 2, 3).reshape(experts, depth, 2, width)
    return (
        jnp.swapaxes(layer_out, 0, 1),
        jnp.swapaxes(grad_tokens, 0, 1),
        shared_own[depth * experts : depth * experts + depth],
        grad_qkv_own,
        grad_qk_own,
        grad_out_own,
        shared_own[depth * (experts + 1) :],
        shared_own[: depth * experts].reshape(depth, experts),
        grad_expert_in,
        grad_expert_out,
    )


def solution(mesh):
    placed = (
        P(("dp", "tensor"), None, None),
        P(("dp", "tensor"), None, None),
        P("dp", None),
        P("dp", None, None),
        P("dp"),
        P("dp", None, "tensor"),
        P("dp", None, "tensor"),
        P("dp", "tensor"),
        P("dp"),
        P("dp", None),
        P(None, "dp", None, "tensor"),
        P(None, "dp", "tensor"),
    )
    return jax.shard_map(
        functools.partial(body, mesh.shape["dp"], mesh.shape["tensor"]),
        mesh=mesh,
        in_specs=placed,
        out_specs=(
            P(("dp", "tensor"), None, None),
            P(("dp", "tensor"), None, None),
            P("dp"),
            P("dp", None, "tensor"),
            P("dp", None, "tensor"),
            P("dp", "tensor"),
            P("dp"),
            P("dp", None),
            P(None, "dp", None, "tensor"),
            P(None, "dp", "tensor"),
        ),
        check_vma=False,
    )
```

```python
import functools
import itertools

import jax
import jax.numpy as jnp
from jax import lax
from jax.experimental import pallas as pl
from jax.experimental.pallas import tpu as pltpu
from jax.sharding import PartitionSpec as P

WINDOW = 128
CAP = 176
EPSILON = 1e-05
MASKED = -1e30

MESH = pl.DeviceIdType.MESH
F32 = jnp.float32
BF16 = jnp.bfloat16


def norm_factor(values):
    return lax.rsqrt(jnp.mean(values * values, axis=-1, keepdims=True) + EPSILON)


def norm_back(values, factor, gain_row, upstream):
    features = values.shape[-1]
    inner = jnp.sum(values * gain_row * upstream, axis=-1, keepdims=True)
    return factor * gain_row * upstream - values * factor**3 * inner / features


def softmax_rows(logits):
    highest = jnp.max(logits, axis=-1, keepdims=True)
    raised = jnp.exp(logits - highest)
    return raised / jnp.sum(raised, axis=-1, keepdims=True)


def dot(spec, left, right):
    return jnp.einsum(spec, left, right, preferred_element_type=F32)


class Places:
    def __init__(self, ranks, pieces):
        rank = lax.axis_index("dp")
        quarter = lax.axis_index("tensor")
        count = ranks // 2
        self.count = count
        self.outer = rank // 2
        self.rank_base = self.outer * 2
        pairs = {
            "inner": lax.rem(rank, 2),
            "side": quarter // 2,
            "core": lax.rem(quarter, 2),
        }
        self.exists = {0: None}
        if any(piece[3] for piece in pieces):
            for steps in range(1, count):
                self.exists[steps] = self.outer + steps < count
                self.exists[-steps] = self.outer - steps >= 0
        self.inner = {}
        self.quarter = {}
        self.whole = {}
        for flips in itertools.product((0, 1), repeat=3):
            names = frozenset(name for name, bit in zip(("inner", "side", "core"), flips) if bit)
            place = {name: 1 - at if name in names else at for name, at in pairs.items()}
            self.inner[names] = self.rank_base + place["inner"]
            self.quarter[names] = place["side"] * 2 + place["core"]
            self.whole[names] = self.inner[names] * 4 + self.quarter[names]

    def device(self, steps, flips):
        names = frozenset(flips)
        return self.inner[names] + 2 * steps if steps else self.inner[names], self.quarter[names]

    def rows(self, piece, steps, flips, rows):
        names = frozenset(flips)
        if not piece[3]:
            index = self.quarter[names]
        elif "side" not in piece[4]:
            index = self.inner[names] + 2 * steps
        else:
            index = self.whole[names] + 8 * steps
        return pl.ds(pl.multiple_of(index * rows, rows), rows)


def run_if(conditions, action):
    conditions = [condition for condition in conditions if condition is not None]
    if not conditions:
        action()
        return
    pl.when(functools.reduce(jnp.logical_and, conditions))(action)


def greet(places, pieces):
    barrier = pltpu.get_barrier_semaphore()
    pairs = sorted({name for piece in pieces for name in piece[4]})
    targets = [(None, 0, (name,)) for name in pairs]
    if any(piece[3] for piece in pieces):
        targets += [(places.exists[steps], steps, ()) for steps in (-1, 1)]

    def signal(steps, flips):
        target = places.device(steps, flips)
        pl.semaphore_signal(barrier, inc=1, device_id=target, device_id_type=MESH)

    expected = len(pairs)
    for condition, steps, flips in targets:
        run_if([condition], functools.partial(signal, steps, flips))
        if condition is not None:
            expected = expected + condition.astype(jnp.int32)
    pl.semaphore_wait(barrier, expected)


def chain_steps(ranks, outer):
    count = ranks // 2
    return [0] + [sign * k for k in range(1, count) for sign in (-1, 1)] if outer else [0]


def all_bits(dims):
    return list(itertools.product((0, 1), repeat=len(dims)))


def semaphores(ranks, pieces):
    starts = [0]
    for _, _, _, outer, dims in pieces:
        starts.append(starts[-1] + len(chain_steps(ranks, outer)) * 2 ** len(dims))
    return starts


def chain_number(ranks, piece, steps):
    return steps + ranks // 2 - 1 if piece[3] else 0


def level_of(bits):
    return max((n + 1 for n, bit in enumerate(bits) if bit), default=0)


def gather_kernel(ranks, arrays, pieces, *refs):
    in_refs, out_refs = refs[:arrays], refs[arrays : 2 * arrays]
    send_sem, recv_sem, local_sem = refs[2 * arrays :]
    count = ranks // 2
    starts = semaphores(ranks, pieces)
    places = Places(ranks, pieces)
    greet(places, pieces)
    started = []

    def flips_of(p, bits):
        return tuple(name for name, bit in zip(pieces[p][4], bits) if bit)

    def copy(p, steps, bits, as_seen, target_steps, target_flips):
        array, start, width, _, dims = pieces[p]
        rows = in_refs[array].shape[0]
        columns = pl.ds(start, width)
        place = out_refs[array].at[
            places.rows(pieces[p], steps, flips_of(p, bits), rows), columns
        ]
        own = steps == 0 and not any(bits)
        seen_steps, seen_bits = as_seen
        sem = chain_number(ranks, pieces[p], seen_steps) * 2 ** len(dims)
        sem += starts[p] + all_bits(dims).index(seen_bits)
        return pltpu.make_async_remote_copy(
            src_ref=in_refs[array].at[:, columns] if own else place,
            dst_ref=place,
            send_sem=send_sem.at[sem],
            recv_sem=recv_sem.at[sem],
            device_id=places.device(target_steps, target_flips),
            device_id_type=MESH,
        )

    def send(conditions, *description):
        run_if(conditions, lambda: copy(*description).start())
        started.append((conditions, description))

    def forward(p, steps, bits):
        outer, dims = pieces[p][3:]
        here = places.exists[steps]
        level = level_of(bits)
        if outer and level == 0:
            for direction in (-1, 1):
                if steps * direction <= 0 and abs(steps) < count - 1:
                    there = places.exists[direction]
                    seen = (steps - direction, bits)
                    send([here, there], p, steps, bits, seen, direction, ())
        for n in range(level, len(dims)):
            seen = (steps, bits[:n] + (1,) + bits[n + 1 :])
            send([here], p, steps, bits, seen, 0, (dims[n],))

    def receive(p, steps, bits):
        here = places.exists[steps]
        run_if([here], lambda: copy(p, steps, bits, (steps, bits), 0, (pieces[p][4][0],)).wait_recv())
        forward(p, steps, bits)

    kept = []
    for array in range(arrays):
        piece = next(piece for piece in pieces if piece[0] == array)
        rows = in_refs[array].shape[0]
        keep = pltpu.make_async_copy(
            in_refs[array],
            out_refs[array].at[places.rows(piece, 0, (), rows)],
            local_sem.at[array],
        )
        keep.start()
        kept.append(keep)
    events = []
    for p, (_, _, _, outer, dims) in enumerate(pieces):
        for n, steps in enumerate(chain_steps(ranks, outer)):
            for bits in all_bits(dims):
                level = level_of(bits)
                turn = 4 if level == len(dims) else max(level - 1, 0)
                key = abs(steps) + level if turn < 4 else 0
                events.append((turn, key, n, level, p, steps, bits))
    for event in sorted(event for event in events if event[5] == 0 and event[3] == 0):
        forward(*event[4:])
    for event in sorted(event for event in events if event[5] or event[3]):
        receive(*event[4:])
    for conditions, description in started:
        run_if(conditions, lambda: copy(*description).wait_send())
    for keep in kept:
        keep.wait()


def gather_blocks(blocks, results, pieces, ranks, collective_id):
    arrays = len(blocks)
    transfers = semaphores(ranks, pieces)[-1]
    return pl.pallas_call(
        functools.partial(gather_kernel, ranks, arrays, pieces),
        out_shape=tuple(
            jax.ShapeDtypeStruct((number * block.shape[0], block.shape[1]), block.dtype)
            for block, number in zip(blocks, results)
        ),
        in_specs=[pl.BlockSpec(memory_space=pl.ANY)] * arrays,
        out_specs=(pl.BlockSpec(memory_space=pl.ANY),) * arrays,
        scratch_shapes=[
            pltpu.SemaphoreType.DMA((transfers,)),
            pltpu.SemaphoreType.DMA((transfers,)),
            pltpu.SemaphoreType.DMA((arrays,)),
        ],
        compiler_params=pltpu.CompilerParams(collective_id=collective_id, has_side_effects=True),
        cost_estimate=pl.CostEstimate(
            flops=0,
            bytes_accessed=sum(2 * n * block.size for block, n in zip(blocks, results)),
            transcendentals=0,
        ),
    )(*blocks)


def gather_everywhere(block, ranks, collective_id):
    columns = block.shape[1]
    cut = columns // 256 * 128
    pieces = (
        (0, 0, cut, True, ("inner", "side", "core")),
        (0, cut, columns - cut, True, ("side", "inner", "core")),
    )
    return gather_blocks([block], [4 * ranks], pieces, ranks, collective_id)[0]


def scatter_kernel(ranks, arrays, pieces, *refs):
    in_refs, out_refs, scratch = refs[:arrays], refs[arrays : 2 * arrays], refs[2 * arrays :]
    buffers, (send_sem, recv_sem, load_sem) = scratch[:-3], scratch[-3:]
    count = ranks // 2
    starts = semaphores(ranks, pieces)
    places = Places(ranks, pieces)
    greet(places, pieces)
    started = []
    held = []
    for _, _, _, _, dims in pieces:
        depth = len(dims)
        own, *paired = buffers[: depth + 1]
        up, down = buffers[depth + 1 : depth + 3]
        held.append((own, paired, up, down))
        buffers = buffers[depth + 3 :]

    def region(p, steps, bits):
        array, start, width, _, dims = pieces[p]
        flips = tuple(name for name, bit in zip(dims, bits) if bit)
        rows = out_refs[array].shape[0]
        return in_refs[array].at[places.rows(pieces[p], steps, flips, rows), pl.ds(start, width)]

    def slot(p, steps, bits):
        place = places.outer + steps if pieces[p][3] else 0
        number = 0
        for bit in bits:
            number = 2 * number + bit
        return place * 2 ** len(bits) + number

    def sem_of(p, steps, bits, kind):
        code = 0
        for bit in bits:
            code = 2 * code + bit
        number = chain_number(ranks, pieces[p], steps) * 2 ** len(bits) + code
        return (starts[p] + number) * 2 + kind

    def own_at(p, steps, bits):
        return held[p][0].at[slot(p, steps, bits)]

    def load(p, steps, bits):
        return pltpu.make_async_copy(
            region(p, steps, bits + (0,)),
            own_at(p, steps, bits),
            load_sem.at[sem_of(p, steps, bits + (0,), 0) // 2],
        )

    def pair_copy(p, steps, bits, n):
        dims = pieces[p][4]
        whole = bits[:n] + (1,) + (0,) * (len(dims) - n - 1)
        last = n == len(dims) - 1
        return pltpu.make_async_remote_copy(
            src_ref=region(p, steps, whole) if last else own_at(p, steps, whole[:-1]),
            dst_ref=held[p][1][n].at[slot(p, steps, bits[:n])],
            send_sem=send_sem.at[sem_of(p, steps, whole, 0)],
            recv_sem=recv_sem.at[sem_of(p, steps, whole, 0)],
            device_id=places.device(0, (dims[n],)),
            device_id_type=MESH,
        )

    def chain_copy(p, steps, direction):
        zeros = (0,) * (len(pieces[p][4]) - 1)
        sem = sem_of(p, steps - direction, zeros + (0,), 1)
        return pltpu.make_async_remote_copy(
            src_ref=own_at(p, steps, zeros),
            dst_ref=held[p][2 if direction > 0 else 3].at[slot(p, steps, ())],
            send_sem=send_sem.at[sem + (0 if direction > 0 else 2)],
            recv_sem=recv_sem.at[sem + (0 if direction > 0 else 2)],
            device_id=places.device(direction, ()),
            device_id_type=MESH,
        )

    def chain_arrival(p, steps, direction):
        zeros = (0,) * (len(pieces[p][4]) - 1)
        sem = sem_of(p, steps, zeros + (0,), 1) + (0 if direction > 0 else 2)
        place = held[p][2 if direction > 0 else 3].at[slot(p, steps, ())]
        return pltpu.make_async_remote_copy(
            src_ref=place,
            dst_ref=place,
            send_sem=send_sem.at[sem],
            recv_sem=recv_sem.at[sem],
            device_id=places.device(-direction, ()),
            device_id_type=MESH,
        )

    def add(target, sources):
        rows = target.shape[0]
        tile = min(rows, 32)

        def step(n, carry):
            part = pl.ds(pl.multiple_of(n * tile, tile), tile)
            total = sources[0][part].astype(F32)
            for source in sources[1:]:
                total = total + source[part].astype(F32)
            target[part] = total.astype(target.dtype)
            return carry

        lax.fori_loop(0, rows // tile, step, 0)

    order = []
    for array in range(arrays):
        entries = []
        for p, (of, _, _, outer, dims) in enumerate(pieces):
            if of == array:
                for n, steps in enumerate(chain_steps(ranks, outer)):
                    for bits in all_bits(dims[:-1]):
                        entries.append((-level_of(bits), -abs(steps), n, p, steps, bits))
        for n, entry in enumerate(sorted(entries)):
            order.append(((n + 1) / len(entries), array, n, entry[3:]))
    order = [entry[3] for entry in sorted(order)]
    for p, steps, bits in order:
        here = places.exists[steps]
        last = len(pieces[p][4]) - 1

        def begin(p=p, steps=steps, bits=bits, last=last):
            pair_copy(p, steps, bits, last).start()
            load(p, steps, bits).start()

        run_if([here], begin)
        started.append(([here], functools.partial(pair_copy, p, steps, bits, last)))
    for p, steps, bits in order:
        here = places.exists[steps]
        dims = pieces[p][4]
        level = level_of(bits)
        own, paired, up, down = held[p]

        def gather_terms(p=p, steps=steps, bits=bits, level=level, dims=dims, paired=paired):
            load(p, steps, bits).wait()
            sources = [own_at(p, steps, bits)]
            for n in range(len(dims) - 1, level - 1, -1):
                pair_copy(p, steps, bits, n).wait_recv()
                sources.append(paired[n].at[slot(p, steps, bits[:n])])
            add(own_at(p, steps, bits), sources)

        run_if([here], gather_terms)
        if level:

            def send_pair(p=p, steps=steps, bits=bits, level=level):
                return pair_copy(p, steps, bits, level - 1)

            run_if([here], lambda: send_pair().start())
            started.append(([here], send_pair))
            continue
        if pieces[p][3]:
            for direction in (1, -1):
                if steps * direction < 0 or abs(steps) == count - 1:
                    continue
                behind = places.exists[-direction]

                def take(p=p, steps=steps, bits=bits, direction=direction):
                    chain_arrival(p, steps, direction).wait_recv()
                    arrived = held[p][2 if direction > 0 else 3].at[slot(p, steps, ())]
                    add(own_at(p, steps, bits), [own_at(p, steps, bits), arrived])

                run_if([here, behind], take)
        if steps:
            direction = 1 if steps > 0 else -1

            def send_chain(p=p, steps=steps, direction=direction):
                return chain_copy(p, steps, direction)

            run_if([here], lambda: send_chain().start())
            started.append(([here], send_chain))
        else:
            array, start, width = pieces[p][:3]
            columns = pl.ds(start - min(piece[1] for piece in pieces if piece[0] == array), width)
            add(out_refs[array].at[:, columns], [own_at(p, 0, bits)])
    for conditions, build in started:
        run_if(conditions, lambda: build().wait_send())


def scatter_blocks(sources, pieces, blocks, ranks, collective_id):
    arrays = len(sources)
    count = ranks // 2
    out_shape = []
    for n, (source, number) in enumerate(zip(sources, blocks)):
        columns = sum(piece[2] for piece in pieces if piece[0] == n)
        out_shape.append(jax.ShapeDtypeStruct((source.shape[0] // number, columns), source.dtype))
    scratch = []
    for array, _, width, outer, dims in pieces:
        chain = count if outer else 1
        sizes = [chain * 2 ** (len(dims) - 1)]
        sizes += [chain * 2**n for n in range(len(dims))]
        sizes += [chain, chain] if outer else [1, 1]
        rows = out_shape[array].shape[0]
        scratch += [pltpu.VMEM((size, rows, width), sources[array].dtype) for size in sizes]
    transfers = semaphores(ranks, pieces)[-1]
    return pl.pallas_call(
        functools.partial(scatter_kernel, ranks, arrays, pieces),
        out_shape=tuple(out_shape),
        in_specs=[pl.BlockSpec(memory_space=pl.ANY)] * arrays,
        out_specs=(pl.BlockSpec(memory_space=pltpu.VMEM),) * arrays,
        scratch_shapes=[
            *scratch,
            pltpu.SemaphoreType.DMA((2 * transfers,)),
            pltpu.SemaphoreType.DMA((2 * transfers,)),
            pltpu.SemaphoreType.DMA((transfers,)),
        ],
        compiler_params=pltpu.CompilerParams(
            collective_id=collective_id,
            has_side_effects=True,
            vmem_limit_bytes=58 * 1024 * 1024,
        ),
        cost_estimate=pl.CostEstimate(
            flops=sum(source.size for source in sources),
            bytes_accessed=sum(2 * source.size for source in sources),
            transcendentals=0,
        ),
    )(*sources)


def scatter_everywhere(array, ranks, collective_id, beside=None):
    tiles = array.shape[1] // 128
    calls = max(1, ranks // 8)
    results = []
    other = None
    for call in range(calls):
        first, last = tiles * call // calls, tiles * (call + 1) // calls
        middle = (first + last + 1) // 2
        dims = ("inner", "side", "core")
        second = dims if beside is not None else ("side", "inner", "core")
        pieces = (
            (0, first * 128, (middle - first) * 128, True, dims),
            (0, middle * 128, (last - middle) * 128, True, second),
        )
        if beside is None or call:
            (result,) = scatter_blocks([array], pieces, [4 * ranks], ranks, collective_id + call)
        else:
            cut = beside.shape[1] // 256 * 128
            pieces += (
                (1, 0, cut, True, ("inner",)),
                (1, cut, beside.shape[1] - cut, True, ("inner",)),
            )
            result, other = scatter_blocks(
                [array, beside], pieces, [4 * ranks, ranks], ranks, collective_id
            )
        results.append(result)
    result = results[0] if calls == 1 else jnp.concatenate(results, axis=1)
    return (result, other) if beside is not None else result


def send_blocks(blocks, ranks):
    own = lax.axis_index("dp")
    received = [(own, blocks[0])]
    for shift in range(1, ranks):
        origin = lax.rem(own + ranks - shift, ranks)
        pairs = [(j, (j + shift) % ranks) for j in range(ranks)]
        received.append((origin, lax.ppermute(blocks[shift], "dp", pairs)))
    return received


def pack_kernel(width, target_ref, in_ref, out_ref, *refs):
    block_refs, (wide_ref, held_ref, sem) = refs[:-3], refs[-3:]
    del target_ref
    at = pl.program_id(0)
    tiles = width // 128
    steps = len(block_refs)
    portion, depth, _ = held_ref.shape[1:]

    def store(n):
        return pltpu.make_async_copy(held_ref.at[n % 2], block_refs[n].at[0], sem.at[n % 2])

    for n in range(2, steps):
        pl.when(at == n)(store(n - 2).wait)
    slot = lax.rem(at, 2)
    for e in range(portion):
        wide_ref[...] = in_ref[e].astype(F32)
        for j in range(2):
            for tile in range(tiles):
                rows = pl.ds(tile * 2 + j, depth, stride=2 * tiles)
                start = j * width + tile * 128
                held_ref[slot, e, :, start : start + 128] = wide_ref[rows, :].astype(BF16)
        held_ref[slot, e, :, 2 * width :] = out_ref[e]
    for n in range(steps):
        pl.when(at == n)(store(n).start)

    @pl.when(at == steps - 1)
    def _():
        for n in range(max(0, steps - 2), steps):
            store(n).wait()


def pack(expert_in, expert_out, ranks, portions):
    experts, depth, _, width = expert_in.shape
    portion = experts // ranks // portions
    tiles = width // 128
    rank = lax.axis_index("dp")
    targets = lax.rem(rank + jnp.arange(ranks, dtype=jnp.int32), ranks)
    in_rows = jnp.swapaxes(expert_in.reshape(experts, depth, 2, tiles, 128), 2, 3)
    in_rows = in_rows.reshape(experts, depth * tiles * 2, 128)
    block = jax.ShapeDtypeStruct((1, portion, depth, 3 * width), BF16)

    def place(step, targets):
        return targets[lax.rem(step, ranks)] * portions + step // ranks, 0, 0

    blocks = pl.pallas_call(
        functools.partial(pack_kernel, width),
        grid_spec=pltpu.PrefetchScalarGridSpec(
            num_scalar_prefetch=1,
            grid=(portions * ranks,),
            in_specs=[
                pl.BlockSpec((portion, depth * tiles * 2, 128), place),
                pl.BlockSpec((portion, depth, width), place),
            ],
            out_specs=(pl.BlockSpec(memory_space=pl.ANY),) * (portions * ranks),
            scratch_shapes=[
                pltpu.VMEM((depth * tiles * 2, 128), F32),
                pltpu.VMEM((2, portion, depth, 3 * width), BF16),
                pltpu.SemaphoreType.DMA((2,)),
            ],
        ),
        out_shape=(block,) * (portions * ranks),
        compiler_params=pltpu.CompilerParams(vmem_limit_bytes=32 * 1024 * 1024),
    )(targets, in_rows, expert_out)
    return [list(blocks[n * ranks : (n + 1) * ranks]) for n in range(portions)]


def settle_kernel(width, origin_ref, *refs):
    block_refs, (in_ref, out_ref, held_ref, load_sem) = refs[:-4], refs[-4:]
    del origin_ref
    at = pl.program_id(0)
    tiles = width // 128

    def load(n):
        return pltpu.make_async_copy(block_refs[n].at[0], held_ref.at[n], load_sem.at[n])

    @pl.when(at == 0)
    def _():
        for n in range(len(block_refs)):
            load(n).start()

    for n in range(len(block_refs)):
        pl.when(at == n)(load(n).wait)
    portion, depth, _ = held_ref.shape[1:]
    for e in range(portion):
        for j in range(2):
            for tile in range(tiles):
                rows = pl.ds(tile * 2 + j, depth, stride=2 * tiles)
                start = j * width + tile * 128
                in_ref[e, rows, :] = held_ref[at, e, :, start : start + 128].astype(F32)
        out_ref[e] = held_ref[at, e, :, 2 * width :].astype(F32)


def settle(sent, owned, width):
    portions = len(sent)
    ranks = len(sent[0])
    blocks = [block for received in sent for _, block in received]
    origins = jnp.stack([origin for origin, _ in sent[0]]).astype(jnp.int32)
    portion, depth, _ = blocks[0].shape[1:]
    in_rows = depth * 2 * width // 128

    def place(step, origins):
        return origins[lax.rem(step, ranks)] * portions + step // ranks, 0, 0

    return pl.pallas_call(
        functools.partial(settle_kernel, width),
        grid_spec=pltpu.PrefetchScalarGridSpec(
            num_scalar_prefetch=1,
            grid=(len(blocks),),
            in_specs=[pl.BlockSpec(memory_space=pl.ANY)] * len(blocks),
            out_specs=(
                pl.BlockSpec((portion, in_rows, 128), place),
                pl.BlockSpec((portion, depth, width), place),
            ),
            scratch_shapes=[
                pltpu.VMEM((len(blocks),) + blocks[0].shape[1:], BF16),
                pltpu.SemaphoreType.DMA((len(blocks),)),
            ],
        ),
        out_shape=(
            jax.ShapeDtypeStruct((owned * ranks, in_rows, 128), F32),
            jax.ShapeDtypeStruct((owned * ranks, depth, width), F32),
        ),
        compiler_params=pltpu.CompilerParams(vmem_limit_bytes=40 * 1024 * 1024),
    )(origins, *blocks)


def tie(value, received, part, parts):
    number = len(received) - 1
    first, last = 1 + number * part // parts, 1 + number * (part + 1) // parts
    blocks = [block for _, block in received[first:last]]
    if not blocks:
        return value, received
    value, blocks = lax.optimization_barrier((value, blocks))
    renewed = [(origin, block) for (origin, _), block in zip(received[first:last], blocks)]
    return value, received[:first] + renewed + received[last:]


def expert_kernel(ranks, owned, width, added, origin_ref, rows_ref, pull_ref, *refs):
    position_ref, across_ref, column_ref, *refs = refs
    block_refs, refs = refs[:ranks], refs[ranks:]
    before, refs = refs[: 2 * added], refs[2 * added :]
    mixture_ref, returned_ref, chosen_ref, pulled_ref, d_gate_up_ref, hidden_ref, *refs = refs
    place_ref, turned_ref, mixed_ref, back_ref, weight_ref, turned_weight_ref, dots_ref, load_sem = refs

    @pl.when(pl.program_id(0) == 0)
    def _():
        loads = [
            pltpu.make_async_copy(
                block_refs[n].at[0], weight_ref.at[origin_ref[n]], load_sem.at[n]
            )
            for n in range(ranks)
        ]
        for load in loads:
            load.start()
        for load in loads:
            load.wait()
        depth = weight_ref.shape[2]
        for e in range(owned):
            for n in range(ranks):
                turned_weight_ref[e, :, n * depth : (n + 1) * depth] = weight_ref[n, e].T

    group_tokens, features = pull_ref.shape
    chunk = min(features, 512)
    slot = lax.broadcasted_iota(jnp.int32, (CAP, group_tokens), 0)
    lane = lax.broadcasted_iota(jnp.int32, (group_tokens, owned * CAP), 1)
    turned = jnp.zeros((group_tokens, owned * CAP), BF16)
    for e in range(owned):
        place_ref[e * CAP : (e + 1) * CAP] = (position_ref[0, e : e + 1] == slot).astype(BF16)
        found = across_ref[0, :, e : e + 1]
        hit = (found >= 0) & (found + e * CAP == lane)
        turned = jnp.where(hit, jnp.ones_like(turned), turned)
    turned_ref[...] = turned
    for start in range(0, features, chunk):
        columns = slice(start, start + chunk)
        chosen = jnp.dot(place_ref[...], rows_ref[:, columns], preferred_element_type=F32)
        chosen_ref[:, 0, :, columns] = chosen.astype(BF16).reshape(owned, CAP, chunk)
        pulled = jnp.dot(place_ref[...], pull_ref[:, columns], preferred_element_type=F32)
        pulled_ref[:, 0, :, columns] = pulled.astype(BF16).reshape(owned, CAP, chunk)
    for e in range(owned):
        weight_in = weight_ref[:, e, :, : 2 * width].reshape(features, 2 * width)
        weight_out = weight_ref[:, e, :, 2 * width :].reshape(features, width)
        gate = jnp.dot(
            place_ref[e * CAP : (e + 1) * CAP],
            rows_ref[:, features:],
            preferred_element_type=F32,
        )
        gate = jnp.sum(gate * column_ref[owned + e : owned + e + 1], axis=1, keepdims=True)
        gate_up = jnp.dot(chosen_ref[e, 0], weight_in, preferred_element_type=F32)
        d_plain = jnp.dot(pulled_ref[e, 0], weight_out, preferred_element_type=F32)
        gate_part = gate_up[:, :width]
        up_part = gate_up[:, width:]
        sigmoid_gate = jax.nn.sigmoid(gate_part)
        activated = gate_part * sigmoid_gate
        hidden = activated * up_part
        slot_dots = jnp.sum(hidden * d_plain, axis=1, keepdims=True)
        dots_ref[e * CAP : (e + 1) * CAP] = (slot_dots * column_ref[e : e + 1]).astype(BF16)
        d_hidden = d_plain * gate
        d_gate_part = d_hidden * up_part * sigmoid_gate * (1.0 + gate_part * (1.0 - sigmoid_gate))
        d_up_part = d_hidden * activated
        hidden_ref[e, 0] = (hidden * gate).astype(BF16)
        d_gate_up_ref[e, 0, :, :width] = d_gate_part.astype(BF16)
        d_gate_up_ref[e, 0, :, width:] = d_up_part.astype(BF16)
        mixed_ref[e * CAP : (e + 1) * CAP] = jnp.dot(
            hidden_ref[e, 0], turned_weight_ref[e, 2 * width :], preferred_element_type=F32
        ).astype(BF16)
        back_ref[e * CAP : (e + 1) * CAP] = jnp.dot(
            d_gate_up_ref[e, 0], turned_weight_ref[e, : 2 * width], preferred_element_type=F32
        ).astype(BF16)
    def finish(target_ref, number, columns, total):
        if added:
            total = total + before[number][:, columns].astype(F32)
        target_ref[:, columns] = total.astype(BF16)

    spread = jnp.dot(turned_ref[...], dots_ref[...], preferred_element_type=F32)
    finish(returned_ref, 1, slice(features, features + 128), spread)
    for start in range(0, features, chunk):
        columns = slice(start, start + chunk)
        for number, (target_ref, source_ref) in enumerate(
            ((mixture_ref, mixed_ref), (returned_ref, back_ref))
        ):
            total = jnp.dot(
                turned_ref[...], source_ref[:, columns], preferred_element_type=F32
            )
            finish(target_ref, number, columns, total)


def expert_math(rows, pull, position, column, received, before, last):
    groups, owned, group_tokens = position.shape
    tokens, features = pull.shape
    ranks = len(received)
    depth = features // ranks
    width = received[0][1].shape[3] // 3
    slots = owned * CAP
    origins = jnp.stack([origin for origin, _ in received]).astype(jnp.int32)
    by_rows = pl.BlockSpec((group_tokens, features), lambda g, _: (g, 0))
    by_group = pl.BlockSpec((1, owned, group_tokens), lambda g, _: (g, 0, 0))
    by_returned = pl.BlockSpec((group_tokens, features + 128), lambda g, _: (g, 0))

    def by_slots(columns):
        return pl.BlockSpec((owned, 1, CAP, columns), lambda g, _: (0, g, 0, 0))

    def slot_array(columns):
        return jax.ShapeDtypeStruct((owned, groups, CAP, columns), BF16)

    aliases = {}
    if before:
        aliases = {6 + ranks: 0, 7 + ranks: 1}
    elif last:
        aliases = {2: 0}
    flops = 2 * groups * slots * features * (4 * group_tokens + 6 * width)
    return pl.pallas_call(
        functools.partial(expert_kernel, ranks, owned, width, 1 if before else 0),
        grid_spec=pltpu.PrefetchScalarGridSpec(
            num_scalar_prefetch=1,
            grid=(groups,),
            in_specs=[
                by_returned,
                by_rows,
                by_group,
                pl.BlockSpec((1, group_tokens, owned), lambda g, _: (g, 0, 0)),
                pl.BlockSpec((2 * owned, 128), lambda g, _: (0, 0)),
            ]
            + [pl.BlockSpec(memory_space=pl.ANY)] * ranks
            + ([by_rows, by_returned] if before else []),
            out_specs=(
                by_rows,
                by_returned,
                by_slots(features),
                by_slots(features),
                by_slots(2 * width),
                by_slots(width),
            ),
            scratch_shapes=[
                pltpu.VMEM((slots, group_tokens), BF16),
                pltpu.VMEM((group_tokens, slots), BF16),
                pltpu.VMEM((slots, features), BF16),
                pltpu.VMEM((slots, features), BF16),
                pltpu.VMEM((ranks, owned, depth, 3 * width), BF16),
                pltpu.VMEM((owned, 3 * width, features), BF16),
                pltpu.VMEM((slots, 128), BF16),
                pltpu.SemaphoreType.DMA((ranks,)),
            ],
        ),
        out_shape=(
            jax.ShapeDtypeStruct((tokens, features), BF16),
            jax.ShapeDtypeStruct((tokens, features + 128), BF16),
            slot_array(features),
            slot_array(features),
            slot_array(2 * width),
            slot_array(width),
        ),
        input_output_aliases=aliases,
        compiler_params=pltpu.CompilerParams(vmem_limit_bytes=60 * 1024 * 1024),
        cost_estimate=pl.CostEstimate(
            flops=flops,
            bytes_accessed=4 * tokens * features * 2 + slots * groups * features * 4,
            transcendentals=0,
        ),
    )(
        origins,
        rows,
        pull,
        position,
        jnp.swapaxes(position, 1, 2),
        column,
        *[block for _, block in received],
        *before,
    )


def body(
    ranks,
    quarters,
    tokens,
    cotangent,
    segments,
    expert_ids,
    attn_gain,
    w_qkv,
    qk_gain,
    w_out,
    mlp_gain,
    router,
    expert_in,
    expert_out,
):
    rank = lax.axis_index("dp")
    local_rows, micro_count, features = tokens.shape
    experts, depth, _, width = expert_in.shape
    top_count = expert_ids.shape[2]
    owned = experts // ranks
    local_tokens = local_rows * micro_count
    group_tokens = quarters * local_tokens
    head_dim = qk_gain.shape[0] * ranks
    local_heads = qk_gain.shape[2]
    local_width = local_heads * head_dim
    seq_len = local_rows * quarters
    scale = head_dim ** (-0.5)
    own_shape = (micro_count, local_rows, features)

    def by_micro(array):
        return jnp.swapaxes(array, 0, 1).reshape(local_tokens, features)

    def to_sequences(array):
        array = array.reshape(quarters, micro_count, local_rows, -1)
        return jnp.swapaxes(array, 0, 1).reshape(micro_count, seq_len, -1)

    def from_sequences(array):
        array = array.reshape(micro_count, quarters, local_rows, -1)
        return jnp.swapaxes(array, 0, 1).reshape(group_tokens, -1)

    small_parts = [router, attn_gain, mlp_gain, qk_gain, expert_ids.astype(BF16)]
    sizes = [part.size for part in small_parts]
    small = jnp.concatenate([part.reshape(-1) for part in small_parts])
    small_width = -(-small.size // (depth * 128)) * 128
    small = jnp.pad(small, (0, depth * small_width - small.size)).reshape(depth, small_width)
    own_tokens = by_micro(tokens)
    pull_own = by_micro(cotangent)
    sources = [w_qkv[:, 0], w_qkv[:, 1], w_qkv[:, 2], small, w_out, own_tokens, pull_own]
    pieces = tuple((n, 0, sources[n].shape[1], True, ("inner",)) for n in range(5))
    pieces += ((5, 0, features, False, ("side", "core")),)
    half = features // 2
    pieces += tuple((6, n * half, half, True, ("inner", "side", "core")) for n in range(2))
    full_q, full_k, full_v, small_all, full_out, raw_rows, pull_all = gather_blocks(
        sources, [ranks] * 5 + [quarters, ranks * quarters], pieces, ranks, 1
    )
    small_all = small_all.reshape(ranks, depth * small_width)
    ends = [sum(sizes[: n + 1]) for n in range(len(sizes))]
    full_router = small_all[:, : ends[0]].reshape(features, experts)
    gain_one = small_all[:, ends[0] : ends[1]].reshape(features).astype(F32)
    gain_two = small_all[:, ends[1] : ends[2]].reshape(features).astype(F32)
    full_qk = small_all[:, ends[2] : ends[3]].reshape(head_dim, 2, local_heads).astype(F32)
    all_ids = small_all[:, ends[3] : ends[4]].astype(jnp.int32)
    qk_rows = jnp.transpose(full_qk, (1, 2, 0)).reshape(2, local_width)

    portions = 2 if owned % 2 == 0 else 1
    portion = owned // portions
    packed = pack(expert_in, expert_out, ranks, portions)
    packed, raw_rows = lax.optimization_barrier((packed, raw_rows))
    held = [send_blocks(blocks, ranks) for blocks in packed]

    raw_rows = raw_rows.astype(F32)
    rows_one = (raw_rows * norm_factor(raw_rows) * gain_one).astype(BF16)
    query_raw = to_sequences(dot("td,df->tf", rows_one, full_q))
    key_raw = to_sequences(dot("td,df->tf", rows_one, full_k))
    value_rows = to_sequences(dot("td,df->tf", rows_one, full_v).astype(BF16))
    square_q, square_k = lax.psum(
        (jnp.sum(query_raw * query_raw, axis=-1), jnp.sum(key_raw * key_raw, axis=-1)), "tensor"
    )
    factor_q = lax.rsqrt(square_q[..., None] / features + EPSILON)
    factor_k = lax.rsqrt(square_k[..., None] / features + EPSILON)
    heads_shape = (micro_count, seq_len, local_heads, head_dim)
    query_heads = (query_raw * factor_q * qk_rows[0]).astype(BF16).reshape(heads_shape)
    key_heads = (key_raw * factor_k * qk_rows[1]).astype(BF16).reshape(heads_shape)
    value_heads = value_rows.reshape(heads_shape)
    seq_major = segments.T
    positions = jnp.arange(seq_len)
    distance = positions[:, None] - positions[None, :]
    same_doc = seq_major[:, :, None] == seq_major[:, None, :]
    allowed = (same_doc & (distance >= 0) & (distance < WINDOW))[:, None]
    scores = jnp.where(allowed, dot("mqhc,mkhc->mhqk", query_heads, key_heads) * scale, MASKED)
    weights_full = softmax_rows(scores)
    weights_low = weights_full.astype(BF16)
    head_out = dot("mhqk,mkhc->mqhc", weights_low, value_heads).astype(BF16)
    head_out = from_sequences(head_out.reshape(micro_count, seq_len, local_width))

    across = ((0, 0, features, False, ("side", "core")),)

    attended = dot("tf,df->td", head_out, full_out).astype(BF16)
    (attended,) = scatter_blocks([attended], across, [quarters], ranks, 2)
    attended, held[0] = tie(attended, held[0], 0, 2)
    inputs = own_tokens.astype(F32).reshape(own_shape)
    residual = inputs + attended.astype(F32).reshape(own_shape)
    factor_two = norm_factor(residual)
    normed_two = (residual * factor_two * gain_two).astype(BF16).reshape(local_tokens, features)

    probs_own = softmax_rows(dot("td,de->te", normed_two, full_router))
    probs_high = probs_own.astype(BF16)
    probs_low = (probs_own - probs_high.astype(F32)).astype(BF16)
    beside = [probs_high, probs_low, jnp.zeros((local_tokens, 128 - 2 * experts), BF16)]
    rows_all = gather_everywhere(jnp.concatenate([normed_two] + beside, axis=1), ranks, 3)
    rows_all, held[0] = tie(rows_all, held[0], 1, 2)
    if portions > 1:
        rows_all, held[1] = tie(rows_all, held[1], 0, 3)

    first = rank * owned
    routes = all_ids.reshape(ranks, quarters, local_rows, micro_count, top_count)
    routes = jnp.swapaxes(routes, 2, 3).reshape(ranks, 1, group_tokens, top_count)
    names = first + jnp.arange(owned, dtype=jnp.int32)
    member = jnp.any(routes == names[:, None, None], axis=-1)
    order = jnp.arange(group_tokens)
    earlier = (order[:, None] < order[None, :]).astype(BF16)
    position = dot("ges,st->get", member.astype(BF16), earlier)
    position = jnp.where(member, position, -1.0).astype(jnp.int32)
    lanes = jnp.arange(128, dtype=jnp.int32)
    column = [names[:, None] == lanes, names[:, None] == lax.rem(lanes, experts)]
    column[1] = column[1] & (lanes < 2 * experts)
    before = ()
    sent = []
    for number in range(portions):
        part = slice(number * portion, (number + 1) * portion)
        mixture_all, returned_all, chosen, pulled, d_gate_up, hidden = expert_math(
            rows_all,
            pull_all,
            position[:, part],
            jnp.concatenate([masks[part] for masks in column]).astype(F32),
            held[number],
            before,
            number == portions - 1,
        )
        by_depth = (portion, ranks, CAP, ranks, depth)
        grad_in = dot("egsrk,egsf->rekf", chosen.reshape(by_depth), d_gate_up)
        grad_out = dot("egsrk,egsf->rekf", pulled.reshape(by_depth), hidden)
        grad_blocks = jnp.concatenate([grad_in.astype(BF16), grad_out.astype(BF16)], axis=3)
        returned_all, grad_blocks = lax.optimization_barrier((returned_all, grad_blocks))
        before = (mixture_all, returned_all)
        if number + 1 < portions:
            grad_blocks, held[number + 1] = tie(grad_blocks, held[number + 1], 0, 1)
        targets = [lax.rem(rank + shift, ranks) for shift in range(ranks)]
        blocks = [lax.dynamic_index_in_dim(grad_blocks, to, 0, keepdims=True) for to in targets]
        sent.append(send_blocks(blocks, ranks))
    if portions > 1:
        for part in range(4):
            returned_all, sent[0] = tie(returned_all, sent[0], part, 7)
    returned_own = scatter_everywhere(returned_all, ranks, 4)
    if portions > 1:
        for part in range(4, 7):
            returned_own, sent[0] = tie(returned_own, sent[0], part, 7)
    for part in range(2):
        returned_own, sent[-1] = tie(returned_own, sent[-1], part, 7)

    returned_f = returned_own[:, :features].astype(F32)
    d_probs = returned_own[:, features : features + experts].astype(F32)
    d_logits = (
        probs_own * (d_probs - jnp.sum(d_probs * probs_own, axis=-1, keepdims=True))
    ).astype(BF16)
    d_normed_two = (returned_f + dot("te,de->td", d_logits, full_router)).reshape(own_shape)
    grad_router = dot("td,te->de", normed_two, d_logits)
    pull_f = pull_own.astype(F32).reshape(own_shape)
    d_residual = pull_f + norm_back(residual, factor_two, gain_two, d_normed_two)
    grad_gain_two = jnp.sum(residual * factor_two * d_normed_two, axis=(0, 1))
    d_attended = d_residual.astype(BF16).reshape(local_tokens, features)

    (rows_back,) = gather_blocks(
        [d_attended], [quarters], ((0, 0, features, False, ("side", "core")),), ranks, 8
    )
    d_heads = to_sequences(dot("td,df->tf", rows_back, full_out).astype(BF16)).reshape(heads_shape)
    grad_w_out = dot("td,tf->df", rows_back, head_out)
    d_weights = dot("mqhc,mkhc->mhqk", d_heads, value_heads)
    d_scores = (
        weights_full * (d_weights - jnp.sum(d_weights * weights_full, axis=-1, keepdims=True))
    ).astype(BF16)
    flat_shape = (micro_count, seq_len, local_width)
    d_queries = (dot("mhqk,mkhc->mqhc", d_scores, key_heads) * scale).reshape(flat_shape)
    d_keys = (dot("mhqk,mqhc->mkhc", d_scores, query_heads) * scale).reshape(flat_shape)
    d_values = dot("mhqk,mqhc->mkhc", weights_low, d_heads).reshape(flat_shape).astype(BF16)
    inner_q, inner_k = lax.psum(
        (
            jnp.sum(query_raw * qk_rows[0] * d_queries, axis=-1),
            jnp.sum(key_raw * qk_rows[1] * d_keys, axis=-1),
        ),
        "tensor",
    )
    d_query_raw = (
        factor_q * qk_rows[0] * d_queries - query_raw * factor_q**3 * inner_q[..., None] / features
    )
    d_key_raw = (
        factor_k * qk_rows[1] * d_keys - key_raw * factor_k**3 * inner_k[..., None] / features
    )
    grad_qk_rows = jnp.stack(
        [
            jnp.sum(query_raw * factor_q * d_queries, axis=(0, 1)),
            jnp.sum(key_raw * factor_k * d_keys, axis=(0, 1)),
        ]
    )
    grad_qk = jnp.transpose(grad_qk_rows.reshape(2, local_heads, head_dim), (2, 0, 1))
    d_q = from_sequences(d_query_raw.astype(BF16))
    d_k = from_sequences(d_key_raw.astype(BF16))
    d_v = from_sequences(d_values)
    d_normed_one = (
        dot("tf,df->td", d_q, full_q)
        + dot("tf,df->td", d_k, full_k)
        + dot("tf,df->td", d_v, full_v)
    ).astype(BF16)
    (d_normed_one,) = scatter_blocks([d_normed_one], across, [quarters], ranks, 2)
    d_normed_one = d_normed_one.astype(F32).reshape(own_shape)
    factor_one = norm_factor(inputs)
    grad_tokens = (d_residual + norm_back(inputs, factor_one, gain_one, d_normed_one)).astype(BF16)
    grad_gain_one = jnp.sum(inputs * factor_one * d_normed_one, axis=(0, 1))

    small_grads = [
        part.reshape(ranks, -1) for part in (grad_router, grad_gain_one, grad_gain_two, grad_qk)
    ]
    small_grads = jnp.concatenate(small_grads, axis=1)
    shared = depth * (experts + 2)
    slim = -(-small_grads.shape[1] // (depth * 128)) * 128
    small_grads = jnp.pad(small_grads, ((0, 0), (0, depth * slim - small_grads.shape[1])))
    grads = [dot("td,tf->df", rows_one, part).astype(BF16) for part in (d_q, d_k, d_v)]
    grads += [grad_w_out.astype(BF16), small_grads.reshape(features, slim).astype(BF16)]
    grads = jnp.concatenate(grads, axis=1)
    for part in range(2, 6):
        grads, sent[-1] = tie(grads, sent[-1], part, 7)
    mixture_own, grads_own = scatter_everywhere(mixture_all, ranks, 10, grads)
    grads_own = grads_own.astype(F32)
    grad_qkv_own = grads_own[:, : 3 * local_width].reshape(depth, 3, local_width)
    grad_out_own = grads_own[:, 3 * local_width : 4 * local_width]
    small_own = grads_own[:, 4 * local_width :].reshape(-1)
    shared_own = lax.psum(small_own[:shared], "tensor")
    grad_qk_own = small_own[shared : shared + qk_gain.size].reshape(qk_gain.shape)

    layer_out = (residual + mixture_own.astype(F32).reshape(own_shape)).astype(BF16)
    grad_expert_in, grad_expert_out = settle(sent, owned, width)
    grad_expert_in = grad_expert_in.reshape(experts, depth, width // 128, 2, 128)
    grad_expert_in = jnp.swapaxes(grad_expert_in, 2, 3).reshape(experts, depth, 2, width)
    return (
        jnp.swapaxes(layer_out, 0, 1),
        jnp.swapaxes(grad_tokens, 0, 1),
        shared_own[depth * experts : depth * experts + depth],
        grad_qkv_own,
        grad_qk_own,
        grad_out_own,
        shared_own[depth * (experts + 1) :],
        shared_own[: depth * experts].reshape(depth, experts),
        grad_expert_in,
        grad_expert_out,
    )


def solution(mesh):
    placed = (
        P(("dp", "tensor"), None, None),
        P(("dp", "tensor"), None, None),
        P("dp", None),
        P("dp", None, None),
        P("dp"),
        P("dp", None, "tensor"),
        P("dp", None, "tensor"),
        P("dp", "tensor"),
        P("dp"),
        P("dp", None),
        P(None, "dp", None, "tensor"),
        P(None, "dp", "tensor"),
    )
    return jax.shard_map(
        functools.partial(body, mesh.shape["dp"], mesh.shape["tensor"]),
        mesh=mesh,
        in_specs=placed,
        out_specs=(
            P(("dp", "tensor"), None, None),
            P(("dp", "tensor"), None, None),
            P("dp"),
            P("dp", None, "tensor"),
            P("dp", None, "tensor"),
            P("dp", "tensor"),
            P("dp"),
            P("dp", None),
            P(None, "dp", None, "tensor"),
            P(None, "dp", "tensor"),
        ),
        check_vma=False,
    )
```
